128 devices in a mesh: seq: 32 (over z_hi, y, x), batch: 4 (over z_lo, core).
Axes of the slice: x: 4, y: 4, z: 4 (z_hi: 2, z_lo: 2; z = z_hi * 2 + z_lo), core: 2. Of those that a mesh axis runs over, the one named last changes fastest.
Arguments:
- ids: int32 [4, 32768], P('batch', 'seq'), may hold values from 0 to 15
- embed: float32 [16, 256], replicated, may hold values from -6 to 6
- low_filter: float32 [2, 256], replicated, may hold values from 0.62 to 0.78
- high_filter: float32 [2, 256], replicated, may hold values from -3 to 3
- level_weights: float32 [14, 256], replicated, may hold values from -3 to 3
- mix: bfloat16 [256, 256], replicated, may hold values from -0.375 to 0.375
- cotangent: bfloat16 [4, 32768, 256], P('batch', 'seq'), may hold values from -6 to 6
Outputs:
- out: float32 [4, 32768, 256], P('batch', 'seq')
- grad_filters: float32 [2, 2, 256], replicated
- grad_levels: float32 [14, 256], replicated
- grad_mix: float32 [256, 256], replicated
- grad_embed: float32 [16, 256], replicated
The draws below stay inside these ranges and needn't reach their ends.
All inputs are finite; a program needn't handle non-finite values.
Results may differ from the reference program's by a relative error of at most 0.003.
Values sent between devices are 32-bit elements; how exact they have to be, the bound alone decides.
A program may use at most 128 MiB of HBM per device.

```python
import math
import jax
import jax.numpy as jnp
from jax import lax

D = 256
VOCAB = 16
LEVELS = 13
SEQS = 4
SEQ_LEN = 32768


def place_ends(array, stream_key, least, top_value):
    spot = [jax.random.randint(jax.random.fold_in(stream_key, axis), (), 0, length) for axis, length in enumerate(array.shape)]
    widest = array.shape.index(max(array.shape))
    neighbour = spot[:widest] + [(spot[widest] + 1) % array.shape[widest]] + spot[widest + 1:]
    return array.at[tuple(spot)].set(least).at[tuple(neighbour)].set(top_value)


def block_scale(rng, shape, cuts, smallest, top_value):
    def one(axis_at, blocks):
        heights = jax.random.uniform(jax.random.fold_in(jax.random.fold_in(rng, 6), axis_at), (blocks,), jnp.float32, smallest / len(cuts), top_value / len(cuts))
        return jnp.repeat(jnp.exp(heights), shape[axis_at] // blocks).reshape((-1,) + (1,) * (len(shape) - axis_at - 1))

    loudness = one(*cuts[0])
    for cut in cuts[1:]:
        loudness = loudness * one(*cut)
    return loudness


def noise(own_key, dims, scale, most, cuts=(), held_as=jnp.bfloat16):
    factor_of = block_scale(own_key, dims, cuts, -0.22, 0.18) if cuts else 1.0
    array = jax.random.normal(own_key, dims, jnp.float32) * scale * factor_of
    return jnp.minimum(jnp.maximum(array, -most), most).astype(held_as)


def setup_inputs(seed: int = 0) -> dict:
    key_of = jax.random.split(jax.random.key(seed), 8)
    return {
        "ids": place_ends(jax.random.randint(key_of[0], (SEQS, SEQ_LEN), 0, VOCAB), jax.random.fold_in(key_of[0], 1), 0, VOCAB - 1).astype(jnp.int32),
        "embed": noise(key_of[1], (VOCAB, D), 1.0, 6.0, (), jnp.float32),
        "low_filter": jnp.clip(jax.random.uniform(key_of[2], (2, D), jnp.float32, 0.62, 0.78), 0.62, 0.78),
        "high_filter": noise(key_of[3], (2, D), 0.7, 3.0, (), jnp.float32),
        "level_weights": noise(key_of[4], (LEVELS + 1, D), 0.3, 3.0, (), jnp.float32),
        "mix": noise(key_of[5], (D, D), D ** -0.5, 0.375),
        "cotangent": noise(key_of[6], (SEQS, SEQ_LEN, D), 1.0, 6.0, ((0, 4), (1, 32))),
    }


def shift_down(value, span):
    length = value.shape[1]
    if span >= length:
        return jnp.zeros_like(value)
    return jnp.concatenate([jnp.zeros_like(value[:, :span]), value[:, :length - span]], axis=1)

def shift_up(value, span):
    length = value.shape[1]
    if span >= length:
        return jnp.zeros_like(value)
    return jnp.concatenate([value[:, span:], jnp.zeros_like(value[:, :span])], axis=1)

def reference(ids, embed, low_filter, high_filter, level_weights, mix, cotangent):
    depth = level_weights.shape[0] - 1
    width = embed.shape[1]
    x = embed[ids]
    stored = []
    current = x
    mixed_sum = jnp.zeros_like(x)
    for level in range(depth):
        shifted = shift_down(current, 2 ** level)
        stored.append(current)
        detail = high_filter[0] * current + high_filter[1] * shifted
        mixed_sum = mixed_sum + level_weights[level] * detail
        current = low_filter[0] * current + low_filter[1] * shifted
    mixed_sum = mixed_sum + level_weights[depth] * current
    hidden = jax.nn.gelu(mixed_sum).astype(jnp.bfloat16)
    flat_hidden = hidden.reshape(-1, width)
    out = x + jnp.dot(flat_hidden, mix, preferred_element_type=jnp.float32).reshape(x.shape)
    flat_cot = cotangent.reshape(-1, width)
    g_hidden = lax.dot_general(flat_cot, mix, (((1,), (1,)), ((), ())), preferred_element_type=jnp.float32).reshape(x.shape)
    g_y = jax.vjp(jax.nn.gelu, mixed_sum)[1](g_hidden)[0]
    scale = 1.0 / math.sqrt(ids.shape[0] * ids.shape[1])
    grad_mix = scale * lax.dot_general(flat_hidden, flat_cot, (((0,), (0,)), ((), ())), preferred_element_type=jnp.float32)
    level_rows = [None] * (depth + 1)
    level_rows[depth] = lax.optimization_barrier(jnp.sum(g_y * current, axis=(0, 1)))
    g_a = level_weights[depth] * g_y
    low_zero = jnp.zeros((width,), jnp.float32)
    low_one = jnp.zeros((width,), jnp.float32)
    high_zero = jnp.zeros((width,), jnp.float32)
    high_one = jnp.zeros((width,), jnp.float32)
    for level in range(depth - 1, -1, -1):
        span = 2 ** level
        value = stored[level]
        shifted = shift_down(value, span)
        detail = high_filter[0] * value + high_filter[1] * shifted
        g_detail = level_weights[level] * g_y
        level_rows[level] = lax.optimization_barrier(jnp.sum(g_y * detail, axis=(0, 1)))
        low_zero = low_zero + lax.optimization_barrier(jnp.sum(g_a * value, axis=(0, 1)))
        low_one = low_one + lax.optimization_barrier(jnp.sum(g_a * shifted, axis=(0, 1)))
        high_zero = high_zero + lax.optimization_barrier(jnp.sum(g_detail * value, axis=(0, 1)))
        high_one = high_one + lax.optimization_barrier(jnp.sum(g_detail * shifted, axis=(0, 1)))
        back = low_filter[1] * g_a + high_filter[1] * g_detail
        g_a = low_filter[0] * g_a + high_filter[0] * g_detail + shift_up(back, span)
    g_x = cotangent.astype(jnp.float32) + g_a
    onehot = (ids.reshape(-1)[:, None] == jnp.arange(embed.shape[0], dtype=jnp.int32)[None, :]).astype(jnp.float32)
    grad_embed = scale * lax.dot_general(onehot, g_x.reshape(-1, width), (((0,), (0,)), ((), ())), precision=lax.Precision.HIGHEST, preferred_element_type=jnp.float32)
    grad_filters = scale * jnp.stack([jnp.stack([low_zero, low_one]), jnp.stack([high_zero, high_one])])
    grad_levels = scale * jnp.stack(level_rows)
    return (out, grad_filters, grad_levels, grad_mix, grad_embed)
```

```python
import functools
import math

import jax
import jax.numpy as jnp
from jax import lax
from jax.experimental import pallas as pl
from jax.experimental.pallas import tpu as pltpu
from jax.sharding import PartitionSpec as P

MESH = pl.DeviceIdType.MESH
F32, BF16 = jnp.float32, jnp.bfloat16
LEVELS = 13
VOCAB = 16
WIDTH = 256
LANES = 128
TOKENS = 1024
BACK = 8
TILES = (BACK + 1) * TOKENS // LANES
NEAR = 56
CLASSES = 136
ROWS = CLASSES * VOCAB


def near_class(level, ones):
    return 1 + level * (level + 1) // 2 + ones


def far_class(shard, ones):
    return NEAR + (shard - 1) * 11 + ones


def far_level(shard):
    return 9 + shard.bit_length()


def dot(a, b):
    return jnp.dot(a, b, preferred_element_type=F32)


def halves(value):
    high = value.astype(BF16)
    return high, (value - high.astype(F32)).astype(BF16)


def ids_kernel(count, ids_ref, out_ref, held, send_sem, recv_sem):
    me = lax.axis_index("seq")
    barrier = pltpu.get_barrier_semaphore()
    for step in range(1, BACK + 1):
        pl.semaphore_signal(
            barrier, inc=1, device_id={"seq": lax.rem(me + count - step, count)}, device_id_type=MESH
        )
    pl.semaphore_wait(barrier, BACK)
    copies = []
    for step in range(1, BACK + 1):
        copy = pltpu.make_async_remote_copy(
            src_ref=ids_ref,
            dst_ref=held.at[step - 1],
            send_sem=send_sem.at[step - 1],
            recv_sem=recv_sem.at[step - 1],
            device_id={"seq": lax.rem(me + step, count)},
            device_id_type=MESH,
        )
        copy.start()
        copies.append(copy)
    out_ref[BACK] = ids_ref[...]
    for step in range(1, BACK + 1):
        copies[step - 1].wait()
        out_ref[BACK - step] = jnp.where(me >= step, held[step - 1], -1)


def window_of_ids(ids, count):
    return pl.pallas_call(
        functools.partial(ids_kernel, count),
        out_shape=jax.ShapeDtypeStruct((BACK + 1, 8, LANES), jnp.int32),
        in_specs=[pl.BlockSpec(memory_space=pltpu.VMEM)],
        out_specs=pl.BlockSpec(memory_space=pltpu.VMEM),
        scratch_shapes=[
            pltpu.VMEM((BACK, 8, LANES), jnp.int32),
            pltpu.SemaphoreType.DMA((BACK,)),
            pltpu.SemaphoreType.DMA((BACK,)),
        ],
        compiler_params=pltpu.CompilerParams(collective_id=0, has_side_effects=True),
    )(ids)


def level_factors(low, high, weights):
    folded = [None] * (LEVELS + 1)
    kappa = [None] * LEVELS
    folded[LEVELS] = weights[LEVELS]
    for level in range(LEVELS - 1, -1, -1):
        kappa[level] = weights[level] * high[1] + low[1] * folded[level + 1]
        folded[level] = weights[level] * high[0] + low[0] * folded[level + 1]
    return folded, kappa


def rows_of(ref):
    return [ref[row : row + 1, :] for row in range(ref.shape[0])]


def make_weights(low, folded, kappa, embed, weights_ref):
    powers = []
    for row in low:
        chain = [jnp.ones_like(row)]
        for _ in range(10):
            chain.append(chain[-1] * row)
        powers.append(chain)

    def passed(level, ones):
        return powers[0][level - ones] * powers[1][ones]

    def put(place, factor):
        high, low_part = halves(factor * embed)
        rows = slice(place * VOCAB, (place + 1) * VOCAB)
        weights_ref[rows, 0:WIDTH] = high
        weights_ref[rows, WIDTH:] = low_part

    put(0, folded[0])
    for level in range(10):
        for ones in range(level + 1):
            put(near_class(level, ones), kappa[level] * passed(level, ones))
    for shard in range(1, 8):
        level = far_level(shard)
        extra = shard.bit_count() - 1
        factor = kappa[level] * powers[0][level - 10 - extra] * powers[1][extra]
        for ones in range(11):
            put(far_class(shard, ones), factor * passed(10, ones))
    weights_ref[(NEAR + 77) * VOCAB :, :] = jnp.zeros(
        ((CLASSES - NEAR - 77) * VOCAB, 2 * WIDTH), BF16
    )
    return powers, passed


def lag_tables():
    place = lax.broadcasted_iota(jnp.int32, (2 * LANES, LANES), 0)
    lag = lax.broadcasted_iota(jnp.int32, (2 * LANES, LANES), 1) - place
    lag = jnp.where(place >= LANES, lag + 2 * LANES, lag)
    inside = (lag >= 0) & (lag < LANES)
    ones = jnp.zeros_like(lag)
    offset = jnp.zeros_like(lag)
    for bit in range(7):
        ones = ones + ((lag >> bit) & 1)
        offset = offset + jnp.where(lag >= 2**bit, bit, 0)
    ones = jnp.where(inside, ones, -1)
    klass = jnp.where(inside, jnp.where(lag == 0, 0, offset + ones), -1)
    return ones, klass


def where_is(table, value):
    return jnp.where(table == value, 1.0, 0.0).astype(BF16)


def make_features(window_ref, tokens_ref, s7, s8, s9, features_ref):
    names = lax.broadcasted_iota(jnp.int32, (VOCAB, LANES), 0)
    tokens_ref[0:VOCAB, LANES:] = jnp.zeros((VOCAB, LANES), BF16)
    for tile in range(TILES):
        row = window_ref[tile // 8, tile % 8 : tile % 8 + 1, :]
        hot = where_is(names, jnp.broadcast_to(row, (VOCAB, LANES)))
        tokens_ref[tile * VOCAB : (tile + 1) * VOCAB, 0:LANES] = hot
        if tile + 1 < TILES:
            tokens_ref[(tile + 1) * VOCAB : (tile + 2) * VOCAB, LANES:] = hot
    ones, klass = lag_tables()
    for pair in range(4):
        table = jnp.concatenate([where_is(ones, 2 * pair), where_is(ones, 2 * pair + 1)], axis=1)
        result = dot(tokens_ref[VOCAB : 71 * VOCAB, :], table).astype(BF16)
        for tile in range(1, 71):
            for half in range(2):
                s7[(2 * pair + half) * VOCAB : (2 * pair + half + 1) * VOCAB, tile * LANES : (tile + 1) * LANES] = (
                    result[(tile - 1) * VOCAB : tile * VOCAB, half * LANES : (half + 1) * LANES]
                )
    own = tokens_ref[64 * VOCAB : 72 * VOCAB, :]
    for first in range(0, 29, 2):
        members = list(range(first, min(first + 2, 29)))
        table = jnp.concatenate([where_is(klass, member) for member in members], axis=1)
        result = dot(own, table).astype(BF16)
        for tile in range(8):
            for half, member in enumerate(members):
                features_ref[member * VOCAB : (member + 1) * VOCAB, tile * LANES : (tile + 1) * LANES] = result[
                    tile * VOCAB : (tile + 1) * VOCAB, half * LANES : (half + 1) * LANES
                ]

    def step(source, level, ones, begin, end):
        span = 2**level
        total = None
        if ones <= level:
            total = source[ones * VOCAB : (ones + 1) * VOCAB, begin:end]
        if ones >= 1:
            late = source[(ones - 1) * VOCAB : ones * VOCAB, begin - span : end - span]
            total = late if total is None else total + late
        return total

    for ones in range(9):
        s8[ones * VOCAB : (ones + 1) * VOCAB, 2 * LANES : 70 * LANES] = step(s7, 7, ones, 2 * LANES, 70 * LANES)
    for ones in range(10):
        s9[ones * VOCAB : (ones + 1) * VOCAB, 4 * LANES : 68 * LANES] = step(s8, 8, ones, 4 * LANES, 68 * LANES)
    for shard in range(1, 8):
        begin = (BACK - shard) * TOKENS
        for ones in range(11):
            place = far_class(shard, ones) * VOCAB
            features_ref[place : place + VOCAB, :] = step(s9, 9, ones, begin, begin + TOKENS)
    home = BACK * TOKENS
    for level, source in ((7, s7), (8, s8), (9, s9)):
        place = near_class(level, 0) * VOCAB
        span = 2**level
        features_ref[place : place + (level + 1) * VOCAB, :] = source[:, home - span : home - span + TOKENS]
    features_ref[(NEAR + 77) * VOCAB :, :] = jnp.zeros(((CLASSES - NEAR - 77) * VOCAB, TOKENS), BF16)


def gelu_parts(y):
    root = math.sqrt(2.0 / math.pi)
    square = y * y
    bend = jnp.tanh(root * (y + 0.044715 * square * y))
    half = 0.5 * (1.0 + bend)
    slope = half + 0.5 * y * (1.0 - bend * bend) * (root * (1.0 + 3 * 0.044715 * square))
    return y * half, slope


def layer_kernel(
    window_ref, embed_ref, low_ref, high_ref, levels_ref, mix_ref, cot_ref,
    out_ref, part_ref,
    tokens_ref, s7, s8, s9, features_ref, weights_ref, turned_ref, g_ref, z_ref,
):
    embed = embed_ref[...]
    low, high, levels = rows_of(low_ref), rows_of(high_ref), rows_of(levels_ref)
    folded, kappa = level_factors(low, high, levels)
    powers, passed = make_weights(low, folded, kappa, embed, weights_ref)
    turned_ref[...] = weights_ref[...].T
    make_features(window_ref, tokens_ref, s7, s8, s9, features_ref)

    first, second = halves(embed)
    third = (embed - first.astype(F32) - second.astype(F32)).astype(BF16)
    table = jnp.concatenate([first, second, third], axis=0)
    mix = mix_ref[...]
    mix_sum = None
    block = 256
    for start in range(0, TOKENS, block):
        span = slice(start, start + block)
        both = dot(turned_ref[...], features_ref[:, span])
        y = (both[:WIDTH] + both[WIDTH:]).T
        active, slope = gelu_parts(y)
        hidden = active.astype(BF16)
        cot = cot_ref[span, :]
        hot = features_ref[0:VOCAB, span]
        x = lax.dot_general(
            jnp.concatenate([hot, hot, hot], axis=0), table, (((0,), (0,)), ((), ())), preferred_element_type=F32
        )
        out_ref[span, :] = x + dot(hidden, mix)
        g_hidden = lax.dot_general(cot, mix, (((1,), (1,)), ((), ())), preferred_element_type=F32)
        g_high, g_low = halves(g_hidden * slope)
        g_ref[span, 0:WIDTH] = g_high
        g_ref[span, WIDTH:] = g_low
        term = lax.dot_general(hidden, cot, (((0,), (0,)), ((), ())), preferred_element_type=F32)
        mix_sum = term if mix_sum is None else mix_sum + term

    for chunk in range(8):
        for tile in range(8):
            row = 32 * chunk + 8 * (tile // 2)
            column = LANES * (tile % 2)
            part_ref[chunk, tile] = mix_sum[row : row + 8, column : column + LANES]

    both = dot(features_ref[...], g_ref[...])
    z_ref[...] = both[:, :WIDTH] + both[:, WIDTH:]

    def z_of(place):
        return z_ref[place * VOCAB : (place + 1) * VOCAB, :]

    def group(terms):
        total = counted = None
        for ones, factor, place in terms:
            term = factor * z_of(place)
            total = term if total is None else total + term
            if ones:
                more = term * float(ones)
                counted = more if counted is None else counted + more
        return total, jnp.zeros_like(total) if counted is None else counted

    totals = []
    for level in range(10):
        totals.append(group([(n, passed(level, n), near_class(level, n)) for n in range(level + 1)]))
    for level in range(10, LEVELS):
        total = counted = None
        for shard in range(2 ** (level - 10), 2 ** (level - 9)):
            extra = shard.bit_count() - 1
            factor = powers[0][level - 10 - extra] * powers[1][extra]
            part, part_counted = group([(n, passed(10, n), far_class(shard, n)) for n in range(11)])
            part_counted = factor * (part_counted + float(extra) * part)
            part = factor * part
            total = part if total is None else total + part
            counted = part_counted if counted is None else counted + part_counted
        totals.append((total, counted))

    def over_names(value):
        return jnp.sum(embed * value, axis=0, keepdims=True)

    z0 = z_of(0)
    rows = [over_names(z0)]
    embed_sum = folded[0] * z0 + dot(features_ref[0:VOCAB, :], cot_ref[...])
    zero_sum = one_sum = jnp.zeros_like(z0)
    for level, (total, counted) in enumerate(totals):
        rows.append(over_names(total))
        embed_sum = embed_sum + kappa[level] * total
        one_sum = one_sum + kappa[level] * counted
        zero_sum = zero_sum + kappa[level] * (float(level) * total - counted)
    rows += [over_names(zero_sum), over_names(one_sum)]
    small = jnp.concatenate(rows + [embed_sum], axis=0)
    for chunk in range(8):
        row, column = 8 * (chunk // 2), LANES * (chunk % 2)
        part_ref[chunk, 8] = small[row : row + 8, column : column + LANES]


def layer(window, embed, low, high, levels, mix, cot):
    vmem = pl.BlockSpec(memory_space=pltpu.VMEM)
    return pl.pallas_call(
        layer_kernel,
        out_shape=(
            jax.ShapeDtypeStruct((TOKENS, WIDTH), F32),
            jax.ShapeDtypeStruct((8, 9, 8, LANES), F32),
        ),
        in_specs=[vmem] * 7,
        out_specs=(vmem, vmem),
        scratch_shapes=[
            pltpu.VMEM((TILES * VOCAB, 2 * LANES), BF16),
            pltpu.VMEM((8 * VOCAB, TILES * LANES), BF16),
            pltpu.VMEM((9 * VOCAB, TILES * LANES), BF16),
            pltpu.VMEM((10 * VOCAB, TILES * LANES), BF16),
            pltpu.VMEM((ROWS, TOKENS), BF16),
            pltpu.VMEM((ROWS, 2 * WIDTH), BF16),
            pltpu.VMEM((2 * WIDTH, ROWS), BF16),
            pltpu.VMEM((TOKENS, 2 * WIDTH), BF16),
            pltpu.VMEM((ROWS, WIDTH), F32),
        ],
        compiler_params=pltpu.CompilerParams(vmem_limit_bytes=56 * 2**20),
    )(window, embed, low, high, levels, mix, cot)


def sum_kernel(
    scale, part_ref, low_ref, high_ref, levels_ref,
    mix_ref, filters_ref, grad_levels_ref, embed_ref,
    near, mine, far, gathered, whole, sends, recvs,
):
    seq, batch = lax.axis_index("seq"), lax.axis_index("batch")
    column, core = lax.rem(seq, 4), lax.rem(batch, 2)
    outer_seq, outer_batch = lax.div(seq, 4), lax.div(batch, 2)
    near_rank = column * 2 + core
    far_rank = outer_seq * 2 + outer_batch

    def near_peer(step):
        rank = lax.rem(near_rank + step, 8)
        return rank, (outer_seq * 4 + lax.div(rank, 2), outer_batch * 2 + lax.rem(rank, 2))

    def far_peer(step):
        rank = lax.rem(far_rank + step, 16)
        return rank, (lax.div(rank, 2) * 4 + column, lax.rem(rank, 2) * 2 + core)

    barrier = pltpu.get_barrier_semaphore()
    for step in range(1, 8):
        pl.semaphore_signal(barrier, inc=1, device_id=near_peer(step)[1], device_id_type=MESH)
    for step in range(1, 16):
        pl.semaphore_signal(barrier, inc=1, device_id=far_peer(step)[1], device_id_type=MESH)
    pl.semaphore_wait(barrier, 22)

    def send(source, target, phase, step, peer):
        copy = pltpu.make_async_remote_copy(
            src_ref=source,
            dst_ref=target,
            send_sem=sends.at[phase, step],
            recv_sem=recvs.at[phase, step],
            device_id=peer,
            device_id_type=MESH,
        )
        copy.start()
        return copy

    copies = []
    for step in range(1, 8):
        rank, peer = near_peer(step)
        copies.append(send(part_ref.at[rank], near.at[step - 1], 0, step, peer))
    total = part_ref[near_rank]
    for step in range(1, 8):
        copies[step - 1].wait()
        total = total + near[step - 1]

    for half in range(16):
        mine[half, 0] = total[half // 2, 4 * (half % 2) : 4 * (half % 2) + 4]
        mine[half, 1] = total[8, 0:4]
        mine[half, 2] = total[8, 4:8]
    copies = []
    for step in range(1, 16):
        rank, peer = far_peer(step)
        copies.append(send(mine.at[rank], far.at[step - 1], 1, step, peer))
    total = mine[far_rank]
    for step in range(1, 16):
        copies[step - 1].wait()
        total = total + far[step - 1]

    gathered[far_rank] = total[0]
    copies = []
    for step in range(1, 16):
        copies.append(send(gathered.at[far_rank], gathered.at[far_rank], 2, step, far_peer(step)[1]))
    whole[near_rank, 8] = jnp.concatenate([total[1], total[2]], axis=0)
    for copy in copies:
        copy.wait()
    for tile in range(8):
        whole[near_rank, tile] = jnp.concatenate([gathered[2 * tile], gathered[2 * tile + 1]], axis=0)
    copies = []
    for step in range(1, 8):
        copies.append(send(whole.at[near_rank], whole.at[near_rank], 3, step, near_peer(step)[1]))
    for copy in copies:
        copy.wait()

    for chunk in range(8):
        for tile in range(8):
            row = 32 * chunk + 8 * (tile // 2)
            start = LANES * (tile % 2)
            mix_ref[row : row + 8, start : start + LANES] = scale * whole[chunk, tile]
    quarters = [
        scale * jnp.concatenate([whole[2 * quarter, 8], whole[2 * quarter + 1, 8]], axis=1)
        for quarter in range(4)
    ]
    embed_ref[0:8, :] = quarters[2]
    embed_ref[8:16, :] = quarters[3]
    shifted = [quarters[row // 8][row % 8 : row % 8 + 1] for row in range(1, 14)]
    zero_inner, one_inner = quarters[1][6:7], quarters[1][7:8]
    low, high, levels = rows_of(low_ref), rows_of(high_ref), rows_of(levels_ref)
    folded, _ = level_factors(low, high, levels)
    current = quarters[0][0:1]
    low_zero, low_one = zero_inner / low[0], one_inner / low[1]
    high_zero = high_one = jnp.zeros_like(current)
    for level in range(LEVELS):
        late = shifted[level]
        grad_levels_ref[level : level + 1, :] = high[0] * current + high[1] * late
        low_zero = low_zero + folded[level + 1] * current
        low_one = low_one + folded[level + 1] * late
        high_zero = high_zero + levels[level] * current
        high_one = high_one + levels[level] * late
        current = low[0] * current + low[1] * late
    grad_levels_ref[LEVELS : LEVELS + 1, :] = current
    filters_ref[0, 0:1, :] = low_zero
    filters_ref[0, 1:2, :] = low_one
    filters_ref[1, 0:1, :] = high_zero
    filters_ref[1, 1:2, :] = high_one


def summed(scale, part, low, high, levels):
    vmem = pl.BlockSpec(memory_space=pltpu.VMEM)
    return pl.pallas_call(
        functools.partial(sum_kernel, scale),
        out_shape=(
            jax.ShapeDtypeStruct((WIDTH, WIDTH), F32),
            jax.ShapeDtypeStruct((2, 2, WIDTH), F32),
            jax.ShapeDtypeStruct((LEVELS + 1, WIDTH), F32),
            jax.ShapeDtypeStruct((VOCAB, WIDTH), F32),
        ),
        in_specs=[vmem] * 4,
        out_specs=(vmem,) * 4,
        scratch_shapes=[
            pltpu.VMEM((7, 9, 8, LANES), F32),
            pltpu.VMEM((16, 3, 4, LANES), F32),
            pltpu.VMEM((15, 3, 4, LANES), F32),
            pltpu.VMEM((16, 4, LANES), F32),
            pltpu.VMEM((8, 9, 8, LANES), F32),
            pltpu.SemaphoreType.DMA((4, 16)),
            pltpu.SemaphoreType.DMA((4, 16)),
        ],
        compiler_params=pltpu.CompilerParams(collective_id=1, has_side_effects=True),
    )(part, low, high, levels)


def per_device(ids, embed, low_filter, high_filter, level_weights, mix, cotangent):
    count = lax.axis_size("seq")
    window = window_of_ids(ids.reshape(8, LANES), count)
    out, part = layer(window, embed, low_filter, high_filter, level_weights, mix, cotangent[0])
    scale = 1.0 / math.sqrt(count * lax.axis_size("batch") * TOKENS)
    grad_mix, grad_filters, grad_levels, grad_embed = summed(
        scale, part, low_filter, high_filter, level_weights
    )
    return out[None], grad_filters, grad_levels, grad_mix, grad_embed


def solution(mesh):
    placed = (P("batch", "seq"), P(), P(), P(), P(), P(), P("batch", "seq", None))
    return jax.shard_map(
        per_device,
        mesh=mesh,
        in_specs=placed,
        out_specs=(P("batch", "seq", None), P(), P(), P(), P()),
        check_vma=False,
    )
```

```python
import functools
import math

import jax
import jax.numpy as jnp
from jax import lax
from jax.experimental import pallas as pl
from jax.experimental.pallas import tpu as pltpu
from jax.sharding import PartitionSpec as P

MESH = pl.DeviceIdType.MESH
F32, BF16 = jnp.float32, jnp.bfloat16
LEVELS = 13
VOCAB = 16
WIDTH = 256
LANES = 128
TOKENS = 1024
BACK = 8
TILES = (BACK + 1) * TOKENS // LANES
CLASSES = 1 + LEVELS * (LEVELS + 1) // 2
ROWS = 96 * VOCAB


def class_of(level, ones):
    return 1 + level * (level + 1) // 2 + ones


def block_of(level, ones):
    return slice(class_of(level, ones) * VOCAB, (class_of(level, ones) + 1) * VOCAB)


def dot(a, b):
    return jnp.dot(a, b, preferred_element_type=F32)


def halves(value):
    high = value.astype(BF16)
    return high, (value - high.astype(F32)).astype(BF16)


def level_factors(low, high, weights):
    folded = [None] * (LEVELS + 1)
    kappa = [None] * LEVELS
    folded[LEVELS] = weights[LEVELS]
    for level in range(LEVELS - 1, -1, -1):
        kappa[level] = weights[level] * high[1] + low[1] * folded[level + 1]
        folded[level] = weights[level] * high[0] + low[0] * folded[level + 1]
    return folded, kappa


def rows_of(ref):
    return [ref[row : row + 1, :] for row in range(ref.shape[0])]


def lag_weights(low):
    chains = []
    for row in low:
        chain = [jnp.ones_like(row)]
        for _ in range(LEVELS - 1):
            chain.append(chain[-1] * row)
        chains.append(chain)
    return lambda level, ones: chains[0][level - ones] * chains[1][ones]


def make_weights(passed, folded, kappa, embed, weights_ref):
    def put(rows, factor):
        high, rest = halves(factor * embed)
        weights_ref[rows, 0:WIDTH] = high
        weights_ref[rows, WIDTH:] = rest

    put(slice(0, VOCAB), folded[0])
    for level in range(LEVELS):
        for ones in range(level + 1):
            put(block_of(level, ones), kappa[level] * passed(level, ones))
    weights_ref[CLASSES * VOCAB :, :] = jnp.zeros((ROWS - CLASSES * VOCAB, 2 * WIDTH), BF16)


def where_is(table, value):
    return jnp.where(table == value, 1.0, 0.0).astype(BF16)


def make_tables(ones_ref, class_ref):
    place = lax.broadcasted_iota(jnp.int32, (2 * LANES, LANES), 0)
    lag = lax.broadcasted_iota(jnp.int32, (2 * LANES, LANES), 1) - place
    lag = jnp.where(place >= LANES, lag + 2 * LANES, lag)
    inside = (lag >= 0) & (lag < LANES)
    ones = jnp.zeros_like(lag)
    offset = jnp.zeros_like(lag)
    for bit in range(7):
        ones = ones + ((lag >> bit) & 1)
        offset = offset + jnp.where(lag >= 2**bit, bit, 0)
    klass = jnp.where(inside, jnp.where(lag == 0, 0, offset + ones), -1)
    ones = jnp.where(inside, ones, -1)
    for value in range(8):
        ones_ref[:, value * LANES : (value + 1) * LANES] = where_is(ones, value)
    for value in range(29):
        class_ref[:, value * LANES : (value + 1) * LANES] = where_is(klass, value)


def make_hot(tokens_ref, first, ids):
    names = lax.broadcasted_iota(jnp.int32, (VOCAB, LANES), 0)
    for row in range(8):
        tile = first + row
        hot = where_is(names, jnp.broadcast_to(ids[row : row + 1, :], (VOCAB, LANES)))
        tokens_ref[tile * VOCAB : (tile + 1) * VOCAB, 0:LANES] = hot
        if tile + 1 < TILES:
            tokens_ref[(tile + 1) * VOCAB : (tile + 2) * VOCAB, LANES:] = hot


def make_near(tokens_ref, class_ref, features_ref):
    own = tokens_ref[64 * VOCAB : 72 * VOCAB, :]
    for first in range(0, 29, 2):
        members = range(first, min(first + 2, 29))
        result = dot(own, class_ref[:, first * LANES : (first + len(members)) * LANES]).astype(BF16)
        for tile in range(8):
            for half, member in enumerate(members):
                features_ref[member * VOCAB : (member + 1) * VOCAB, tile * LANES : (tile + 1) * LANES] = result[
                    tile * VOCAB : (tile + 1) * VOCAB, half * LANES : (half + 1) * LANES
                ]


def make_far(tokens_ref, ones_ref, s7, s8, s9, s10, features_ref):
    for pair in range(4):
        result = dot(
            tokens_ref[VOCAB : 71 * VOCAB, :], ones_ref[:, 2 * pair * LANES : 2 * (pair + 1) * LANES]
        ).astype(BF16)
        for tile in range(1, 71):
            for half in range(2):
                value = 2 * pair + half
                s7[value * VOCAB : (value + 1) * VOCAB, tile * LANES : (tile + 1) * LANES] = result[
                    (tile - 1) * VOCAB : tile * VOCAB, half * LANES : (half + 1) * LANES
                ]

    def step(source, level, ones, begin, end):
        span = 2**level
        total = None
        if 0 <= ones <= level:
            total = source[ones * VOCAB : (ones + 1) * VOCAB, begin:end]
        if 1 <= ones <= level + 1:
            late = source[(ones - 1) * VOCAB : ones * VOCAB, begin - span : end - span]
            total = late if total is None else total + late
        return total

    def both(one, other):
        if one is None or other is None:
            return other if one is None else one
        return one + other

    for ones in range(9):
        s8[ones * VOCAB : (ones + 1) * VOCAB, 2 * LANES : 70 * LANES] = step(s7, 7, ones, 2 * LANES, 70 * LANES)
    for ones in range(10):
        s9[ones * VOCAB : (ones + 1) * VOCAB, 4 * LANES : 68 * LANES] = step(s8, 8, ones, 4 * LANES, 68 * LANES)
    for ones in range(11):
        s10[ones * VOCAB : (ones + 1) * VOCAB, 8 * LANES : 64 * LANES] = step(s9, 9, ones, 8 * LANES, 64 * LANES)
    home = BACK * TOKENS
    for level, source in ((7, s7), (8, s8), (9, s9), (10, s10)):
        rows = slice(class_of(level, 0) * VOCAB, class_of(level + 1, 0) * VOCAB)
        begin = home - 2**level
        features_ref[rows, :] = source[:, begin : begin + TOKENS]
    for ones in range(12):
        begin = home - 2048
        features_ref[block_of(11, ones), :] = step(s10, 10, ones, begin, begin + TOKENS)
    for ones in range(13):
        begin = home - 4096
        near = step(s10, 10, ones, begin, begin + TOKENS)
        late = step(s10, 10, ones - 1, begin - 2048, begin - 2048 + TOKENS)
        features_ref[block_of(12, ones), :] = both(near, late)
    features_ref[CLASSES * VOCAB :, :] = jnp.zeros((ROWS - CLASSES * VOCAB, TOKENS), BF16)


def gelu_parts(y):
    root = math.sqrt(2.0 / math.pi)
    square = y * y
    bend = jnp.tanh(root * (y + 0.044715 * square * y))
    half = 0.5 * (1.0 + bend)
    slope = half + 0.5 * y * (1.0 - bend * bend) * (root * (1.0 + 3 * 0.044715 * square))
    return y * half, slope


def forward(turned_ref, features_ref, mix_ref, cot_ref, hidden_ref, g_ref):
    mix = mix_ref[...]
    mix_sum = None
    block = 256
    for start in range(0, TOKENS, block):
        span = slice(start, start + block)
        both = dot(turned_ref[...], features_ref[:, span])
        y = (both[:WIDTH] + both[WIDTH:]).T
        active, slope = gelu_parts(y)
        hidden = active.astype(BF16)
        hidden_ref[span, :] = hidden
        cot = cot_ref[span, :]
        g_hidden = lax.dot_general(cot, mix, (((1,), (1,)), ((), ())), preferred_element_type=F32)
        g_high, g_rest = halves(g_hidden * slope)
        g_ref[span, 0:WIDTH] = g_high
        g_ref[span, WIDTH:] = g_rest
        term = lax.dot_general(hidden, cot, (((0,), (0,)), ((), ())), preferred_element_type=F32)
        mix_sum = term if mix_sum is None else mix_sum + term
    return mix_sum


def backward(passed, folded, kappa, embed, features_ref, g_ref, cot_ref, z_ref):
    both = dot(features_ref[0 : CLASSES * VOCAB, :], g_ref[...])
    z_ref[...] = both[:, :WIDTH] + both[:, WIDTH:]

    def over_names(value):
        return jnp.sum(embed * value, axis=0, keepdims=True)

    z0 = z_ref[0:VOCAB, :]
    rows = [over_names(z0)]
    embed_sum = folded[0] * z0 + dot(features_ref[0:VOCAB, :], cot_ref[...])
    zero_sum = one_sum = jnp.zeros_like(z0)
    for level in range(LEVELS):
        total = passed(level, 0) * z_ref[block_of(level, 0), :]
        counted = jnp.zeros_like(total)
        for ones in range(1, level + 1):
            term = passed(level, ones) * z_ref[block_of(level, ones), :]
            total = total + term
            counted = counted + float(ones) * term
        rows.append(over_names(total))
        embed_sum = embed_sum + kappa[level] * total
        one_sum = one_sum + kappa[level] * counted
        zero_sum = zero_sum + kappa[level] * (float(level) * total - counted)
    rows += [over_names(zero_sum), over_names(one_sum)]
    return jnp.concatenate(rows + [embed_sum], axis=0)


def layer_kernel(
    count, ids_ref, embed_ref, low_ref, high_ref, levels_ref, mix_ref, cot_ref,
    hidden_ref, whole,
    held, ids_send, ids_recv, ones_ref, class_ref, tokens_ref, s7, s8, s9, s10, features_ref, weights_ref, turned_ref,
    g_ref, z_ref, part, sibling, halved, first, second, third, sends, recvs,
):
    seq, batch = lax.axis_index("seq"), lax.axis_index("batch")
    x, y = lax.rem(seq, 4), lax.rem(lax.div(seq, 4), 4)
    core = lax.rem(batch, 2)
    z = lax.div(seq, 16) * 2 + lax.div(batch, 2)

    def device(x, y, z, core):
        return lax.div(z, 2) * 16 + y * 4 + x, lax.rem(z, 2) * 2 + core

    spots = (x + core * (y - x), y + core * (z - y), z + core * (x - z))

    def peer_of(axis, step):
        spot = list(spots)
        spot[axis] = lax.rem(spots[axis] + step, 4)
        a, b, c = spot
        return device(a + core * (c - a), b + core * (a - b), c + core * (b - c), core)

    other = device(x, y, z, 1 - core)
    barrier = pltpu.get_barrier_semaphore()

    def greet(peer):
        pl.semaphore_signal(barrier, inc=1, device_id=peer, device_id_type=MESH)

    for step in range(1, BACK + 1):
        greet((lax.rem(seq + count - step, count), batch))
    greet(other)
    for axis in range(3):
        for step in range(1, 4):
            greet(peer_of(axis, step))
    pl.semaphore_wait(barrier, BACK + 10)

    def copy_to(source, target, sent, received, peer):
        copy = pltpu.make_async_remote_copy(
            src_ref=source, dst_ref=target, send_sem=sent, recv_sem=received, device_id=peer, device_id_type=MESH
        )
        copy.start()
        return copy

    id_copies = [
        copy_to(
            ids_ref, held.at[step], ids_send.at[step], ids_recv.at[step], (lax.rem(seq + step + 1, count), batch)
        )
        for step in range(BACK)
    ]

    embed = embed_ref[...]
    low, high, levels = rows_of(low_ref), rows_of(high_ref), rows_of(levels_ref)
    folded, kappa = level_factors(low, high, levels)
    passed = lag_weights(low)
    make_weights(passed, folded, kappa, embed, weights_ref)
    turned_ref[...] = weights_ref[...].T
    make_tables(ones_ref, class_ref)
    tokens_ref[0:VOCAB, LANES:] = jnp.zeros((VOCAB, LANES), BF16)
    make_hot(tokens_ref, 8 * BACK, ids_ref[...])
    for step in range(BACK):
        id_copies[step].wait()
        make_hot(tokens_ref, 8 * (BACK - 1 - step), jnp.where(seq > step, held[step], -1))
    make_near(tokens_ref, class_ref, features_ref)
    make_far(tokens_ref, ones_ref, s7, s8, s9, s10, features_ref)
    mix_sum = forward(turned_ref, features_ref, mix_ref, cot_ref, hidden_ref, g_ref)
    small = backward(passed, folded, kappa, embed, features_ref, g_ref, cot_ref, z_ref)

    for chunk in range(8):
        for tile in range(8):
            row = 32 * chunk + 8 * (tile // 2)
            column = LANES * (tile % 2)
            part[chunk, tile] = mix_sum[row : row + 8, column : column + LANES]
        row, column = 8 * (chunk // 2), LANES * (chunk % 2)
        part[chunk, 8] = small[row : row + 8, column : column + LANES]

    copy_to(
        part.at[pl.ds(4 * (1 - core), 4)], sibling, sends.at[0, 0], recvs.at[0, 0], other
    ).wait()
    for chunk in range(4):
        halved[chunk] = part[4 * core + chunk] + sibling[chunk]

    def exchange(phase, axis, source_of, target):
        copies = [
            copy_to(source_of(step), target.at[spots[axis]], sends.at[phase, step], recvs.at[phase, step], peer_of(axis, step))
            for step in range(1, 4)
        ]
        for copy in copies:
            copy.wait()

    first[spots[0]] = halved[spots[0]]
    exchange(1, 0, lambda step: halved.at[lax.rem(spots[0] + step, 4)], first)
    second[spots[1]] = (first[0] + first[1]) + (first[2] + first[3])
    exchange(2, 1, lambda step: second.at[spots[1]], second)
    third[spots[2]] = (second[0] + second[1]) + (second[2] + second[3])
    exchange(3, 2, lambda step: third.at[spots[2]], third)
    mine = 4 * core + spots[0]
    whole[mine] = (third[0] + third[1]) + (third[2] + third[3])
    copies = [
        copy_to(whole.at[mine], whole.at[mine], sends.at[4, step], recvs.at[4, step], peer_of(0, step))
        for step in range(1, 4)
    ]
    for copy in copies:
        copy.wait()
    ours = whole.at[pl.ds(4 * core, 4)]
    copy_to(ours, ours, sends.at[5, 0], recvs.at[5, 0], other).wait()


def layer(count, ids, embed, low, high, levels, mix, cot):
    vmem = pl.BlockSpec(memory_space=pltpu.VMEM)
    chunk = (9, 8, LANES)
    return pl.pallas_call(
        functools.partial(layer_kernel, count),
        out_shape=(
            jax.ShapeDtypeStruct((TOKENS, WIDTH), BF16),
            jax.ShapeDtypeStruct((8,) + chunk, F32),
        ),
        in_specs=[vmem] * 7,
        out_specs=(vmem, vmem),
        scratch_shapes=[
            pltpu.VMEM((BACK, 8, LANES), jnp.int32),
            pltpu.SemaphoreType.DMA((BACK,)),
            pltpu.SemaphoreType.DMA((BACK,)),
            pltpu.VMEM((2 * LANES, 8 * LANES), BF16),
            pltpu.VMEM((2 * LANES, 29 * LANES), BF16),
            pltpu.VMEM((TILES * VOCAB, 2 * LANES), BF16),
            pltpu.VMEM((8 * VOCAB, TILES * LANES), BF16),
            pltpu.VMEM((9 * VOCAB, TILES * LANES), BF16),
            pltpu.VMEM((10 * VOCAB, TILES * LANES), BF16),
            pltpu.VMEM((11 * VOCAB, TILES * LANES), BF16),
            pltpu.VMEM((ROWS, TOKENS), BF16),
            pltpu.VMEM((ROWS, 2 * WIDTH), BF16),
            pltpu.VMEM((2 * WIDTH, ROWS), BF16),
            pltpu.VMEM((TOKENS, 2 * WIDTH), BF16),
            pltpu.VMEM((CLASSES * VOCAB, WIDTH), F32),
            pltpu.VMEM((8,) + chunk, F32),
            pltpu.VMEM((4,) + chunk, F32),
            pltpu.VMEM((4,) + chunk, F32),
            pltpu.VMEM((4,) + chunk, F32),
            pltpu.VMEM((4,) + chunk, F32),
            pltpu.VMEM((4,) + chunk, F32),
            pltpu.SemaphoreType.DMA((6, 4)),
            pltpu.SemaphoreType.DMA((6, 4)),
        ],
        compiler_params=pltpu.CompilerParams(
            collective_id=0, has_side_effects=True, vmem_limit_bytes=56 * 2**20
        ),
    )(ids, embed, low, high, levels, mix, cot)


def finish_kernel(
    scale, ids_ref, hidden_ref, whole, embed_in_ref, mix_in_ref, low_ref, high_ref, levels_ref,
    out_ref, filters_ref, grad_levels_ref, mix_ref, embed_ref,
):
    embed = embed_in_ref[...]
    high_part, middle = halves(embed)
    rest = (embed - high_part.astype(F32) - middle.astype(F32)).astype(BF16)
    table = jnp.concatenate([high_part, middle, rest], axis=0)
    names = lax.broadcasted_iota(jnp.int32, (VOCAB, LANES), 0)
    for tile in range(8):
        rows = slice(tile * LANES, (tile + 1) * LANES)
        hot = where_is(names, jnp.broadcast_to(ids_ref[tile : tile + 1, :], (VOCAB, LANES)))
        hot = jnp.concatenate([hot, hot, hot], axis=0)
        x = lax.dot_general(hot, table, (((0,), (0,)), ((), ())), preferred_element_type=F32)
        out_ref[rows, :] = x + dot(hidden_ref[rows, :], mix_in_ref[...])
    for chunk in range(8):
        for tile in range(8):
            row = 32 * chunk + 8 * (tile // 2)
            start = LANES * (tile % 2)
            mix_ref[row : row + 8, start : start + LANES] = scale * whole[chunk, tile]
    quarters = [
        scale * jnp.concatenate([whole[2 * quarter, 8], whole[2 * quarter + 1, 8]], axis=1)
        for quarter in range(4)
    ]
    embed_ref[0:8, :] = quarters[2]
    embed_ref[8:16, :] = quarters[3]
    shifted = [quarters[row // 8][row % 8 : row % 8 + 1] for row in range(1, 14)]
    zero_inner, one_inner = quarters[1][6:7], quarters[1][7:8]
    low, high, levels = rows_of(low_ref), rows_of(high_ref), rows_of(levels_ref)
    folded, _ = level_factors(low, high, levels)
    current = quarters[0][0:1]
    low_zero, low_one = zero_inner / low[0], one_inner / low[1]
    high_zero = high_one = jnp.zeros_like(current)
    for level in range(LEVELS):
        late = shifted[level]
        grad_levels_ref[level : level + 1, :] = high[0] * current + high[1] * late
        low_zero = low_zero + folded[level + 1] * current
        low_one = low_one + folded[level + 1] * late
        high_zero = high_zero + levels[level] * current
        high_one = high_one + levels[level] * late
        current = low[0] * current + low[1] * late
    grad_levels_ref[LEVELS : LEVELS + 1, :] = current
    filters_ref[0, 0:1, :] = low_zero
    filters_ref[0, 1:2, :] = low_one
    filters_ref[1, 0:1, :] = high_zero
    filters_ref[1, 1:2, :] = high_one


def finish(scale, ids, hidden, whole, embed, mix, low, high, levels):
    vmem = pl.BlockSpec(memory_space=pltpu.VMEM)
    return pl.pallas_call(
        functools.partial(finish_kernel, scale),
        out_shape=(
            jax.ShapeDtypeStruct((TOKENS, WIDTH), F32),
            jax.ShapeDtypeStruct((2, 2, WIDTH), F32),
            jax.ShapeDtypeStruct((LEVELS + 1, WIDTH), F32),
            jax.ShapeDtypeStruct((WIDTH, WIDTH), F32),
            jax.ShapeDtypeStruct((VOCAB, WIDTH), F32),
        ),
        in_specs=[vmem] * 8,
        out_specs=(vmem,) * 5,
        compiler_params=pltpu.CompilerParams(vmem_limit_bytes=56 * 2**20),
    )(ids, hidden, whole, embed, mix, low, high, levels)


def per_device(ids, embed, low_filter, high_filter, level_weights, mix, cotangent):
    count = lax.axis_size("seq")
    ids = ids.reshape(8, LANES)
    hidden, whole = layer(count, ids, embed, low_filter, high_filter, level_weights, mix, cotangent[0])
    scale = 1.0 / math.sqrt(count * lax.axis_size("batch") * TOKENS)
    out, grad_filters, grad_levels, grad_mix, grad_embed = finish(
        scale, ids, hidden, whole, embed, mix, low_filter, high_filter, level_weights
    )
    return out[None], grad_filters, grad_levels, grad_mix, grad_embed


def solution(mesh):
    placed = (P("batch", "seq"), P(), P(), P(), P(), P(), P("batch", "seq", None))
    return jax.shard_map(
        per_device,
        mesh=mesh,
        in_specs=placed,
        out_specs=(P("batch", "seq", None), P(), P(), P(), P()),
        check_vma=False,
    )
```

```python
import functools
import math

import jax
import jax.numpy as jnp
from jax import lax
from jax.experimental import pallas as pl
from jax.experimental.pallas import tpu as pltpu
from jax.sharding import PartitionSpec as P

MESH = pl.DeviceIdType.MESH
F32, BF16 = jnp.float32, jnp.bfloat16
LEVELS = 13
VOCAB = 16
WIDTH = 256
LANES = 128
TOKENS = 1024
BACK = 8
TILES = (BACK + 1) * TOKENS // LANES
CLASSES = 1 + LEVELS * (LEVELS + 1) // 2
ROWS = 96 * VOCAB


def class_of(level, ones):
    return 1 + level * (level + 1) // 2 + ones


def block_of(level, ones):
    return slice(class_of(level, ones) * VOCAB, (class_of(level, ones) + 1) * VOCAB)


def dot(a, b):
    return jnp.dot(a, b, preferred_element_type=F32)


def halves(value):
    high = value.astype(BF16)
    return high, (value - high.astype(F32)).astype(BF16)


def level_factors(low, high, weights):
    folded = [None] * (LEVELS + 1)
    kappa = [None] * LEVELS
    folded[LEVELS] = weights[LEVELS]
    for level in range(LEVELS - 1, -1, -1):
        kappa[level] = weights[level] * high[1] + low[1] * folded[level + 1]
        folded[level] = weights[level] * high[0] + low[0] * folded[level + 1]
    return folded, kappa


def rows_of(ref):
    return [ref[row : row + 1, :] for row in range(ref.shape[0])]


def lag_weights(low):
    chains = []
    for row in low:
        chain = [jnp.ones_like(row)]
        for _ in range(LEVELS - 1):
            chain.append(chain[-1] * row)
        chains.append(chain)
    return lambda level, ones: chains[0][level - ones] * chains[1][ones]


def make_weights(passed, folded, kappa, embed, weights_ref):
    def put(rows, factor):
        high, rest = halves(factor * embed)
        weights_ref[rows, 0:WIDTH] = high
        weights_ref[rows, WIDTH:] = rest

    put(slice(0, VOCAB), folded[0])
    for level in range(LEVELS):
        for ones in range(level + 1):
            put(block_of(level, ones), kappa[level] * passed(level, ones))
    weights_ref[CLASSES * VOCAB :, :] = jnp.zeros((ROWS - CLASSES * VOCAB, 2 * WIDTH), BF16)


def where_is(table, value):
    return jnp.where(table == value, 1.0, 0.0).astype(BF16)


def make_tables(ones_ref, class_ref):
    place = lax.broadcasted_iota(jnp.int32, (2 * LANES, LANES), 0)
    lag = lax.broadcasted_iota(jnp.int32, (2 * LANES, LANES), 1) - place
    lag = jnp.where(place >= LANES, lag + 2 * LANES, lag)
    inside = (lag >= 0) & (lag < LANES)
    ones = jnp.zeros_like(lag)
    offset = jnp.zeros_like(lag)
    for bit in range(7):
        ones = ones + ((lag >> bit) & 1)
        offset = offset + jnp.where(lag >= 2**bit, bit, 0)
    klass = jnp.where(inside, jnp.where(lag == 0, 0, offset + ones), -1)
    ones = jnp.where(inside, ones, -1)
    for value in range(8):
        ones_ref[:, value * LANES : (value + 1) * LANES] = where_is(ones, value)
    for value in range(29):
        class_ref[:, value * LANES : (value + 1) * LANES] = where_is(klass, value)


def make_hot(tokens_ref, first, ids):
    names = lax.broadcasted_iota(jnp.int32, (VOCAB, LANES), 0)
    for row in range(8):
        tile = first + row
        hot = where_is(names, jnp.broadcast_to(ids[row : row + 1, :], (VOCAB, LANES)))
        tokens_ref[tile * VOCAB : (tile + 1) * VOCAB, 0:LANES] = hot
        if tile + 1 < TILES:
            tokens_ref[(tile + 1) * VOCAB : (tile + 2) * VOCAB, LANES:] = hot


def make_near(tokens_ref, class_ref, features_ref):
    own = tokens_ref[64 * VOCAB : 72 * VOCAB, :]
    for first in range(0, 29, 2):
        members = range(first, min(first + 2, 29))
        result = dot(own, class_ref[:, first * LANES : (first + len(members)) * LANES]).astype(BF16)
        for tile in range(8):
            for half, member in enumerate(members):
                features_ref[member * VOCAB : (member + 1) * VOCAB, tile * LANES : (tile + 1) * LANES] = result[
                    tile * VOCAB : (tile + 1) * VOCAB, half * LANES : (half + 1) * LANES
                ]


def make_far(tokens_ref, ones_ref, s7, s8, s9, s10, features_ref):
    for pair in range(4):
        result = dot(
            tokens_ref[VOCAB : 71 * VOCAB, :], ones_ref[:, 2 * pair * LANES : 2 * (pair + 1) * LANES]
        ).astype(BF16)
        for tile in range(1, 71):
            for half in range(2):
                value = 2 * pair + half
                s7[value * VOCAB : (value + 1) * VOCAB, tile * LANES : (tile + 1) * LANES] = result[
                    (tile - 1) * VOCAB : tile * VOCAB, half * LANES : (half + 1) * LANES
                ]

    def step(source, level, ones, begin, end):
        span = 2**level
        total = None
        if 0 <= ones <= level:
            total = source[ones * VOCAB : (ones + 1) * VOCAB, begin:end]
        if 1 <= ones <= level + 1:
            late = source[(ones - 1) * VOCAB : ones * VOCAB, begin - span : end - span]
            total = late if total is None else total + late
        return total

    def both(one, other):
        if one is None or other is None:
            return other if one is None else one
        return one + other

    for ones in range(9):
        s8[ones * VOCAB : (ones + 1) * VOCAB, 2 * LANES : 70 * LANES] = step(s7, 7, ones, 2 * LANES, 70 * LANES)
    for ones in range(10):
        s9[ones * VOCAB : (ones + 1) * VOCAB, 4 * LANES : 68 * LANES] = step(s8, 8, ones, 4 * LANES, 68 * LANES)
    for ones in range(11):
        s10[ones * VOCAB : (ones + 1) * VOCAB, 8 * LANES : 64 * LANES] = step(s9, 9, ones, 8 * LANES, 64 * LANES)
    home = BACK * TOKENS
    for level, source in ((7, s7), (8, s8), (9, s9), (10, s10)):
        rows = slice(class_of(level, 0) * VOCAB, class_of(level + 1, 0) * VOCAB)
        begin = home - 2**level
        features_ref[rows, :] = source[:, begin : begin + TOKENS]
    for ones in range(12):
        begin = home - 2048
        features_ref[block_of(11, ones), :] = step(s10, 10, ones, begin, begin + TOKENS)
    for ones in range(13):
        begin = home - 4096
        near = step(s10, 10, ones, begin, begin + TOKENS)
        late = step(s10, 10, ones - 1, begin - 2048, begin - 2048 + TOKENS)
        features_ref[block_of(12, ones), :] = both(near, late)
    features_ref[CLASSES * VOCAB :, :] = jnp.zeros((ROWS - CLASSES * VOCAB, TOKENS), BF16)


def gelu_parts(y):
    root = math.sqrt(2.0 / math.pi)
    square = y * y
    bend = jnp.tanh(root * (y + 0.044715 * square * y))
    half = 0.5 * (1.0 + bend)
    slope = half + 0.5 * y * (1.0 - bend * bend) * (root * (1.0 + 3 * 0.044715 * square))
    return y * half, slope


def forward(turned_ref, features_ref, mix_ref, cot_ref, hidden_ref, g_ref):
    mix = mix_ref[...]
    mix_sum = None
    block = 256
    for start in range(0, TOKENS, block):
        span = slice(start, start + block)
        both = dot(turned_ref[...], features_ref[:, span])
        y = (both[:WIDTH] + both[WIDTH:]).T
        active, slope = gelu_parts(y)
        hidden = active.astype(BF16)
        hidden_ref[span, :] = hidden
        cot = cot_ref[span, :]
        g_hidden = lax.dot_general(cot, mix, (((1,), (1,)), ((), ())), preferred_element_type=F32)
        g_high, g_rest = halves(g_hidden * slope)
        g_ref[span, 0:WIDTH] = g_high
        g_ref[span, WIDTH:] = g_rest
        term = lax.dot_general(hidden, cot, (((0,), (0,)), ((), ())), preferred_element_type=F32)
        mix_sum = term if mix_sum is None else mix_sum + term
    return mix_sum


def backward(passed, folded, kappa, embed, features_ref, g_ref, cot_ref, z_ref):
    both = dot(features_ref[0 : CLASSES * VOCAB, :], g_ref[...])
    z_ref[...] = both[:, :WIDTH] + both[:, WIDTH:]

    def over_names(value):
        return jnp.sum(embed * value, axis=0, keepdims=True)

    z0 = z_ref[0:VOCAB, :]
    rows = [over_names(z0)]
    embed_sum = folded[0] * z0 + dot(features_ref[0:VOCAB, :], cot_ref[...])
    zero_sum = one_sum = jnp.zeros_like(z0)
    for level in range(LEVELS):
        total = passed(level, 0) * z_ref[block_of(level, 0), :]
        counted = jnp.zeros_like(total)
        for ones in range(1, level + 1):
            term = passed(level, ones) * z_ref[block_of(level, ones), :]
            total = total + term
            counted = counted + float(ones) * term
        rows.append(over_names(total))
        embed_sum = embed_sum + kappa[level] * total
        one_sum = one_sum + kappa[level] * counted
        zero_sum = zero_sum + kappa[level] * (float(level) * total - counted)
    rows += [over_names(zero_sum), over_names(one_sum)]
    return jnp.concatenate(rows + [embed_sum], axis=0)


def layer_kernel(
    count, ids_ref, embed_ref, low_ref, high_ref, levels_ref, mix_ref, cot_hbm,
    hidden_hbm, whole_hbm,
    held, ids_send, ids_recv, ones_ref, class_ref, tokens_ref, s7, s8, s9, s10, features_ref, weights_ref, turned_ref,
    cot_ref, hidden_ref, g_ref, z_ref, local_sem, mix_part, small_part, mix_in, small_in, second, third, total,
    sends, recvs,
):
    seq, batch = lax.axis_index("seq"), lax.axis_index("batch")
    x, y = lax.rem(seq, 4), lax.rem(lax.div(seq, 4), 4)
    core = lax.rem(batch, 2)
    z = lax.div(seq, 16) * 2 + lax.div(batch, 2)

    def along(order):
        return [x + order * (y - x), y + order * (z - y), z + order * (x - z)]

    def device(order, spots, core):
        a, b, c = spots
        x, y, z = a + order * (c - a), b + order * (a - b), c + order * (b - c)
        return lax.div(z, 2) * 16 + y * 4 + x, lax.rem(z, 2) * 2 + core

    def moved(spots, axis, step):
        return [lax.rem(spot + step, 4) if place == axis else spot for place, spot in enumerate(spots)]

    mine, theirs = along(core), along(1 - core)
    own_peer = lambda axis, step: device(core, moved(mine, axis, step), core)
    their_peer = lambda step: device(1 - core, moved(theirs, 0, step), 1 - core)
    cross_peer = lambda step: device(core, moved(mine, 0, step), 1 - core)

    cot_copy = pltpu.make_async_copy(cot_hbm, cot_ref, local_sem.at[0])
    cot_copy.start()
    barrier = pltpu.get_barrier_semaphore()

    def greet(peer):
        pl.semaphore_signal(barrier, inc=1, device_id=peer, device_id_type=MESH)

    for step in range(1, BACK + 1):
        greet((lax.rem(seq + count - step, count), batch))
    for step in range(4):
        greet(their_peer(step))
    for step in range(1, 4):
        greet(cross_peer(step))
        for axis in range(3):
            greet(own_peer(axis, step))
    pl.semaphore_wait(barrier, BACK + 16)

    def copy_to(source, target, sent, received, peer):
        copy = pltpu.make_async_remote_copy(
            src_ref=source, dst_ref=target, send_sem=sent, recv_sem=received, device_id=peer, device_id_type=MESH
        )
        copy.start()
        return copy

    id_copies = [
        copy_to(
            ids_ref, held.at[step], ids_send.at[step], ids_recv.at[step], (lax.rem(seq + step + 1, count), batch)
        )
        for step in range(BACK)
    ]

    embed = embed_ref[...]
    low, high, levels = rows_of(low_ref), rows_of(high_ref), rows_of(levels_ref)
    folded, kappa = level_factors(low, high, levels)
    passed = lag_weights(low)
    make_weights(passed, folded, kappa, embed, weights_ref)
    turned_ref[...] = weights_ref[...].T
    make_tables(ones_ref, class_ref)
    tokens_ref[0:VOCAB, LANES:] = jnp.zeros((VOCAB, LANES), BF16)
    make_hot(tokens_ref, 8 * BACK, ids_ref[...])

    def receive(step):
        id_copies[step].wait()
        make_hot(tokens_ref, 8 * (BACK - 1 - step), jnp.where(seq > step, held[step], -1))

    receive(0)
    make_near(tokens_ref, class_ref, features_ref)
    for step in range(1, BACK):
        receive(step)
    make_far(tokens_ref, ones_ref, s7, s8, s9, s10, features_ref)
    cot_copy.wait()
    mix_sum = forward(turned_ref, features_ref, mix_ref, cot_ref, hidden_ref, g_ref)
    hidden_copy = pltpu.make_async_copy(hidden_ref, hidden_hbm, local_sem.at[1])
    hidden_copy.start()

    def spread(phase, part, target):
        copies = []
        for step in range(1, 4):
            place = 4 * core + lax.rem(mine[0] + step, 4)
            copies.append(
                copy_to(part.at[place], target.at[step - 1], sends.at[phase, step - 1], recvs.at[phase, step - 1], own_peer(0, step))
            )
        for step in range(4):
            place = 4 * (1 - core) + lax.rem(theirs[0] + step, 4)
            copies.append(
                copy_to(part.at[place], target.at[step + 3], sends.at[phase, step + 3], recvs.at[phase, step + 3], their_peer(step))
            )
        return copies

    home = 4 * core + mine[0]
    for chunk in range(8):
        for tile in range(8):
            row = 32 * chunk + 8 * (tile // 2)
            column = LANES * (tile % 2)
            mix_part[chunk, tile] = mix_sum[row : row + 8, column : column + LANES]
    mix_copies = spread(0, mix_part, mix_in)
    small = backward(passed, folded, kappa, embed, features_ref, g_ref, cot_ref, z_ref)
    for chunk in range(8):
        row, column = 8 * (chunk // 2), LANES * (chunk % 2)
        small_part[chunk] = small[row : row + 8, column : column + LANES]
    small_copies = spread(1, small_part, small_in)
    for copy in mix_copies:
        copy.wait()
    mixed = mix_part[home]
    for slot in range(7):
        mixed = mixed + mix_in[slot]
    second[mine[1], 0:8] = mixed
    for copy in small_copies:
        copy.wait()
    rows = small_part[home]
    for slot in range(7):
        rows = rows + small_in[slot]
    second[mine[1], 8] = rows

    def exchange(phase, axis, target):
        spot = target.at[mine[axis]]
        copies = [
            copy_to(spot, spot, sends.at[phase, step], recvs.at[phase, step], own_peer(axis, step))
            for step in range(1, 4)
        ]
        for copy in copies:
            copy.wait()

    exchange(2, 1, second)
    third[mine[2]] = (second[0] + second[1]) + (second[2] + second[3])
    exchange(3, 2, third)
    total[...] = (third[0] + third[1]) + (third[2] + third[3])
    local = pltpu.make_async_copy(total, whole_hbm.at[home], local_sem.at[2])
    local.start()
    copies = []
    for step in range(1, 4):
        copies.append(
            copy_to(total, whole_hbm.at[home], sends.at[4, step - 1], recvs.at[4, step - 1], own_peer(0, step))
        )
    for step in range(4):
        copies.append(
            copy_to(total, whole_hbm.at[home], sends.at[4, step + 3], recvs.at[4, step + 3], cross_peer(step))
        )
    hidden_copy.wait()
    local.wait()
    for copy in copies:
        copy.wait()


def layer(count, ids, embed, low, high, levels, mix, cot):
    vmem = pl.BlockSpec(memory_space=pltpu.VMEM)
    anywhere = pl.BlockSpec(memory_space=pl.ANY)
    tile = (8, LANES)
    return pl.pallas_call(
        functools.partial(layer_kernel, count),
        out_shape=(
            jax.ShapeDtypeStruct((TOKENS, WIDTH), BF16),
            jax.ShapeDtypeStruct((8, 9) + tile, F32),
        ),
        in_specs=[vmem] * 6 + [anywhere],
        out_specs=(anywhere, anywhere),
        scratch_shapes=[
            pltpu.VMEM((BACK,) + tile, jnp.int32),
            pltpu.SemaphoreType.DMA((BACK,)),
            pltpu.SemaphoreType.DMA((BACK,)),
            pltpu.VMEM((2 * LANES, 8 * LANES), BF16),
            pltpu.VMEM((2 * LANES, 29 * LANES), BF16),
            pltpu.VMEM((TILES * VOCAB, 2 * LANES), BF16),
            pltpu.VMEM((8 * VOCAB, TILES * LANES), BF16),
            pltpu.VMEM((9 * VOCAB, TILES * LANES), BF16),
            pltpu.VMEM((10 * VOCAB, TILES * LANES), BF16),
            pltpu.VMEM((11 * VOCAB, TILES * LANES), BF16),
            pltpu.VMEM((ROWS, TOKENS), BF16),
            pltpu.VMEM((ROWS, 2 * WIDTH), BF16),
            pltpu.VMEM((2 * WIDTH, ROWS), BF16),
            pltpu.VMEM((TOKENS, WIDTH), BF16),
            pltpu.VMEM((TOKENS, WIDTH), BF16),
            pltpu.VMEM((TOKENS, 2 * WIDTH), BF16),
            pltpu.VMEM((CLASSES * VOCAB, WIDTH), F32),
            pltpu.SemaphoreType.DMA((3,)),
            pltpu.VMEM((8, 8) + tile, F32),
            pltpu.VMEM((8,) + tile, F32),
            pltpu.VMEM((7, 8) + tile, F32),
            pltpu.VMEM((7,) + tile, F32),
            pltpu.VMEM((4, 9) + tile, F32),
            pltpu.VMEM((4, 9) + tile, F32),
            pltpu.VMEM((9,) + tile, F32),
            pltpu.SemaphoreType.DMA((5, 8)),
            pltpu.SemaphoreType.DMA((5, 8)),
        ],
        compiler_params=pltpu.CompilerParams(
            collective_id=0, has_side_effects=True, vmem_limit_bytes=56 * 2**20
        ),
    )(ids, embed, low, high, levels, mix, cot)


def finish_kernel(
    scale, ids_ref, hidden_hbm, whole_hbm, embed_in_ref, mix_in_ref, low_ref, high_ref, levels_ref,
    out_hbm, filters_ref, grad_levels_ref, mix_hbm, embed_ref,
    hidden, whole, out, mix, sems,
):
    parts = 4
    length = TOKENS // parts
    spans = [pl.ds(part * length, length) for part in range(parts)]
    loads = [pltpu.make_async_copy(hidden_hbm.at[span], hidden.at[span], sems.at[0, part]) for part, span in enumerate(spans)]
    for load in loads:
        load.start()
    whole_load = pltpu.make_async_copy(whole_hbm, whole, sems.at[2, 0])
    whole_load.start()
    stores = []
    embed = embed_in_ref[...]
    high_part, middle = halves(embed)
    rest = (embed - high_part.astype(F32) - middle.astype(F32)).astype(BF16)
    table = jnp.concatenate([high_part, middle, rest], axis=0)
    names = lax.broadcasted_iota(jnp.int32, (VOCAB, LANES), 0)
    for part in range(parts):
        hot = jnp.concatenate(
            [
                where_is(names, jnp.broadcast_to(ids_ref[tile : tile + 1, :], (VOCAB, LANES)))
                for tile in range(2 * part, 2 * part + 2)
            ],
            axis=1,
        )
        hot = jnp.concatenate([hot, hot, hot], axis=0)
        x = lax.dot_general(hot, table, (((0,), (0,)), ((), ())), preferred_element_type=F32)
        loads[part].wait()
        rows = slice(part * length, (part + 1) * length)
        out[rows, :] = x + dot(hidden[rows, :], mix_in_ref[...])
        store = pltpu.make_async_copy(out.at[spans[part]], out_hbm.at[spans[part]], sems.at[1, part])
        store.start()
        stores.append(store)
    whole_load.wait()
    for chunk in range(8):
        for tile in range(8):
            row = 32 * chunk + 8 * (tile // 2)
            start = LANES * (tile % 2)
            mix[row : row + 8, start : start + LANES] = scale * whole[chunk, tile]
    store = pltpu.make_async_copy(mix, mix_hbm, sems.at[2, 1])
    store.start()
    stores.append(store)
    quarters = [
        scale * jnp.concatenate([whole[2 * quarter, 8], whole[2 * quarter + 1, 8]], axis=1)
        for quarter in range(4)
    ]
    embed_ref[0:8, :] = quarters[2]
    embed_ref[8:16, :] = quarters[3]
    shifted = [quarters[row // 8][row % 8 : row % 8 + 1] for row in range(1, 14)]
    zero_inner, one_inner = quarters[1][6:7], quarters[1][7:8]
    low, high, levels = rows_of(low_ref), rows_of(high_ref), rows_of(levels_ref)
    folded, _ = level_factors(low, high, levels)
    current = quarters[0][0:1]
    low_zero, low_one = zero_inner / low[0], one_inner / low[1]
    high_zero = high_one = jnp.zeros_like(current)
    for level in range(LEVELS):
        late = shifted[level]
        grad_levels_ref[level : level + 1, :] = high[0] * current + high[1] * late
        low_zero = low_zero + folded[level + 1] * current
        low_one = low_one + folded[level + 1] * late
        high_zero = high_zero + levels[level] * current
        high_one = high_one + levels[level] * late
        current = low[0] * current + low[1] * late
    grad_levels_ref[LEVELS : LEVELS + 1, :] = current
    filters_ref[0, 0:1, :] = low_zero
    filters_ref[0, 1:2, :] = low_one
    filters_ref[1, 0:1, :] = high_zero
    filters_ref[1, 1:2, :] = high_one
    for store in stores:
        store.wait()


def finish(scale, ids, hidden, whole, embed, mix, low, high, levels):
    vmem = pl.BlockSpec(memory_space=pltpu.VMEM)
    anywhere = pl.BlockSpec(memory_space=pl.ANY)
    return pl.pallas_call(
        functools.partial(finish_kernel, scale),
        out_shape=(
            jax.ShapeDtypeStruct((TOKENS, WIDTH), F32),
            jax.ShapeDtypeStruct((2, 2, WIDTH), F32),
            jax.ShapeDtypeStruct((LEVELS + 1, WIDTH), F32),
            jax.ShapeDtypeStruct((WIDTH, WIDTH), F32),
            jax.ShapeDtypeStruct((VOCAB, WIDTH), F32),
        ),
        in_specs=[vmem, anywhere, anywhere] + [vmem] * 5,
        out_specs=(anywhere, vmem, vmem, anywhere, vmem),
        scratch_shapes=[
            pltpu.VMEM((TOKENS, WIDTH), BF16),
            pltpu.VMEM((8, 9, 8, LANES), F32),
            pltpu.VMEM((TOKENS, WIDTH), F32),
            pltpu.VMEM((WIDTH, WIDTH), F32),
            pltpu.SemaphoreType.DMA((3, 4)),
        ],
        compiler_params=pltpu.CompilerParams(vmem_limit_bytes=56 * 2**20),
    )(ids, hidden, whole, embed, mix, low, high, levels)


def per_device(ids, embed, low_filter, high_filter, level_weights, mix, cotangent):
    count = lax.axis_size("seq")
    ids = ids.reshape(8, LANES)
    hidden, whole = layer(count, ids, embed, low_filter, high_filter, level_weights, mix, cotangent[0])
    scale = 1.0 / math.sqrt(count * lax.axis_size("batch") * TOKENS)
    out, grad_filters, grad_levels, grad_mix, grad_embed = finish(
        scale, ids, hidden, whole, embed, mix, low_filter, high_filter, level_weights
    )
    return out[None], grad_filters, grad_levels, grad_mix, grad_embed


def solution(mesh):
    placed = (P("batch", "seq"), P(), P(), P(), P(), P(), P("batch", "seq", None))
    return jax.shard_map(
        per_device,
        mesh=mesh,
        in_specs=placed,
        out_specs=(P("batch", "seq", None), P(), P(), P(), P()),
        check_vma=False,
    )
```

```python
import functools
import math

import jax
import jax.numpy as jnp
from jax import lax
from jax.experimental import pallas as pl
from jax.experimental.pallas import tpu as pltpu
from jax.sharding import PartitionSpec as P

MESH = pl.DeviceIdType.MESH
F32, BF16 = jnp.float32, jnp.bfloat16
LEVELS = 13
VOCAB = 16
WIDTH = 256
LANES = 128
TOKENS = 1024
BACK = 8
TILES = (BACK + 1) * TOKENS // LANES
CLASSES = 1 + LEVELS * (LEVELS + 1) // 2
ROWS = 96 * VOCAB
NEAR = 56 * VOCAB
CHUNKS = 32


def class_of(level, ones):
    return 1 + level * (level + 1) // 2 + ones


def block_of(level, ones):
    return slice(class_of(level, ones) * VOCAB, (class_of(level, ones) + 1) * VOCAB)


def dot(a, b):
    return jnp.dot(a, b, preferred_element_type=F32)


def halves(value):
    high = value.astype(BF16)
    return high, (value - high.astype(F32)).astype(BF16)


def level_factors(low, high, weights):
    folded = [None] * (LEVELS + 1)
    kappa = [None] * LEVELS
    folded[LEVELS] = weights[LEVELS]
    for level in range(LEVELS - 1, -1, -1):
        kappa[level] = weights[level] * high[1] + low[1] * folded[level + 1]
        folded[level] = weights[level] * high[0] + low[0] * folded[level + 1]
    return folded, kappa


def rows_of(ref):
    return [ref[row : row + 1, :] for row in range(ref.shape[0])]


def lag_weights(low):
    chains = []
    for row in low:
        chain = [jnp.ones_like(row)]
        for _ in range(LEVELS - 1):
            chain.append(chain[-1] * row)
        chains.append(chain)
    return lambda level, ones: chains[0][level - ones] * chains[1][ones]


def make_weights(passed, folded, kappa, embed, weights_ref):
    def put(rows, factor):
        high, rest = halves(factor * embed)
        weights_ref[rows, 0:WIDTH] = high
        weights_ref[rows, WIDTH:] = rest

    put(slice(0, VOCAB), folded[0])
    for level in range(LEVELS):
        for ones in range(level + 1):
            put(block_of(level, ones), kappa[level] * passed(level, ones))
    weights_ref[CLASSES * VOCAB :, :] = jnp.zeros((ROWS - CLASSES * VOCAB, 2 * WIDTH), BF16)


def where_is(table, value):
    return jnp.where(table == value, 1.0, 0.0).astype(BF16)


def make_tables(ones_ref, class_ref):
    place = lax.broadcasted_iota(jnp.int32, (2 * LANES, LANES), 0)
    lag = lax.broadcasted_iota(jnp.int32, (2 * LANES, LANES), 1) - place
    lag = jnp.where(place >= LANES, lag + 2 * LANES, lag)
    inside = (lag >= 0) & (lag < LANES)
    ones = jnp.zeros_like(lag)
    offset = jnp.zeros_like(lag)
    for bit in range(7):
        ones = ones + ((lag >> bit) & 1)
        offset = offset + jnp.where(lag >= 2**bit, bit, 0)
    klass = jnp.where(inside, jnp.where(lag == 0, 0, offset + ones), -1)
    ones = jnp.where(inside, ones, -1)
    for value in range(8):
        ones_ref[:, value * LANES : (value + 1) * LANES] = where_is(ones, value)
    for value in range(29):
        class_ref[:, value * LANES : (value + 1) * LANES] = where_is(klass, value)


def make_hot(tokens_ref, first, ids):
    names = lax.broadcasted_iota(jnp.int32, (VOCAB, LANES), 0)
    for row in range(8):
        tile = first + row
        hot = where_is(names, jnp.broadcast_to(ids[row : row + 1, :], (VOCAB, LANES)))
        tokens_ref[tile * VOCAB : (tile + 1) * VOCAB, 0:LANES] = hot
        if tile + 1 < TILES:
            tokens_ref[(tile + 1) * VOCAB : (tile + 2) * VOCAB, LANES:] = hot


def put_counts(result, s7, first, last, pair):
    for tile in range(first, last):
        for half in range(2):
            value = 2 * pair + half
            s7[value * VOCAB : (value + 1) * VOCAB, tile * LANES : (tile + 1) * LANES] = result[
                (tile - first) * VOCAB : (tile - first + 1) * VOCAB, half * LANES : (half + 1) * LANES
            ]


def count_tiles(tokens_ref, ones_ref, s7, first, last):
    for pair in range(4):
        table = ones_ref[:, 2 * pair * LANES : 2 * (pair + 1) * LANES]
        result = dot(tokens_ref[first * VOCAB : last * VOCAB, :], table).astype(BF16)
        put_counts(result, s7, first, last, pair)


def widened(source, level, ones, first, last):
    begin, end, span = first * LANES, last * LANES, 2**level
    total = None
    if 0 <= ones <= level:
        total = source[ones * VOCAB : (ones + 1) * VOCAB, begin:end]
    if 1 <= ones <= level + 1:
        late = source[(ones - 1) * VOCAB : ones * VOCAB, begin - span : end - span]
        total = late if total is None else total + late
    return total


def widen(source, target, level, first, last):
    for ones in range(level + 2):
        target[ones * VOCAB : (ones + 1) * VOCAB, first * LANES : last * LANES] = widened(
            source, level, ones, first, last
        )


def place_level(source, level, features_ref):
    rows = slice(class_of(level, 0) * VOCAB, class_of(level + 1, 0) * VOCAB)
    begin = BACK * TOKENS - 2**level
    features_ref[rows, :] = source[:, begin : begin + TOKENS]


def make_near(tokens_ref, class_ref, ones_ref, s7, s8, s9, features_ref):
    own = tokens_ref[64 * VOCAB : 72 * VOCAB, :]
    for first in range(0, 29, 2):
        members = range(first, min(first + 2, 29))
        result = dot(own, class_ref[:, first * LANES : (first + len(members)) * LANES]).astype(BF16)
        for tile in range(8):
            for half, member in enumerate(members):
                features_ref[member * VOCAB : (member + 1) * VOCAB, tile * LANES : (tile + 1) * LANES] = result[
                    tile * VOCAB : (tile + 1) * VOCAB, half * LANES : (half + 1) * LANES
                ]
    count_tiles(tokens_ref, ones_ref, s7, 57, 71)
    widen(s7, s8, 7, 58, 70)
    widen(s8, s9, 8, 60, 68)
    place_level(s7, 7, features_ref)
    place_level(s8, 8, features_ref)
    place_level(s9, 9, features_ref)


def make_far(tokens_ref, ones_ref, s7, s8, s9, s10, features_ref):
    count_tiles(tokens_ref, ones_ref, s7, 1, 57)
    widen(s7, s8, 7, 2, 58)
    widen(s8, s9, 8, 4, 60)
    widen(s9, s10, 9, 8, 64)
    place_level(s10, 10, features_ref)
    for ones in range(12):
        features_ref[block_of(11, ones), :] = widened(s10, 10, ones, 48, 56)
    for ones in range(13):
        near, late = widened(s10, 10, ones, 32, 40), widened(s10, 10, ones - 1, 16, 24)
        features_ref[block_of(12, ones), :] = late if near is None else near if late is None else near + late


def gelu_parts(y):
    root = math.sqrt(2.0 / math.pi)
    square = y * y
    bend = jnp.tanh(root * (y + 0.044715 * square * y))
    half = 0.5 * (1.0 + bend)
    slope = half + 0.5 * y * (1.0 - bend * bend) * (root * (1.0 + 3 * 0.044715 * square))
    return y * half, slope


def near_part(turned_ref, features_ref, y_ref):
    for start in range(0, TOKENS, 256):
        span = slice(start, start + 256)
        both = dot(turned_ref[:, 0:NEAR], features_ref[0:NEAR, span])
        y_ref[:, span] = both[:WIDTH] + both[WIDTH:]


def forward(turned_ref, features_ref, y_ref, mix_ref, cot_ref, hidden_ref, g_ref):
    mix = mix_ref[...]
    mix_sum = None
    block = 256
    for start in range(0, TOKENS, block):
        span = slice(start, start + block)
        both = dot(turned_ref[:, NEAR:], features_ref[NEAR:, span])
        y = (y_ref[:, span] + both[:WIDTH] + both[WIDTH:]).T
        active, slope = gelu_parts(y)
        hidden = active.astype(BF16)
        hidden_ref[span, :] = hidden
        cot = cot_ref[span, :]
        g_hidden = lax.dot_general(cot, mix, (((1,), (1,)), ((), ())), preferred_element_type=F32)
        g_high, g_rest = halves(g_hidden * slope)
        g_ref[span, 0:WIDTH] = g_high
        g_ref[span, WIDTH:] = g_rest
        term = lax.dot_general(hidden, cot, (((0,), (0,)), ((), ())), preferred_element_type=F32)
        mix_sum = term if mix_sum is None else mix_sum + term
    return mix_sum


def backward(passed, folded, kappa, embed, features_ref, g_ref, cot_ref, z_ref):
    both = dot(features_ref[0 : CLASSES * VOCAB, :], g_ref[...])
    z_ref[...] = both[:, :WIDTH] + both[:, WIDTH:]

    def over_names(value):
        return jnp.sum(embed * value, axis=0, keepdims=True)

    z0 = z_ref[0:VOCAB, :]
    rows = [over_names(z0)]
    embed_sum = folded[0] * z0 + dot(features_ref[0:VOCAB, :], cot_ref[...])
    zero_sum = one_sum = jnp.zeros_like(z0)
    for level in range(LEVELS):
        total = passed(level, 0) * z_ref[block_of(level, 0), :]
        counted = jnp.zeros_like(total)
        for ones in range(1, level + 1):
            term = passed(level, ones) * z_ref[block_of(level, ones), :]
            total = total + term
            counted = counted + float(ones) * term
        rows.append(over_names(total))
        embed_sum = embed_sum + kappa[level] * total
        one_sum = one_sum + kappa[level] * counted
        zero_sum = zero_sum + kappa[level] * (float(level) * total - counted)
    rows += [over_names(zero_sum), over_names(one_sum)]
    return jnp.concatenate(rows + [embed_sum], axis=0)


def layer_kernel(
    count, ids_hbm, embed_hbm, low_hbm, high_hbm, levels_hbm, mix_hbm, cot_hbm,
    hidden_ref, whole,
    held, ids_send, ids_recv, ones_ref, class_ref, tokens_ref, s7, s8, s9, s10, features_ref, weights_ref, turned_ref,
    y_ref, g_ref, z_ref, ids_ref, embed_ref, low_ref, high_ref, levels_ref, mix_ref, cot_ref, local_sem,
    mix_part, small_part, mix_in, small_in, second, third, sends, recvs,
):
    seq, batch = lax.axis_index("seq"), lax.axis_index("batch")
    x, y = lax.rem(seq, 4), lax.rem(lax.div(seq, 4), 4)
    core = lax.rem(batch, 2)
    z = lax.div(seq, 16) * 2 + lax.div(batch, 2)

    def along(order):
        return x + order * (y - x), y + order * (z - y), z + order * (x - z)

    def device(order, spots, core):
        a, b, c = spots
        x, y, z = a + order * (c - a), b + order * (a - b), c + order * (b - c)
        return lax.div(z, 2) * 16 + y * 4 + x, lax.rem(z, 2) * 2 + core

    def moved(spots, i, j, k):
        return lax.rem(spots[0] + i, 4), lax.rem(spots[1] + j, 4), lax.rem(spots[2] + k, 4)

    mine, theirs = along(core), along(1 - core)
    plane = [(i, j) for i in range(4) for j in range(4)]
    others = plane[1:]
    own_peer = lambda i, j, k: device(core, moved(mine, i, j, k), core)
    their_peer = lambda i, j: device(1 - core, moved(theirs, i, j, 0), 1 - core)
    cross_peer = lambda i, j: device(core, moved(mine, i, j, 0), 1 - core)
    chunk_of = lambda core, spots: 16 * core + 4 * spots[0] + spots[1]

    barrier = pltpu.get_barrier_semaphore()

    def greet(peer):
        pl.semaphore_signal(barrier, inc=1, device_id=peer, device_id_type=MESH)

    for step in range(1, BACK + 1):
        greet((lax.rem(seq + count - step, count), batch))
    for i, j in others:
        greet(own_peer(i, j, 0))
    for k in range(1, 4):
        greet(own_peer(0, 0, k))
    for i, j in plane:
        greet(their_peer(i, j))
        if i:
            greet(cross_peer(i + core * (j - i), j + core * (i - j)))
    loads = [
        pltpu.make_async_copy(source, target, local_sem.at[place])
        for place, (source, target) in enumerate(
            [
                (ids_hbm, ids_ref),
                (embed_hbm, embed_ref),
                (low_hbm, low_ref),
                (high_hbm, high_ref),
                (levels_hbm, levels_ref),
                (mix_hbm, mix_ref),
                (cot_hbm, cot_ref),
            ]
        )
    ]
    for load in loads:
        load.start()
    pl.semaphore_wait(barrier, BACK + 46)

    def copy_to(source, target, sent, received, peer):
        copy = pltpu.make_async_remote_copy(
            src_ref=source, dst_ref=target, send_sem=sent, recv_sem=received, device_id=peer, device_id_type=MESH
        )
        copy.start()
        return copy

    id_copies = [
        copy_to(
            ids_hbm, held.at[step], ids_send.at[step], ids_recv.at[step], (lax.rem(seq + step + 1, count), batch)
        )
        for step in range(BACK)
    ]

    for load in loads:
        load.wait()
    embed = embed_ref[...]
    low, high, levels = rows_of(low_ref), rows_of(high_ref), rows_of(levels_ref)
    folded, kappa = level_factors(low, high, levels)
    passed = lag_weights(low)
    make_weights(passed, folded, kappa, embed, weights_ref)
    turned_ref[...] = weights_ref[...].T
    make_tables(ones_ref, class_ref)
    tokens_ref[0:VOCAB, LANES:] = jnp.zeros((VOCAB, LANES), BF16)
    features_ref[CLASSES * VOCAB :, :] = jnp.zeros((ROWS - CLASSES * VOCAB, TOKENS), BF16)
    make_hot(tokens_ref, 8 * BACK, ids_ref[...])

    def receive(step):
        id_copies[step].wait()
        make_hot(tokens_ref, 8 * (BACK - 1 - step), jnp.where(seq > step, held[step], -1))

    receive(0)
    make_near(tokens_ref, class_ref, ones_ref, s7, s8, s9, features_ref)
    near_part(turned_ref, features_ref, y_ref)
    for step in range(1, BACK):
        receive(step)
    make_far(tokens_ref, ones_ref, s7, s8, s9, s10, features_ref)
    mix_sum = forward(turned_ref, features_ref, y_ref, mix_ref, cot_ref, hidden_ref, g_ref)

    def spread(phase, part, target):
        copies = []
        for slot, (i, j) in enumerate(others):
            place = chunk_of(core, moved(mine, i, j, 0))
            copies.append(
                copy_to(part.at[place], target.at[slot], sends.at[phase, slot], recvs.at[phase, slot], own_peer(i, j, 0))
            )
        for slot, (i, j) in enumerate(plane, 15):
            place = chunk_of(1 - core, moved(theirs, i, j, 0))
            copies.append(
                copy_to(part.at[place], target.at[slot], sends.at[phase, slot], recvs.at[phase, slot], their_peer(i, j))
            )
        return copies

    home = chunk_of(core, mine)
    for chunk in range(CHUNKS):
        mix_part[chunk] = mix_sum[8 * chunk : 8 * chunk + 8]
    mix_copies = spread(0, mix_part, mix_in)
    small = backward(passed, folded, kappa, embed, features_ref, g_ref, cot_ref, z_ref)
    for chunk in range(CHUNKS):
        small_part[chunk] = small[chunk : chunk + 1]
    small_copies = spread(1, small_part, small_in)
    for copy in mix_copies:
        copy.wait()
    mixed = mix_part[home]
    for slot in range(CHUNKS - 1):
        mixed = mixed + mix_in[slot]
    for row in range(8):
        second[mine[2], row] = mixed[row : row + 1]
    for copy in small_copies:
        copy.wait()
    row = small_part[home]
    for slot in range(CHUNKS - 1):
        row = row + small_in[slot]
    second[mine[2], 8] = row
    spot = second.at[mine[2]]
    copies = [
        copy_to(spot, spot, sends.at[2, k], recvs.at[2, k], own_peer(0, 0, k)) for k in range(1, 4)
    ]
    for copy in copies:
        copy.wait()
    third[...] = (second[0] + second[1]) + (second[2] + second[3])
    landing = whole.at[pl.ds(9 * home, 9)]
    copies = []
    for slot, (i, j) in enumerate(others):
        copies.append(copy_to(third, landing, sends.at[3, slot], recvs.at[3, slot], own_peer(i, j, 0)))
    for slot, (i, j) in enumerate(plane, 15):
        copies.append(copy_to(third, landing, sends.at[3, slot], recvs.at[3, slot], cross_peer(i, j)))
    whole[pl.ds(9 * home, 9)] = third[...]
    for copy in copies:
        copy.wait()


def layer(count, ids, embed, low, high, levels, mix, cot):
    vmem = pl.BlockSpec(memory_space=pltpu.VMEM)
    far = pl.BlockSpec(memory_space=pltpu.HBM)
    arguments = (ids, embed, low, high, levels, mix, cot)
    return pl.pallas_call(
        functools.partial(layer_kernel, count),
        out_shape=(
            jax.ShapeDtypeStruct((TOKENS, WIDTH), BF16),
            jax.ShapeDtypeStruct((9 * CHUNKS, 1, WIDTH), F32),
        ),
        in_specs=[far] * 7,
        out_specs=(vmem, vmem),
        scratch_shapes=[
            pltpu.VMEM((BACK, 8, LANES), jnp.int32),
            pltpu.SemaphoreType.DMA((BACK,)),
            pltpu.SemaphoreType.DMA((BACK,)),
            pltpu.VMEM((2 * LANES, 8 * LANES), BF16),
            pltpu.VMEM((2 * LANES, 29 * LANES), BF16),
            pltpu.VMEM((TILES * VOCAB, 2 * LANES), BF16),
            pltpu.VMEM((8 * VOCAB, TILES * LANES), BF16),
            pltpu.VMEM((9 * VOCAB, TILES * LANES), BF16),
            pltpu.VMEM((10 * VOCAB, TILES * LANES), BF16),
            pltpu.VMEM((11 * VOCAB, TILES * LANES), BF16),
            pltpu.VMEM((ROWS, TOKENS), BF16),
            pltpu.VMEM((ROWS, 2 * WIDTH), BF16),
            pltpu.VMEM((2 * WIDTH, ROWS), BF16),
            pltpu.VMEM((WIDTH, TOKENS), F32),
            pltpu.VMEM((TOKENS, 2 * WIDTH), BF16),
            pltpu.VMEM((CLASSES * VOCAB, WIDTH), F32),
            *[pltpu.VMEM(array.shape, array.dtype) for array in arguments],
            pltpu.SemaphoreType.DMA((7,)),
            pltpu.VMEM((CHUNKS, 8, WIDTH), F32),
            pltpu.VMEM((CHUNKS, 1, WIDTH), F32),
            pltpu.VMEM((CHUNKS - 1, 8, WIDTH), F32),
            pltpu.VMEM((CHUNKS - 1, 1, WIDTH), F32),
            pltpu.VMEM((4, 9, 1, WIDTH), F32),
            pltpu.VMEM((9, 1, WIDTH), F32),
            pltpu.SemaphoreType.DMA((4, CHUNKS)),
            pltpu.SemaphoreType.DMA((4, CHUNKS)),
        ],
        compiler_params=pltpu.CompilerParams(
            collective_id=0, has_side_effects=True, vmem_limit_bytes=44 * 2**20
        ),
    )(*arguments)


def finish_kernel(
    scale, ids_ref, hidden_ref, whole, embed_in_ref, mix_in_ref, low_ref, high_ref, levels_ref,
    out_ref, filters_ref, grad_levels_ref, mix_ref, embed_ref,
):
    embed = embed_in_ref[...]
    high_part, middle = halves(embed)
    rest = (embed - high_part.astype(F32) - middle.astype(F32)).astype(BF16)
    table = jnp.concatenate([high_part, middle, rest], axis=0)
    names = lax.broadcasted_iota(jnp.int32, (VOCAB, LANES), 0)
    for tile in range(8):
        rows = slice(tile * LANES, (tile + 1) * LANES)
        hot = where_is(names, jnp.broadcast_to(ids_ref[tile : tile + 1, :], (VOCAB, LANES)))
        hot = jnp.concatenate([hot, hot, hot], axis=0)
        x = lax.dot_general(hot, table, (((0,), (0,)), ((), ())), preferred_element_type=F32)
        out_ref[rows, :] = x + dot(hidden_ref[rows, :], mix_in_ref[...])
    for chunk in range(CHUNKS):
        for row in range(8):
            mix_ref[8 * chunk + row : 8 * chunk + row + 1, :] = scale * whole[9 * chunk + row]
    summed = [scale * whole[9 * chunk + 8] for chunk in range(CHUNKS)]
    for name in range(VOCAB):
        embed_ref[name : name + 1, :] = summed[16 + name]
    shifted = summed[1:14]
    zero_inner, one_inner = summed[14], summed[15]
    low, high, levels = rows_of(low_ref), rows_of(high_ref), rows_of(levels_ref)
    folded, _ = level_factors(low, high, levels)
    current = summed[0]
    low_zero, low_one = zero_inner / low[0], one_inner / low[1]
    high_zero = high_one = jnp.zeros_like(current)
    for level in range(LEVELS):
        late = shifted[level]
        grad_levels_ref[level : level + 1, :] = high[0] * current + high[1] * late
        low_zero = low_zero + folded[level + 1] * current
        low_one = low_one + folded[level + 1] * late
        high_zero = high_zero + levels[level] * current
        high_one = high_one + levels[level] * late
        current = low[0] * current + low[1] * late
    grad_levels_ref[LEVELS : LEVELS + 1, :] = current
    filters_ref[0, 0:1, :] = low_zero
    filters_ref[0, 1:2, :] = low_one
    filters_ref[1, 0:1, :] = high_zero
    filters_ref[1, 1:2, :] = high_one


def finish(scale, ids, hidden, whole, embed, mix, low, high, levels):
    vmem = pl.BlockSpec(memory_space=pltpu.VMEM)
    return pl.pallas_call(
        functools.partial(finish_kernel, scale),
        out_shape=(
            jax.ShapeDtypeStruct((TOKENS, WIDTH), F32),
            jax.ShapeDtypeStruct((2, 2, WIDTH), F32),
            jax.ShapeDtypeStruct((LEVELS + 1, WIDTH), F32),
            jax.ShapeDtypeStruct((WIDTH, WIDTH), F32),
            jax.ShapeDtypeStruct((VOCAB, WIDTH), F32),
        ),
        in_specs=[vmem] * 8,
        out_specs=(vmem,) * 5,
        compiler_params=pltpu.CompilerParams(vmem_limit_bytes=16 * 2**20),
    )(ids, hidden, whole, embed, mix, low, high, levels)


def per_device(ids, embed, low_filter, high_filter, level_weights, mix, cotangent):
    count = lax.axis_size("seq")
    ids = ids.reshape(8, LANES)
    hidden, whole = layer(count, ids, embed, low_filter, high_filter, level_weights, mix, cotangent[0])
    scale = 1.0 / math.sqrt(count * lax.axis_size("batch") * TOKENS)
    out, grad_filters, grad_levels, grad_mix, grad_embed = finish(
        scale, ids, hidden, whole, embed, mix, low_filter, high_filter, level_weights
    )
    return out[None], grad_filters, grad_levels, grad_mix, grad_embed


def solution(mesh):
    placed = (P("batch", "seq"), P(), P(), P(), P(), P(), P("batch", "seq", None))
    return jax.shard_map(
        per_device,
        mesh=mesh,
        in_specs=placed,
        out_specs=(P("batch", "seq", None), P(), P(), P(), P()),
        check_vma=False,
    )
```

```python
import functools
import math

import jax
import jax.numpy as jnp
from jax import lax
from jax.experimental import pallas as pl
from jax.experimental.pallas import tpu as pltpu
from jax.sharding import PartitionSpec as P

MESH = pl.DeviceIdType.MESH
F32, BF16 = jnp.float32, jnp.bfloat16
LEVELS = 13
VOCAB = 16
WIDTH = 256
LANES = 128
TOKENS = 1024
BACK = 8
TILES = (BACK + 1) * TOKENS // LANES
CLASSES = 1 + LEVELS * (LEVELS + 1) // 2
ROWS = 96 * VOCAB
NEAR = 56 * VOCAB
CHUNKS = 32


def class_of(level, ones):
    return 1 + level * (level + 1) // 2 + ones


def block_of(level, ones):
    return slice(class_of(level, ones) * VOCAB, (class_of(level, ones) + 1) * VOCAB)


def dot(a, b):
    return jnp.dot(a, b, preferred_element_type=F32)


def halves(value):
    high = value.astype(BF16)
    return high, (value - high.astype(F32)).astype(BF16)


def level_factors(low, high, weights):
    folded = [None] * (LEVELS + 1)
    kappa = [None] * LEVELS
    folded[LEVELS] = weights[LEVELS]
    for level in range(LEVELS - 1, -1, -1):
        kappa[level] = weights[level] * high[1] + low[1] * folded[level + 1]
        folded[level] = weights[level] * high[0] + low[0] * folded[level + 1]
    return folded, kappa


def rows_of(ref):
    return [ref[row : row + 1, :] for row in range(ref.shape[0])]


def lag_weights(low):
    chains = []
    for row in low:
        chain = [jnp.ones_like(row)]
        for _ in range(LEVELS - 1):
            chain.append(chain[-1] * row)
        chains.append(chain)
    return lambda level, ones: chains[0][level - ones] * chains[1][ones]


def make_weights(passed, folded, kappa, embed, weights_ref):
    def put(rows, factor):
        high, rest = halves(factor * embed)
        weights_ref[rows, 0:WIDTH] = high
        weights_ref[rows, WIDTH:] = rest

    put(slice(0, VOCAB), folded[0])
    for level in range(LEVELS):
        for ones in range(level + 1):
            put(block_of(level, ones), kappa[level] * passed(level, ones))
    weights_ref[CLASSES * VOCAB :, :] = jnp.zeros((ROWS - CLASSES * VOCAB, 2 * WIDTH), BF16)


def where_is(table, value):
    return jnp.where(table == value, 1.0, 0.0).astype(BF16)


def make_tables(ones_ref, class_ref):
    place = lax.broadcasted_iota(jnp.int32, (2 * LANES, LANES), 0)
    lag = lax.broadcasted_iota(jnp.int32, (2 * LANES, LANES), 1) - place
    lag = jnp.where(place >= LANES, lag + 2 * LANES, lag)
    inside = (lag >= 0) & (lag < LANES)
    ones = jnp.zeros_like(lag)
    offset = jnp.zeros_like(lag)
    for bit in range(7):
        ones = ones + ((lag >> bit) & 1)
        offset = offset + jnp.where(lag >= 2**bit, bit, 0)
    klass = jnp.where(inside, jnp.where(lag == 0, 0, offset + ones), -1)
    ones = jnp.where(inside, ones, -1)
    for value in range(8):
        ones_ref[:, value * LANES : (value + 1) * LANES] = where_is(ones, value)
    for value in range(29):
        class_ref[:, value * LANES : (value + 1) * LANES] = where_is(klass, value)


def make_hot(tokens_ref, first, ids):
    names = lax.broadcasted_iota(jnp.int32, (VOCAB, LANES), 0)
    for row in range(8):
        tile = first + row
        hot = where_is(names, jnp.broadcast_to(ids[row : row + 1, :], (VOCAB, LANES)))
        tokens_ref[tile * VOCAB : (tile + 1) * VOCAB, 0:LANES] = hot
        if tile + 1 < TILES:
            tokens_ref[(tile + 1) * VOCAB : (tile + 2) * VOCAB, LANES:] = hot


def put_counts(result, s7, first, last, pair):
    for tile in range(first, last):
        for half in range(2):
            value = 2 * pair + half
            s7[value * VOCAB : (value + 1) * VOCAB, tile * LANES : (tile + 1) * LANES] = result[
                (tile - first) * VOCAB : (tile - first + 1) * VOCAB, half * LANES : (half + 1) * LANES
            ]


def count_tiles(tokens_ref, ones_ref, s7, first, last):
    for pair in range(4):
        table = ones_ref[:, 2 * pair * LANES : 2 * (pair + 1) * LANES]
        result = dot(tokens_ref[first * VOCAB : last * VOCAB, :], table).astype(BF16)
        put_counts(result, s7, first, last, pair)


def widened(source, level, ones, first, last):
    begin, end, span = first * LANES, last * LANES, 2**level
    total = None
    if 0 <= ones <= level:
        total = source[ones * VOCAB : (ones + 1) * VOCAB, begin:end]
    if 1 <= ones <= level + 1:
        late = source[(ones - 1) * VOCAB : ones * VOCAB, begin - span : end - span]
        total = late if total is None else total + late
    return total


def widen(source, target, level, first, last):
    for ones in range(level + 2):
        target[ones * VOCAB : (ones + 1) * VOCAB, first * LANES : last * LANES] = widened(
            source, level, ones, first, last
        )


def place_level(source, level, features_ref):
    rows = slice(class_of(level, 0) * VOCAB, class_of(level + 1, 0) * VOCAB)
    begin = BACK * TOKENS - 2**level
    features_ref[rows, :] = source[:, begin : begin + TOKENS]


def make_near(tokens_ref, class_ref, ones_ref, s7, s8, s9, features_ref):
    own = tokens_ref[64 * VOCAB : 72 * VOCAB, :]
    for first in range(0, 29, 2):
        members = range(first, min(first + 2, 29))
        result = dot(own, class_ref[:, first * LANES : (first + len(members)) * LANES]).astype(BF16)
        for tile in range(8):
            for half, member in enumerate(members):
                features_ref[member * VOCAB : (member + 1) * VOCAB, tile * LANES : (tile + 1) * LANES] = result[
                    tile * VOCAB : (tile + 1) * VOCAB, half * LANES : (half + 1) * LANES
                ]
    count_tiles(tokens_ref, ones_ref, s7, 57, 71)
    widen(s7, s8, 7, 58, 70)
    widen(s8, s9, 8, 60, 68)
    place_level(s7, 7, features_ref)
    place_level(s8, 8, features_ref)
    place_level(s9, 9, features_ref)


def make_far(tokens_ref, ones_ref, s7, s8, s9, s10, features_ref):
    count_tiles(tokens_ref, ones_ref, s7, 1, 57)
    widen(s7, s8, 7, 2, 58)
    widen(s8, s9, 8, 4, 60)
    widen(s9, s10, 9, 8, 64)
    place_level(s10, 10, features_ref)
    for ones in range(12):
        features_ref[block_of(11, ones), :] = widened(s10, 10, ones, 48, 56)
    for ones in range(13):
        near, late = widened(s10, 10, ones, 32, 40), widened(s10, 10, ones - 1, 16, 24)
        features_ref[block_of(12, ones), :] = late if near is None else near if late is None else near + late


def gelu_parts(y):
    root = math.sqrt(2.0 / math.pi)
    square = y * y
    bend = jnp.tanh(root * (y + 0.044715 * square * y))
    half = 0.5 * (1.0 + bend)
    slope = half + 0.5 * y * (1.0 - bend * bend) * (root * (1.0 + 3 * 0.044715 * square))
    return y * half, slope


def near_part(turned_ref, features_ref, y_ref):
    for start in range(0, TOKENS, 256):
        span = slice(start, start + 256)
        both = dot(turned_ref[:, 0:NEAR], features_ref[0:NEAR, span])
        y_ref[:, span] = both[:WIDTH] + both[WIDTH:]


def forward(turned_ref, features_ref, y_ref, mix_ref, cot_ref, hidden_ref, g_ref):
    mix = mix_ref[...]
    mix_sum = None
    block = 256
    for start in range(0, TOKENS, block):
        span = slice(start, start + block)
        both = dot(turned_ref[:, NEAR:], features_ref[NEAR:, span])
        y = (y_ref[:, span] + both[:WIDTH] + both[WIDTH:]).T
        active, slope = gelu_parts(y)
        hidden = active.astype(BF16)
        hidden_ref[span, :] = hidden
        cot = cot_ref[span, :]
        g_hidden = lax.dot_general(cot, mix, (((1,), (1,)), ((), ())), preferred_element_type=F32)
        g_high, g_rest = halves(g_hidden * slope)
        g_ref[span, 0:WIDTH] = g_high
        g_ref[span, WIDTH:] = g_rest
        term = lax.dot_general(hidden, cot, (((0,), (0,)), ((), ())), preferred_element_type=F32)
        mix_sum = term if mix_sum is None else mix_sum + term
    return mix_sum


def outputs(embed, features_ref, hidden_ref, mix_ref, out_ref):
    high, middle = halves(embed)
    rest = (embed - high.astype(F32) - middle.astype(F32)).astype(BF16)
    table = jnp.concatenate([high, middle, rest], axis=0)
    for start in range(0, TOKENS, 256):
        span = slice(start, start + 256)
        hot = features_ref[0:VOCAB, span]
        hot = jnp.concatenate([hot, hot, hot], axis=0)
        x = lax.dot_general(hot, table, (((0,), (0,)), ((), ())), preferred_element_type=F32)
        out_ref[span, :] = x + dot(hidden_ref[span, :], mix_ref[...])


def backward(passed, folded, kappa, embed, features_ref, g_ref, cot_ref, z_ref):
    both = dot(features_ref[0 : CLASSES * VOCAB, :], g_ref[...])
    z_ref[...] = both[:, :WIDTH] + both[:, WIDTH:]

    def over_names(value):
        return jnp.sum(embed * value, axis=0, keepdims=True)

    z0 = z_ref[0:VOCAB, :]
    rows = [over_names(z0)]
    embed_sum = folded[0] * z0 + dot(features_ref[0:VOCAB, :], cot_ref[...])
    zero_sum = one_sum = jnp.zeros_like(z0)
    for level in range(LEVELS):
        total = passed(level, 0) * z_ref[block_of(level, 0), :]
        counted = jnp.zeros_like(total)
        for ones in range(1, level + 1):
            term = passed(level, ones) * z_ref[block_of(level, ones), :]
            total = total + term
            counted = counted + float(ones) * term
        rows.append(over_names(total))
        embed_sum = embed_sum + kappa[level] * total
        one_sum = one_sum + kappa[level] * counted
        zero_sum = zero_sum + kappa[level] * (float(level) * total - counted)
    rows += [over_names(zero_sum), over_names(one_sum)]
    return jnp.concatenate(rows + [embed_sum], axis=0)


def layer_kernel(
    count, scale, ids_hbm, embed_hbm, low_hbm, high_hbm, levels_hbm, mix_hbm, cot_hbm,
    out_ref, whole, factors_ref,
    held, ids_sems, ones_ref, class_ref, tokens_ref, s7, s8, s9, s10, features_ref, weights_ref, turned_ref,
    y_ref, hidden_ref, g_ref, z_ref, ids_ref, embed_ref, low_ref, high_ref, levels_ref, mix_ref, cot_ref, local_sem,
    mix_part, small_part, mix_in, small_in, second, third, sends, recvs,
):
    seq, batch = lax.axis_index("seq"), lax.axis_index("batch")
    x, y = lax.rem(seq, 4), lax.rem(lax.div(seq, 4), 4)
    core = lax.rem(batch, 2)
    z = lax.div(seq, 16) * 2 + lax.div(batch, 2)

    def along(order):
        return x + order * (y - x), y + order * (z - y), z + order * (x - z)

    def device(order, spots, core):
        a, b, c = spots
        x, y, z = a + order * (c - a), b + order * (a - b), c + order * (b - c)
        return lax.div(z, 2) * 16 + y * 4 + x, lax.rem(z, 2) * 2 + core

    def moved(spots, i, j, k):
        return lax.rem(spots[0] + i, 4), lax.rem(spots[1] + j, 4), lax.rem(spots[2] + k, 4)

    mine, theirs = along(core), along(1 - core)
    hops = lambda spot: sum(min(step, 4 - step) for step in spot)
    plane = sorted([(i, j) for i in range(4) for j in range(4)], key=hops, reverse=True)
    others = plane[:-1]
    own_peer = lambda i, j, k: device(core, moved(mine, i, j, k), core)
    their_peer = lambda i, j: device(1 - core, moved(theirs, i, j, 0), 1 - core)
    cross_peer = lambda i, j: device(core, moved(mine, i, j, 0), 1 - core)
    chunk_of = lambda core, spots: 16 * core + 4 * spots[0] + spots[1]

    barrier = pltpu.get_barrier_semaphore()

    def greet(peer):
        pl.semaphore_signal(barrier, inc=1, device_id=peer, device_id_type=MESH)

    for step in range(1, BACK + 1):
        greet((lax.rem(seq + count - step, count), batch))
    for i, j in others:
        greet(own_peer(i, j, 0))
    for k in range(1, 4):
        greet(own_peer(0, 0, k))
    for i, j in plane:
        greet(their_peer(i, j))
        if i:
            greet(cross_peer(i + core * (j - i), j + core * (i - j)))
    loads = [
        pltpu.make_async_copy(source, target, local_sem.at[place])
        for place, (source, target) in enumerate(
            [
                (ids_hbm, ids_ref),
                (embed_hbm, embed_ref),
                (low_hbm, low_ref),
                (high_hbm, high_ref),
                (levels_hbm, levels_ref),
                (mix_hbm, mix_ref),
                (cot_hbm, cot_ref),
            ]
        )
    ]
    for load in loads:
        load.start()
    pl.semaphore_wait(barrier, BACK + 46)

    def copy_to(source, target, sent, received, peer):
        copy = pltpu.make_async_remote_copy(
            src_ref=source, dst_ref=target, send_sem=sent, recv_sem=received, device_id=peer, device_id_type=MESH
        )
        copy.start()
        return copy

    def drain(ref, sem):
        pltpu.make_async_copy(ref, ref, sem).wait()

    for step in reversed(range(BACK)):
        received = ids_sems.at[1 if step else 0]
        copy_to(ids_hbm, held.at[step], ids_sems.at[2], received, (lax.rem(seq + step + 1, count), batch))

    for load in loads:
        load.wait()
    embed = embed_ref[...]
    low, high, levels = rows_of(low_ref), rows_of(high_ref), rows_of(levels_ref)
    folded, kappa = level_factors(low, high, levels)
    passed = lag_weights(low)
    make_weights(passed, folded, kappa, embed, weights_ref)
    turned_ref[...] = weights_ref[...].T
    make_tables(ones_ref, class_ref)
    tokens_ref[0:VOCAB, LANES:] = jnp.zeros((VOCAB, LANES), BF16)
    features_ref[CLASSES * VOCAB :, :] = jnp.zeros((ROWS - CLASSES * VOCAB, TOKENS), BF16)
    make_hot(tokens_ref, 8 * BACK, ids_ref[...])

    def receive(step):
        make_hot(tokens_ref, 8 * (BACK - 1 - step), jnp.where(seq > step, held[step], -1))

    drain(held.at[0], ids_sems.at[0])
    receive(0)
    make_near(tokens_ref, class_ref, ones_ref, s7, s8, s9, features_ref)
    near_part(turned_ref, features_ref, y_ref)
    factors_ref[0:2, :] = low_ref[...]
    factors_ref[2:4, :] = high_ref[...]
    factors_ref[4:18, :] = levels_ref[...]
    for level in range(LEVELS + 1):
        factors_ref[18 + level : 19 + level, :] = folded[level]
    drain(held.at[pl.ds(1, BACK - 1)], ids_sems.at[1])
    for step in range(1, BACK):
        receive(step)
    make_far(tokens_ref, ones_ref, s7, s8, s9, s10, features_ref)
    mix_sum = forward(turned_ref, features_ref, y_ref, mix_ref, cot_ref, hidden_ref, g_ref)

    home = chunk_of(core, mine)

    def spread(phase, part, target):
        for slot, (i, j) in enumerate(plane):
            place = chunk_of(1 - core, moved(theirs, i, j, 0))
            copy_to(part.at[place], target.at[slot + 15], sends.at[phase], recvs.at[phase], their_peer(i, j))
            if (i, j) in others:
                place = chunk_of(core, moved(mine, i, j, 0))
                copy_to(part.at[place], target.at[slot], sends.at[phase], recvs.at[phase], own_peer(i, j, 0))

    for chunk in range(CHUNKS):
        mix_part[chunk] = scale * mix_sum[8 * chunk : 8 * chunk + 8]
    spread(0, mix_part, mix_in)
    small = scale * backward(passed, folded, kappa, embed, features_ref, g_ref, cot_ref, z_ref)
    for chunk in range(CHUNKS):
        small_part[chunk] = small[chunk : chunk + 1]
    spread(1, small_part, small_in)
    drain(mix_in, recvs.at[0])
    mixed = mix_part[home]
    for slot in range(CHUNKS - 1):
        mixed = mixed + mix_in[slot]
    for row in range(8):
        second[mine[2], row] = mixed[row : row + 1]
    drain(small_in, recvs.at[1])
    row = small_part[home]
    for slot in range(CHUNKS - 1):
        row = row + small_in[slot]
    second[mine[2], 8] = row
    spot = second.at[mine[2]]
    for k in (2, 1, 3):
        copy_to(spot, spot, sends.at[2], recvs.at[2], own_peer(0, 0, k))
    outputs(embed, features_ref, hidden_ref, mix_ref, out_ref)
    drain(second.at[pl.ds(0, 3)], recvs.at[2])
    third[...] = (second[0] + second[1]) + (second[2] + second[3])
    landing = whole.at[pl.ds(9 * home, 9)]
    for i, j in plane:
        copy_to(third, landing, sends.at[3], recvs.at[3], cross_peer(i, j))
        if (i, j) in others:
            copy_to(third, landing, sends.at[3], recvs.at[3], own_peer(i, j, 0))
    whole[pl.ds(9 * home, 9)] = third[...]
    drain(held, ids_sems.at[2])
    drain(mix_in, sends.at[0])
    drain(small_in, sends.at[1])
    drain(second.at[pl.ds(0, 3)], sends.at[2])
    gathered = whole.at[pl.ds(0, 9 * (CHUNKS - 1))]
    drain(gathered, recvs.at[3])
    drain(gathered, sends.at[3])


def layer(count, scale, ids, embed, low, high, levels, mix, cot):
    vmem = pl.BlockSpec(memory_space=pltpu.VMEM)
    far = pl.BlockSpec(memory_space=pltpu.HBM)
    arguments = tuple(
        pltpu.with_memory_space_constraint(array, pltpu.HBM) for array in (ids, embed, low, high, levels, mix, cot)
    )
    return pl.pallas_call(
        functools.partial(layer_kernel, count, scale),
        out_shape=(
            jax.ShapeDtypeStruct((TOKENS, WIDTH), F32),
            jax.ShapeDtypeStruct((9 * CHUNKS, 1, WIDTH), F32),
            jax.ShapeDtypeStruct((32, WIDTH), F32),
        ),
        in_specs=[far] * 7,
        out_specs=(vmem,) * 3,
        scratch_shapes=[
            pltpu.VMEM((BACK, 8, LANES), jnp.int32),
            pltpu.SemaphoreType.DMA((3,)),
            pltpu.VMEM((2 * LANES, 8 * LANES), BF16),
            pltpu.VMEM((2 * LANES, 29 * LANES), BF16),
            pltpu.VMEM((TILES * VOCAB, 2 * LANES), BF16),
            pltpu.VMEM((8 * VOCAB, TILES * LANES), BF16),
            pltpu.VMEM((9 * VOCAB, TILES * LANES), BF16),
            pltpu.VMEM((10 * VOCAB, TILES * LANES), BF16),
            pltpu.VMEM((11 * VOCAB, TILES * LANES), BF16),
            pltpu.VMEM((ROWS, TOKENS), BF16),
            pltpu.VMEM((ROWS, 2 * WIDTH), BF16),
            pltpu.VMEM((2 * WIDTH, ROWS), BF16),
            pltpu.VMEM((WIDTH, TOKENS), F32),
            pltpu.VMEM((TOKENS, WIDTH), BF16),
            pltpu.VMEM((TOKENS, 2 * WIDTH), BF16),
            pltpu.VMEM((CLASSES * VOCAB, WIDTH), F32),
            *[pltpu.VMEM(array.shape, array.dtype) for array in arguments],
            pltpu.SemaphoreType.DMA((7,)),
            pltpu.VMEM((CHUNKS, 8, WIDTH), F32),
            pltpu.VMEM((CHUNKS, 1, WIDTH), F32),
            pltpu.VMEM((CHUNKS - 1, 8, WIDTH), F32),
            pltpu.VMEM((CHUNKS - 1, 1, WIDTH), F32),
            pltpu.VMEM((4, 9, 1, WIDTH), F32),
            pltpu.VMEM((9, 1, WIDTH), F32),
            pltpu.SemaphoreType.DMA((4,)),
            pltpu.SemaphoreType.DMA((4,)),
        ],
        compiler_params=pltpu.CompilerParams(
            collective_id=0, has_side_effects=True, vmem_limit_bytes=44 * 2**20
        ),
    )(*arguments)


def finish_kernel(
    out_ref, whole, factors_ref, out_hbm, filters_ref, grad_levels_ref, mix_ref, embed_ref, sem
):
    store = pltpu.make_async_copy(out_ref, out_hbm, sem)
    store.start()
    for chunk in range(CHUNKS):
        for row in range(8):
            mix_ref[8 * chunk + row : 8 * chunk + row + 1, :] = whole[9 * chunk + row]
    summed = [whole[9 * chunk + 8] for chunk in range(CHUNKS)]
    for name in range(VOCAB):
        embed_ref[name : name + 1, :] = summed[16 + name]
    shifted = summed[1:14]
    factors = rows_of(factors_ref)
    low, high, levels, folded = factors[0:2], factors[2:4], factors[4:18], factors[18:32]
    current = summed[0]
    low_zero, low_one = summed[14] / low[0], summed[15] / low[1]
    high_zero = high_one = jnp.zeros_like(current)
    for level in range(LEVELS):
        late = shifted[level]
        grad_levels_ref[level : level + 1, :] = high[0] * current + high[1] * late
        low_zero = low_zero + folded[level + 1] * current
        low_one = low_one + folded[level + 1] * late
        high_zero = high_zero + levels[level] * current
        high_one = high_one + levels[level] * late
        current = low[0] * current + low[1] * late
    grad_levels_ref[LEVELS : LEVELS + 1, :] = current
    filters_ref[0, 0:1, :] = low_zero
    filters_ref[0, 1:2, :] = low_one
    filters_ref[1, 0:1, :] = high_zero
    filters_ref[1, 1:2, :] = high_one
    store.wait()


def finish(out, whole, factors):
    vmem = pl.BlockSpec(memory_space=pltpu.VMEM)
    return pl.pallas_call(
        finish_kernel,
        out_shape=(
            jax.ShapeDtypeStruct((TOKENS, WIDTH), F32),
            jax.ShapeDtypeStruct((2, 2, WIDTH), F32),
            jax.ShapeDtypeStruct((LEVELS + 1, WIDTH), F32),
            jax.ShapeDtypeStruct((WIDTH, WIDTH), F32),
            jax.ShapeDtypeStruct((VOCAB, WIDTH), F32),
        ),
        in_specs=[vmem] * 3,
        out_specs=(pl.BlockSpec(memory_space=pl.ANY),) + (vmem,) * 4,
        scratch_shapes=[pltpu.SemaphoreType.DMA],
        compiler_params=pltpu.CompilerParams(vmem_limit_bytes=16 * 2**20),
    )(out, whole, factors)


def per_device(ids, embed, low_filter, high_filter, level_weights, mix, cotangent):
    count = lax.axis_size("seq")
    scale = 1.0 / math.sqrt(count * lax.axis_size("batch") * TOKENS)
    out, whole, factors = layer(
        count, scale, ids.reshape(8, LANES), embed, low_filter, high_filter, level_weights, mix, cotangent[0]
    )
    out, grad_filters, grad_levels, grad_mix, grad_embed = finish(out, whole, factors)
    return out[None], grad_filters, grad_levels, grad_mix, grad_embed


def solution(mesh):
    placed = (P("batch", "seq"), P(), P(), P(), P(), P(), P("batch", "seq", None))
    return jax.shard_map(
        per_device,
        mesh=mesh,
        in_specs=placed,
        out_specs=(P("batch", "seq", None), P(), P(), P(), P()),
        check_vma=False,
    )
```

```python
import functools
import math

import jax
import jax.numpy as jnp
from jax import lax
from jax.experimental import pallas as pl
from jax.experimental.pallas import tpu as pltpu
from jax.sharding import PartitionSpec as P

MESH = pl.DeviceIdType.MESH
F32, BF16 = jnp.float32, jnp.bfloat16
LEVELS = 13
VOCAB = 16
WIDTH = 256
LANES = 128
TOKENS = 1024
BACK = 8
TILES = (BACK + 1) * TOKENS // LANES
CLASSES = 93
ROWS = 96 * VOCAB
NEAR = 56 * VOCAB
LAST = 80 * VOCAB
CHUNKS = 32


def class_of(level, ones):
    return 1 + level * (level + 1) // 2 + ones + level // 12


def block_of(level, ones):
    return slice(class_of(level, ones) * VOCAB, (class_of(level, ones) + 1) * VOCAB)


def dot(a, b):
    return jnp.dot(a, b, preferred_element_type=F32)


def halves(value):
    high = value.astype(BF16)
    return high, (value - high.astype(F32)).astype(BF16)


def level_factors(low, high, weights):
    folded = [None] * (LEVELS + 1)
    kappa = [None] * LEVELS
    folded[LEVELS] = weights[LEVELS]
    for level in range(LEVELS - 1, -1, -1):
        kappa[level] = weights[level] * high[1] + low[1] * folded[level + 1]
        folded[level] = weights[level] * high[0] + low[0] * folded[level + 1]
    return folded, kappa


def rows_of(ref):
    return [ref[row : row + 1, :] for row in range(ref.shape[0])]


def lag_weights(low):
    chains = []
    for row in low:
        chain = [jnp.ones_like(row)]
        for _ in range(LEVELS - 1):
            chain.append(chain[-1] * row)
        chains.append(chain)
    return lambda level, ones: chains[0][level - ones] * chains[1][ones]


def clear_padding(ref):
    for rows in (slice(LAST - VOCAB, LAST), slice(CLASSES * VOCAB, ROWS)):
        ref[rows, :] = jnp.zeros((rows.stop - rows.start, ref.shape[1]), BF16)


def make_weights(passed, folded, kappa, embed, weights_ref):
    def put(rows, factor):
        high, rest = halves(factor * embed)
        weights_ref[rows, 0:WIDTH] = high
        weights_ref[rows, WIDTH:] = rest

    put(slice(0, VOCAB), folded[0])
    for level in range(LEVELS):
        for ones in range(level + 1):
            put(block_of(level, ones), kappa[level] * passed(level, ones))
    clear_padding(weights_ref)


def where_is(table, value):
    return jnp.where(table == value, 1.0, 0.0).astype(BF16)


def make_tables(ones_ref, class_ref):
    place = lax.broadcasted_iota(jnp.int32, (2 * LANES, LANES), 0)
    lag = lax.broadcasted_iota(jnp.int32, (2 * LANES, LANES), 1) - place
    lag = jnp.where(place >= LANES, lag + 2 * LANES, lag)
    inside = (lag >= 0) & (lag < LANES)
    ones = jnp.zeros_like(lag)
    offset = jnp.zeros_like(lag)
    for bit in range(7):
        ones = ones + ((lag >> bit) & 1)
        offset = offset + jnp.where(lag >= 2**bit, bit, 0)
    klass = jnp.where(inside, jnp.where(lag == 0, 0, offset + ones), -1)
    ones = jnp.where(inside, ones, -1)
    for value in range(8):
        ones_ref[:, value * LANES : (value + 1) * LANES] = where_is(ones, value)
    for value in range(29):
        class_ref[:, value * LANES : (value + 1) * LANES] = where_is(klass, value)


def make_hot(tokens_ref, first, ids):
    names = lax.broadcasted_iota(jnp.int32, (VOCAB, LANES), 0)
    for row in range(8):
        tile = first + row
        hot = where_is(names, jnp.broadcast_to(ids[row : row + 1, :], (VOCAB, LANES)))
        tokens_ref[tile * VOCAB : (tile + 1) * VOCAB, 0:LANES] = hot
        if tile + 1 < TILES:
            tokens_ref[(tile + 1) * VOCAB : (tile + 2) * VOCAB, LANES:] = hot


def put_counts(result, s7, first, last, pair):
    for tile in range(first, last):
        for half in range(2):
            value = 2 * pair + half
            s7[value * VOCAB : (value + 1) * VOCAB, tile * LANES : (tile + 1) * LANES] = result[
                (tile - first) * VOCAB : (tile - first + 1) * VOCAB, half * LANES : (half + 1) * LANES
            ]


def count_tiles(tokens_ref, ones_ref, s7, first, last):
    for pair in range(4):
        table = ones_ref[:, 2 * pair * LANES : 2 * (pair + 1) * LANES]
        result = dot(tokens_ref[first * VOCAB : last * VOCAB, :], table).astype(BF16)
        put_counts(result, s7, first, last, pair)


def widened(source, level, ones, first, last):
    begin, end, span = first * LANES, last * LANES, 2**level
    total = None
    if 0 <= ones <= level:
        total = source[ones * VOCAB : (ones + 1) * VOCAB, begin:end]
    if 1 <= ones <= level + 1:
        late = source[(ones - 1) * VOCAB : ones * VOCAB, begin - span : end - span]
        total = late if total is None else total + late
    return total


def widen(source, target, level, first, last):
    for ones in range(level + 2):
        target[ones * VOCAB : (ones + 1) * VOCAB, first * LANES : last * LANES] = widened(
            source, level, ones, first, last
        )


def place_level(source, level, features_ref):
    rows = slice(class_of(level, 0) * VOCAB, class_of(level + 1, 0) * VOCAB)
    begin = BACK * TOKENS - 2**level
    features_ref[rows, :] = source[:, begin : begin + TOKENS]


def make_near(tokens_ref, class_ref, ones_ref, s7, s8, s9, features_ref):
    own = tokens_ref[64 * VOCAB : 72 * VOCAB, :]
    for first in range(0, 29, 2):
        members = range(first, min(first + 2, 29))
        result = dot(own, class_ref[:, first * LANES : (first + len(members)) * LANES]).astype(BF16)
        for tile in range(8):
            for half, member in enumerate(members):
                features_ref[member * VOCAB : (member + 1) * VOCAB, tile * LANES : (tile + 1) * LANES] = result[
                    tile * VOCAB : (tile + 1) * VOCAB, half * LANES : (half + 1) * LANES
                ]
    count_tiles(tokens_ref, ones_ref, s7, 57, 71)
    widen(s7, s8, 7, 58, 70)
    widen(s8, s9, 8, 60, 68)
    place_level(s7, 7, features_ref)
    place_level(s8, 8, features_ref)
    place_level(s9, 9, features_ref)


def make_middle(tokens_ref, ones_ref, s7, s8, s9, s10, features_ref):
    count_tiles(tokens_ref, ones_ref, s7, 33, 57)
    widen(s7, s8, 7, 34, 58)
    widen(s8, s9, 8, 36, 60)
    widen(s9, s10, 9, 40, 64)
    place_level(s10, 10, features_ref)
    for ones in range(12):
        features_ref[block_of(11, ones), :] = widened(s10, 10, ones, 48, 56)


def make_last(tokens_ref, ones_ref, s7, s8, s9, s10, features_ref):
    count_tiles(tokens_ref, ones_ref, s7, 1, 33)
    widen(s7, s8, 7, 2, 34)
    widen(s8, s9, 8, 4, 36)
    widen(s9, s10, 9, 8, 40)
    for ones in range(13):
        near, late = widened(s10, 10, ones, 32, 40), widened(s10, 10, ones - 1, 16, 24)
        features_ref[block_of(12, ones), :] = late if near is None else near if late is None else near + late


def gelu_parts(y):
    root = math.sqrt(2.0 / math.pi)
    square = y * y
    bend = jnp.tanh(root * (y + 0.044715 * square * y))
    half = 0.5 * (1.0 + bend)
    slope = half + 0.5 * y * (1.0 - bend * bend) * (root * (1.0 + 3 * 0.044715 * square))
    return y * half, slope


def add_part(turned_ref, features_ref, y_ref, first, last):
    for start in range(0, TOKENS, 256):
        span = slice(start, start + 256)
        both = dot(turned_ref[:, first:last], features_ref[first:last, span])
        part = both[:WIDTH] + both[WIDTH:]
        y_ref[:, span] = part if first == 0 else y_ref[:, span] + part


def before_gelu(mix_ref, cot_ref, g_hidden_ref):
    g_hidden_ref[...] = lax.dot_general(
        cot_ref[...], mix_ref[...], (((1,), (1,)), ((), ())), preferred_element_type=F32
    )


def forward(turned_ref, features_ref, y_ref, g_hidden_ref, cot_ref, hidden_ref, g_ref):
    mix_sum = None
    block = 256
    for start in range(0, TOKENS, block):
        span = slice(start, start + block)
        both = dot(turned_ref[:, LAST:], features_ref[LAST:, span])
        y = (y_ref[:, span] + both[:WIDTH] + both[WIDTH:]).T
        active, slope = gelu_parts(y)
        hidden = active.astype(BF16)
        hidden_ref[span, :] = hidden
        g_high, g_rest = halves(g_hidden_ref[span, :] * slope)
        g_ref[span, 0:WIDTH] = g_high
        g_ref[span, WIDTH:] = g_rest
        term = lax.dot_general(hidden, cot_ref[span, :], (((0,), (0,)), ((), ())), preferred_element_type=F32)
        mix_sum = term if mix_sum is None else mix_sum + term
    return mix_sum


def outputs(embed, features_ref, hidden_ref, mix_ref, out_ref):
    high, middle = halves(embed)
    rest = (embed - high.astype(F32) - middle.astype(F32)).astype(BF16)
    table = jnp.concatenate([high, middle, rest], axis=0)
    for start in range(0, TOKENS, 256):
        span = slice(start, start + 256)
        hot = features_ref[0:VOCAB, span]
        hot = jnp.concatenate([hot, hot, hot], axis=0)
        x = lax.dot_general(hot, table, (((0,), (0,)), ((), ())), preferred_element_type=F32)
        out_ref[span, :] = x + dot(hidden_ref[span, :], mix_ref[...])


def backward(passed, folded, kappa, embed, features_ref, g_ref, cot_ref, z_ref):
    def over_names(value):
        return jnp.sum(embed * value, axis=0, keepdims=True)

    def products(first, last):
        both = dot(features_ref[first:last, :], g_ref[...])
        z_ref[first:last, :] = both[:, :WIDTH] + both[:, WIDTH:]

    ends = {0: class_of(8, 0) * VOCAB, 8: class_of(11, 0) * VOCAB, 11: CLASSES * VOCAB}
    begin = 0
    rows = []
    for level in range(LEVELS):
        if level in ends:
            products(begin, ends[level])
            begin = ends[level]
        if level == 0:
            z0 = z_ref[0:VOCAB, :]
            rows.append(over_names(z0))
            embed_sum = folded[0] * z0 + dot(features_ref[0:VOCAB, :], cot_ref[...])
            zero_sum = one_sum = jnp.zeros_like(z0)
        total = passed(level, 0) * z_ref[block_of(level, 0), :]
        counted = jnp.zeros_like(total)
        for ones in range(1, level + 1):
            term = passed(level, ones) * z_ref[block_of(level, ones), :]
            total = total + term
            counted = counted + float(ones) * term
        rows.append(over_names(total))
        embed_sum = embed_sum + kappa[level] * total
        one_sum = one_sum + kappa[level] * counted
        zero_sum = zero_sum + kappa[level] * (float(level) * total - counted)
    rows += [over_names(zero_sum), over_names(one_sum)]
    return jnp.concatenate(rows + [embed_sum], axis=0)


def layer_kernel(
    count, scale, ids_hbm, embed_hbm, low_hbm, high_hbm, levels_hbm, mix_hbm, cot_hbm,
    out_ref, whole, factors_ref,
    held, ids_sems, ones_ref, class_ref, tokens_ref, s7, s8, s9, s10, features_ref, weights_ref, turned_ref,
    y_ref, g_hidden_ref, hidden_ref, g_ref, z_ref, ids_ref, embed_ref, low_ref, high_ref, levels_ref, mix_ref, cot_ref, local_sem,
    mix_part, small_part, mix_in, small_in, second, third, sends, recvs,
):
    seq, batch = lax.axis_index("seq"), lax.axis_index("batch")
    x, y = lax.rem(seq, 4), lax.rem(lax.div(seq, 4), 4)
    core = lax.rem(batch, 2)
    z = lax.div(seq, 16) * 2 + lax.div(batch, 2)

    def along(order):
        return x + order * (y - x), y + order * (z - y), z + order * (x - z)

    def device(order, spots, core):
        a, b, c = spots
        x, y, z = a + order * (c - a), b + order * (a - b), c + order * (b - c)
        return lax.div(z, 2) * 16 + y * 4 + x, lax.rem(z, 2) * 2 + core

    def moved(spots, i, j, k):
        return lax.rem(spots[0] + i, 4), lax.rem(spots[1] + j, 4), lax.rem(spots[2] + k, 4)

    mine, theirs = along(core), along(1 - core)
    hops = lambda spot: sum(min(step, 4 - step) for step in spot)
    plane = sorted([(i, j) for i in range(4) for j in range(4)], key=hops, reverse=True)
    others = plane[:-1]
    own_peer = lambda i, j, k: device(core, moved(mine, i, j, k), core)
    their_peer = lambda i, j: device(1 - core, moved(theirs, i, j, 0), 1 - core)
    cross_peer = lambda i, j: device(core, moved(mine, i, j, 0), 1 - core)
    chunk_of = lambda core, spots: 16 * core + 4 * spots[0] + spots[1]

    barrier = pltpu.get_barrier_semaphore()

    def greet(peer):
        pl.semaphore_signal(barrier, inc=1, device_id=peer, device_id_type=MESH)

    for step in range(1, BACK + 1):
        greet((lax.rem(seq + count - step, count), batch))
    for i, j in others:
        greet(own_peer(i, j, 0))
    for k in range(1, 4):
        greet(own_peer(0, 0, k))
    for i, j in plane:
        greet(their_peer(i, j))
        if i:
            greet(cross_peer(i + core * (j - i), j + core * (i - j)))
    loads = [
        pltpu.make_async_copy(source, target, local_sem.at[place])
        for place, (source, target) in enumerate(
            [
                (ids_hbm, ids_ref),
                (embed_hbm, embed_ref),
                (low_hbm, low_ref),
                (high_hbm, high_ref),
                (levels_hbm, levels_ref),
                (mix_hbm, mix_ref),
                (cot_hbm, cot_ref),
            ]
        )
    ]
    for load in loads:
        load.start()
    pl.semaphore_wait(barrier, BACK + 46)

    def copy_to(source, target, sent, received, peer):
        copy = pltpu.make_async_remote_copy(
            src_ref=source, dst_ref=target, send_sem=sent, recv_sem=received, device_id=peer, device_id_type=MESH
        )
        copy.start()
        return copy

    def drain(ref, sem):
        pltpu.make_async_copy(ref, ref, sem).wait()

    arrivals = [(0, 1), (1, 4), (4, BACK)]
    for group, (first, last) in reversed(list(enumerate(arrivals))):
        for step in range(first, last):
            peer = lax.rem(seq + step + 1, count), batch
            copy_to(ids_hbm, held.at[step], ids_sems.at[3], ids_sems.at[group], peer)

    for load in loads:
        load.wait()
    embed = embed_ref[...]
    low, high, levels = rows_of(low_ref), rows_of(high_ref), rows_of(levels_ref)
    folded, kappa = level_factors(low, high, levels)
    passed = lag_weights(low)
    make_weights(passed, folded, kappa, embed, weights_ref)
    turned_ref[...] = weights_ref[...].T
    make_tables(ones_ref, class_ref)
    tokens_ref[0:VOCAB, LANES:] = jnp.zeros((VOCAB, LANES), BF16)
    clear_padding(features_ref)
    before_gelu(mix_ref, cot_ref, g_hidden_ref)
    make_hot(tokens_ref, 8 * BACK, ids_ref[...])

    factors_ref[0:2, :] = low_ref[...]
    factors_ref[2:4, :] = high_ref[...]
    factors_ref[4:18, :] = levels_ref[...]
    for level in range(LEVELS + 1):
        factors_ref[18 + level : 19 + level, :] = folded[level]

    def receive(group):
        first, last = arrivals[group]
        drain(held.at[pl.ds(first, last - first)], ids_sems.at[group])
        for step in range(first, last):
            make_hot(tokens_ref, 8 * (BACK - 1 - step), jnp.where(seq > step, held[step], -1))

    receive(0)
    make_near(tokens_ref, class_ref, ones_ref, s7, s8, s9, features_ref)
    add_part(turned_ref, features_ref, y_ref, 0, NEAR)
    receive(1)
    make_middle(tokens_ref, ones_ref, s7, s8, s9, s10, features_ref)
    add_part(turned_ref, features_ref, y_ref, NEAR, LAST)
    receive(2)
    make_last(tokens_ref, ones_ref, s7, s8, s9, s10, features_ref)
    mix_sum = forward(turned_ref, features_ref, y_ref, g_hidden_ref, cot_ref, hidden_ref, g_ref)

    home = chunk_of(core, mine)

    def spread(phase, part, target):
        for slot, (i, j) in enumerate(plane):
            place = chunk_of(1 - core, moved(theirs, i, j, 0))
            copy_to(part.at[place], target.at[slot + 15], sends.at[phase], recvs.at[phase], their_peer(i, j))
            if (i, j) in others:
                place = chunk_of(core, moved(mine, i, j, 0))
                copy_to(part.at[place], target.at[slot], sends.at[phase], recvs.at[phase], own_peer(i, j, 0))

    for chunk in range(CHUNKS):
        mix_part[chunk] = scale * mix_sum[8 * chunk : 8 * chunk + 8]
    spread(0, mix_part, mix_in)
    small = scale * backward(passed, folded, kappa, embed, features_ref, g_ref, cot_ref, z_ref)
    for chunk in range(CHUNKS):
        small_part[chunk] = small[chunk : chunk + 1]
    spread(1, small_part, small_in)
    drain(mix_in, recvs.at[0])
    mixed = mix_part[home]
    for slot in range(CHUNKS - 1):
        mixed = mixed + mix_in[slot]
    for row in range(8):
        second[mine[2], row] = mixed[row : row + 1]
    drain(small_in, recvs.at[1])
    row = small_part[home]
    for slot in range(CHUNKS - 1):
        row = row + small_in[slot]
    second[mine[2], 8] = row
    spot = second.at[mine[2]]
    for k in (2, 1, 3):
        copy_to(spot, spot, sends.at[2], recvs.at[2], own_peer(0, 0, k))
    outputs(embed, features_ref, hidden_ref, mix_ref, out_ref)
    drain(second.at[pl.ds(0, 3)], recvs.at[2])
    third[...] = (second[0] + second[1]) + (second[2] + second[3])
    landing = whole.at[pl.ds(9 * home, 9)]
    for i, j in plane:
        copy_to(third, landing, sends.at[3], recvs.at[3], cross_peer(i, j))
        if (i, j) in others:
            copy_to(third, landing, sends.at[3], recvs.at[3], own_peer(i, j, 0))
    whole[pl.ds(9 * home, 9)] = third[...]
    drain(held, ids_sems.at[3])
    drain(mix_in, sends.at[0])
    drain(small_in, sends.at[1])
    drain(second.at[pl.ds(0, 3)], sends.at[2])
    gathered = whole.at[pl.ds(0, 9 * (CHUNKS - 1))]
    drain(gathered, recvs.at[3])
    drain(gathered, sends.at[3])


def layer(count, scale, ids, embed, low, high, levels, mix, cot):
    vmem = pl.BlockSpec(memory_space=pltpu.VMEM)
    far = pl.BlockSpec(memory_space=pltpu.HBM)
    arguments = tuple(
        pltpu.with_memory_space_constraint(array, pltpu.HBM) for array in (ids, embed, low, high, levels, mix, cot)
    )
    return pl.pallas_call(
        functools.partial(layer_kernel, count, scale),
        out_shape=(
            jax.ShapeDtypeStruct((TOKENS, WIDTH), F32),
            jax.ShapeDtypeStruct((9 * CHUNKS, 1, WIDTH), F32),
            jax.ShapeDtypeStruct((32, WIDTH), F32),
        ),
        in_specs=[far] * 7,
        out_specs=(vmem,) * 3,
        scratch_shapes=[
            pltpu.VMEM((BACK, 8, LANES), jnp.int32),
            pltpu.SemaphoreType.DMA((4,)),
            pltpu.VMEM((2 * LANES, 8 * LANES), BF16),
            pltpu.VMEM((2 * LANES, 29 * LANES), BF16),
            pltpu.VMEM((TILES * VOCAB, 2 * LANES), BF16),
            pltpu.VMEM((8 * VOCAB, TILES * LANES), BF16),
            pltpu.VMEM((9 * VOCAB, TILES * LANES), BF16),
            pltpu.VMEM((10 * VOCAB, TILES * LANES), BF16),
            pltpu.VMEM((11 * VOCAB, TILES * LANES), BF16),
            pltpu.VMEM((ROWS, TOKENS), BF16),
            pltpu.VMEM((ROWS, 2 * WIDTH), BF16),
            pltpu.VMEM((2 * WIDTH, ROWS), BF16),
            pltpu.VMEM((WIDTH, TOKENS), F32),
            pltpu.VMEM((TOKENS, WIDTH), F32),
            pltpu.VMEM((TOKENS, WIDTH), BF16),
            pltpu.VMEM((TOKENS, 2 * WIDTH), BF16),
            pltpu.VMEM((CLASSES * VOCAB, WIDTH), F32),
            *[pltpu.VMEM(array.shape, array.dtype) for array in arguments],
            pltpu.SemaphoreType.DMA((7,)),
            pltpu.VMEM((CHUNKS, 8, WIDTH), F32),
            pltpu.VMEM((CHUNKS, 1, WIDTH), F32),
            pltpu.VMEM((CHUNKS - 1, 8, WIDTH), F32),
            pltpu.VMEM((CHUNKS - 1, 1, WIDTH), F32),
            pltpu.VMEM((4, 9, 1, WIDTH), F32),
            pltpu.VMEM((9, 1, WIDTH), F32),
            pltpu.SemaphoreType.DMA((4,)),
            pltpu.SemaphoreType.DMA((4,)),
        ],
        compiler_params=pltpu.CompilerParams(
            collective_id=0, has_side_effects=True, vmem_limit_bytes=44 * 2**20
        ),
    )(*arguments)


def finish_kernel(
    out_ref, whole, factors_ref,
    out_hbm, filters_hbm, levels_hbm, mix_hbm, embed_hbm,
    filters_ref, grad_levels_ref, mix_ref, embed_ref, sems,
):
    stores = []

    def store(source, target):
        copy = pltpu.make_async_copy(source, target, sems.at[len(stores)])
        copy.start()
        stores.append(copy)

    store(out_ref, out_hbm)
    for chunk in range(CHUNKS):
        for row in range(8):
            mix_ref[8 * chunk + row : 8 * chunk + row + 1, :] = whole[9 * chunk + row]
    store(mix_ref, mix_hbm)
    summed = [whole[9 * chunk + 8] for chunk in range(CHUNKS)]
    for name in range(VOCAB):
        embed_ref[name : name + 1, :] = summed[16 + name]
    store(embed_ref, embed_hbm)
    shifted = summed[1:14]
    factors = rows_of(factors_ref)
    low, high, levels, folded = factors[0:2], factors[2:4], factors[4:18], factors[18:32]
    current = summed[0]
    low_zero, low_one = summed[14] / low[0], summed[15] / low[1]
    high_zero = high_one = jnp.zeros_like(current)
    for level in range(LEVELS):
        late = shifted[level]
        grad_levels_ref[level : level + 1, :] = high[0] * current + high[1] * late
        low_zero = low_zero + folded[level + 1] * current
        low_one = low_one + folded[level + 1] * late
        high_zero = high_zero + levels[level] * current
        high_one = high_one + levels[level] * late
        current = low[0] * current + low[1] * late
    grad_levels_ref[LEVELS : LEVELS + 1, :] = current
    filters_ref[0, 0:1, :] = low_zero
    filters_ref[0, 1:2, :] = low_one
    filters_ref[1, 0:1, :] = high_zero
    filters_ref[1, 1:2, :] = high_one
    store(filters_ref, filters_hbm)
    store(grad_levels_ref, levels_hbm)
    for copy in stores:
        copy.wait()


def finish(out, whole, factors):
    shapes = [(TOKENS, WIDTH), (2, 2, WIDTH), (LEVELS + 1, WIDTH), (WIDTH, WIDTH), (VOCAB, WIDTH)]
    return pl.pallas_call(
        finish_kernel,
        out_shape=tuple(jax.ShapeDtypeStruct(shape, F32) for shape in shapes),
        in_specs=[pl.BlockSpec(memory_space=pltpu.VMEM)] * 3,
        out_specs=(pl.BlockSpec(memory_space=pl.ANY),) * 5,
        scratch_shapes=[pltpu.VMEM(shape, F32) for shape in shapes[1:]] + [pltpu.SemaphoreType.DMA((5,))],
        compiler_params=pltpu.CompilerParams(vmem_limit_bytes=16 * 2**20),
    )(out, whole, factors)


def per_device(ids, embed, low_filter, high_filter, level_weights, mix, cotangent):
    count = lax.axis_size("seq")
    scale = 1.0 / math.sqrt(count * lax.axis_size("batch") * TOKENS)
    out, whole, factors = layer(
        count, scale, ids.reshape(8, LANES), embed, low_filter, high_filter, level_weights, mix, cotangent[0]
    )
    out, grad_filters, grad_levels, grad_mix, grad_embed = finish(out, whole, factors)
    return out[None], grad_filters, grad_levels, grad_mix, grad_embed


def solution(mesh):
    placed = (P("batch", "seq"), P(), P(), P(), P(), P(), P("batch", "seq", None))
    return jax.shard_map(
        per_device,
        mesh=mesh,
        in_specs=placed,
        out_specs=(P("batch", "seq", None), P(), P(), P(), P()),
        check_vma=False,
    )
```

```python
import functools
import math

import jax
import jax.numpy as jnp
from jax import lax
from jax.experimental import pallas as pl
from jax.experimental.pallas import tpu as pltpu
from jax.sharding import PartitionSpec as P

MESH = pl.DeviceIdType.MESH
F32, BF16 = jnp.float32, jnp.bfloat16
LEVELS = 13
VOCAB = 16
WIDTH = 256
LANES = 128
TOKENS = 1024
BACK = 8
TILES = (BACK + 1) * TOKENS // LANES
CLASSES = 93
ROWS = 96 * VOCAB
NEAR = 56 * VOCAB
LAST = 80 * VOCAB
OWNERS = 16
SHARE = WIDTH // OWNERS
PART = SHARE + 2


def class_of(level, ones):
    return 1 + level * (level + 1) // 2 + ones + level // 12


def block_of(level, ones):
    return slice(class_of(level, ones) * VOCAB, (class_of(level, ones) + 1) * VOCAB)


def dot(a, b):
    return jnp.dot(a, b, preferred_element_type=F32)


def halves(value):
    high = value.astype(BF16)
    return high, (value - high.astype(F32)).astype(BF16)


def level_factors(low, high, weights):
    folded = [None] * (LEVELS + 1)
    kappa = [None] * LEVELS
    folded[LEVELS] = weights[LEVELS]
    for level in range(LEVELS - 1, -1, -1):
        kappa[level] = weights[level] * high[1] + low[1] * folded[level + 1]
        folded[level] = weights[level] * high[0] + low[0] * folded[level + 1]
    return folded, kappa


def rows_of(ref):
    return [ref[row : row + 1, :] for row in range(ref.shape[0])]


def lag_weights(low):
    chains = []
    for row in low:
        chain = [jnp.ones_like(row)]
        for _ in range(LEVELS - 1):
            chain.append(chain[-1] * row)
        chains.append(chain)
    return lambda level, ones: chains[0][level - ones] * chains[1][ones]


def clear_padding(ref):
    for rows in (slice(LAST - VOCAB, LAST), slice(CLASSES * VOCAB, ROWS)):
        ref[rows, :] = jnp.zeros((rows.stop - rows.start, ref.shape[1]), BF16)


def make_weights(passed, folded, kappa, embed, weights_ref):
    def put(rows, factor):
        high, rest = halves(factor * embed)
        weights_ref[rows, 0:WIDTH] = high
        weights_ref[rows, WIDTH:] = rest

    put(slice(0, VOCAB), folded[0])
    for level in range(LEVELS):
        for ones in range(level + 1):
            put(block_of(level, ones), kappa[level] * passed(level, ones))
    clear_padding(weights_ref)


def where_is(table, value):
    return jnp.where(table == value, 1.0, 0.0).astype(BF16)


def make_tables(ones_ref, class_ref):
    place = lax.broadcasted_iota(jnp.int32, (2 * LANES, LANES), 0)
    lag = lax.broadcasted_iota(jnp.int32, (2 * LANES, LANES), 1) - place
    lag = jnp.where(place >= LANES, lag + 2 * LANES, lag)
    inside = (lag >= 0) & (lag < LANES)
    ones = jnp.zeros_like(lag)
    offset = jnp.zeros_like(lag)
    for bit in range(7):
        ones = ones + ((lag >> bit) & 1)
        offset = offset + jnp.where(lag >= 2**bit, bit, 0)
    klass = jnp.where(inside, jnp.where(lag == 0, 0, offset + ones), -1)
    ones = jnp.where(inside, ones, -1)
    for value in range(8):
        ones_ref[:, value * LANES : (value + 1) * LANES] = where_is(ones, value)
    for value in range(29):
        class_ref[:, value * LANES : (value + 1) * LANES] = where_is(klass, value)


def make_hot(tokens_ref, first, ids):
    names = lax.broadcasted_iota(jnp.int32, (VOCAB, LANES), 0)
    for row in range(8):
        tile = first + row
        hot = where_is(names, jnp.broadcast_to(ids[row : row + 1, :], (VOCAB, LANES)))
        tokens_ref[tile * VOCAB : (tile + 1) * VOCAB, 0:LANES] = hot
        if tile + 1 < TILES:
            tokens_ref[(tile + 1) * VOCAB : (tile + 2) * VOCAB, LANES:] = hot


def put_counts(result, s7, first, last, pair):
    for tile in range(first, last):
        for half in range(2):
            value = 2 * pair + half
            s7[value * VOCAB : (value + 1) * VOCAB, tile * LANES : (tile + 1) * LANES] = result[
                (tile - first) * VOCAB : (tile - first + 1) * VOCAB, half * LANES : (half + 1) * LANES
            ]


def count_tiles(tokens_ref, ones_ref, s7, first, last):
    for pair in range(4):
        table = ones_ref[:, 2 * pair * LANES : 2 * (pair + 1) * LANES]
        result = dot(tokens_ref[first * VOCAB : last * VOCAB, :], table).astype(BF16)
        put_counts(result, s7, first, last, pair)


def widened(source, level, ones, first, last):
    begin, end, span = first * LANES, last * LANES, 2**level
    total = None
    if 0 <= ones <= level:
        total = source[ones * VOCAB : (ones + 1) * VOCAB, begin:end]
    if 1 <= ones <= level + 1:
        late = source[(ones - 1) * VOCAB : ones * VOCAB, begin - span : end - span]
        total = late if total is None else total + late
    return total


def widen(source, target, level, first, last):
    for ones in range(level + 2):
        target[ones * VOCAB : (ones + 1) * VOCAB, first * LANES : last * LANES] = widened(
            source, level, ones, first, last
        )


def place_level(source, level, features_ref):
    rows = slice(class_of(level, 0) * VOCAB, class_of(level + 1, 0) * VOCAB)
    begin = BACK * TOKENS - 2**level
    features_ref[rows, :] = source[:, begin : begin + TOKENS]


def make_near(tokens_ref, class_ref, ones_ref, s7, s8, s9, features_ref):
    own = tokens_ref[64 * VOCAB : 72 * VOCAB, :]
    for first in range(0, 29, 2):
        members = range(first, min(first + 2, 29))
        result = dot(own, class_ref[:, first * LANES : (first + len(members)) * LANES]).astype(BF16)
        for tile in range(8):
            for half, member in enumerate(members):
                features_ref[member * VOCAB : (member + 1) * VOCAB, tile * LANES : (tile + 1) * LANES] = result[
                    tile * VOCAB : (tile + 1) * VOCAB, half * LANES : (half + 1) * LANES
                ]
    count_tiles(tokens_ref, ones_ref, s7, 57, 71)
    widen(s7, s8, 7, 58, 70)
    widen(s8, s9, 8, 60, 68)
    place_level(s7, 7, features_ref)
    place_level(s8, 8, features_ref)
    place_level(s9, 9, features_ref)


def make_middle(tokens_ref, ones_ref, s7, s8, s9, s10, features_ref):
    count_tiles(tokens_ref, ones_ref, s7, 33, 57)
    widen(s7, s8, 7, 34, 58)
    widen(s8, s9, 8, 36, 60)
    widen(s9, s10, 9, 40, 64)
    place_level(s10, 10, features_ref)
    for ones in range(12):
        features_ref[block_of(11, ones), :] = widened(s10, 10, ones, 48, 56)


def make_last(tokens_ref, ones_ref, s7, s8, s9, s10, features_ref):
    count_tiles(tokens_ref, ones_ref, s7, 1, 33)
    widen(s7, s8, 7, 2, 34)
    widen(s8, s9, 8, 4, 36)
    widen(s9, s10, 9, 8, 40)
    for ones in range(13):
        near, late = widened(s10, 10, ones, 32, 40), widened(s10, 10, ones - 1, 16, 24)
        features_ref[block_of(12, ones), :] = late if near is None else near if late is None else near + late


def gelu_parts(y):
    root = math.sqrt(2.0 / math.pi)
    square = y * y
    bend = jnp.tanh(root * (y + 0.044715 * square * y))
    half = 0.5 * (1.0 + bend)
    slope = half + 0.5 * y * (1.0 - bend * bend) * (root * (1.0 + 3 * 0.044715 * square))
    return y * half, slope


def add_part(turned_ref, features_ref, y_ref, first, last):
    for start in range(0, TOKENS, 256):
        span = slice(start, start + 256)
        both = dot(turned_ref[:, first:last], features_ref[first:last, span])
        part = both[:WIDTH] + both[WIDTH:]
        y_ref[:, span] = part if first == 0 else y_ref[:, span] + part


def before_gelu(mix_ref, cot_ref, g_hidden_ref):
    g_hidden_ref[...] = lax.dot_general(
        cot_ref[...], mix_ref[...], (((1,), (1,)), ((), ())), preferred_element_type=F32
    )


def forward(turned_ref, features_ref, y_ref, g_hidden_ref, cot_ref, hidden_ref, g_ref):
    mix_sum = None
    block = 256
    for start in range(0, TOKENS, block):
        span = slice(start, start + block)
        both = dot(turned_ref[:, LAST:], features_ref[LAST:, span])
        y = (y_ref[:, span] + both[:WIDTH] + both[WIDTH:]).T
        active, slope = gelu_parts(y)
        hidden = active.astype(BF16)
        hidden_ref[span, :] = hidden
        g_high, g_rest = halves(g_hidden_ref[span, :] * slope)
        g_ref[span, 0:WIDTH] = g_high
        g_ref[span, WIDTH:] = g_rest
        term = lax.dot_general(hidden, cot_ref[span, :], (((0,), (0,)), ((), ())), preferred_element_type=F32)
        mix_sum = term if mix_sum is None else mix_sum + term
    return mix_sum


def outputs(embed, features_ref, hidden_ref, mix_ref, out_ref):
    high, middle = halves(embed)
    rest = (embed - high.astype(F32) - middle.astype(F32)).astype(BF16)
    table = jnp.concatenate([high, middle, rest], axis=0)
    for start in range(0, TOKENS, 256):
        span = slice(start, start + 256)
        hot = features_ref[0:VOCAB, span]
        hot = jnp.concatenate([hot, hot, hot], axis=0)
        x = lax.dot_general(hot, table, (((0,), (0,)), ((), ())), preferred_element_type=F32)
        out_ref[span, :] = x + dot(hidden_ref[span, :], mix_ref[...])


def backward(passed, folded, kappa, embed, features_ref, g_ref, cot_ref, z_ref):
    def over_names(value):
        return jnp.sum(embed * value, axis=0, keepdims=True)

    def products(first, last):
        both = dot(features_ref[first:last, :], g_ref[...])
        z_ref[first:last, :] = both[:, :WIDTH] + both[:, WIDTH:]

    ends = {0: class_of(8, 0) * VOCAB, 8: class_of(11, 0) * VOCAB, 11: CLASSES * VOCAB}
    begin = 0
    rows = []
    for level in range(LEVELS):
        if level in ends:
            products(begin, ends[level])
            begin = ends[level]
        if level == 0:
            z0 = z_ref[0:VOCAB, :]
            rows.append(over_names(z0))
            embed_sum = folded[0] * z0 + dot(features_ref[0:VOCAB, :], cot_ref[...])
            zero_sum = one_sum = jnp.zeros_like(z0)
        total = passed(level, 0) * z_ref[block_of(level, 0), :]
        counted = jnp.zeros_like(total)
        for ones in range(1, level + 1):
            term = passed(level, ones) * z_ref[block_of(level, ones), :]
            total = total + term
            counted = counted + float(ones) * term
        rows.append(over_names(total))
        embed_sum = embed_sum + kappa[level] * total
        one_sum = one_sum + kappa[level] * counted
        zero_sum = zero_sum + kappa[level] * (float(level) * total - counted)
    rows += [over_names(zero_sum), over_names(one_sum)]
    return jnp.concatenate(rows + [embed_sum], axis=0)


def layer_kernel(
    count, scale, ids_hbm, embed_hbm, low_hbm, high_hbm, levels_hbm, mix_hbm, cot_hbm,
    out_ref, whole, factors_ref,
    held, ids_sems, ones_ref, class_ref, tokens_ref, s7, s8, s9, s10, features_ref, weights_ref, turned_ref,
    y_ref, g_hidden_ref, hidden_ref, g_ref, z_ref, ids_ref, embed_ref, low_ref, high_ref, levels_ref, mix_ref, cot_ref, local_sem,
    mix_part, small_part, mix_in, small_in, second, third, sends, recvs,
):
    seq, batch = lax.axis_index("seq"), lax.axis_index("batch")
    x, y = lax.rem(seq, 4), lax.rem(lax.div(seq, 4), 4)
    core = lax.rem(batch, 2)
    z = lax.div(seq, 16) * 2 + lax.div(batch, 2)

    def chip(i, j, k, core):
        x_to, y_to, z_to = lax.rem(x + i, 4), lax.rem(y + j, 4), lax.rem(z + k, 4)
        return lax.div(z_to, 2) * 16 + y_to * 4 + x_to, lax.rem(z_to, 2) * 2 + core

    part_of = lambda i, j: 4 * lax.rem(x + i, 4) + lax.rem(y + j, 4)
    hops = lambda spot: sum(min(step, 4 - step) for step in spot)
    plane = sorted([(i, j) for i in range(4) for j in range(4)], key=hops, reverse=True)
    others = plane[:-1]
    barrier = pltpu.get_barrier_semaphore()

    def greet(peer):
        pl.semaphore_signal(barrier, inc=1, device_id=peer, device_id_type=MESH)

    for step in range(1, BACK + 1):
        greet((lax.rem(seq + count - step, count), batch))
    for i, j in others:
        greet(chip(i, j, 0, 1))

    @pl.when(core == 0)
    def _():
        greet(chip(0, 0, 0, 1))

    @pl.when(core == 1)
    def _():
        for i, j in plane:
            greet(chip(i, j, 0, 0))
        for k in range(1, 4):
            greet(chip(0, 0, k, 1))

    loads = [
        pltpu.make_async_copy(source, target, local_sem.at[place])
        for place, (source, target) in enumerate(
            [
                (ids_hbm, ids_ref),
                (embed_hbm, embed_ref),
                (low_hbm, low_ref),
                (high_hbm, high_ref),
                (levels_hbm, levels_ref),
                (mix_hbm, mix_ref),
                (cot_hbm, cot_ref),
            ]
        )
    ]
    for load in loads:
        load.start()
    pl.semaphore_wait(barrier, BACK + 16 + 18 * core)

    def copy_to(source, target, sent, received, peer):
        copy = pltpu.make_async_remote_copy(
            src_ref=source, dst_ref=target, send_sem=sent, recv_sem=received, device_id=peer, device_id_type=MESH
        )
        copy.start()
        return copy

    def drain(ref, sem):
        pltpu.make_async_copy(ref, ref, sem).wait()

    arrivals = [(0, 1), (1, 4), (4, BACK)]
    for group, (first, last) in reversed(list(enumerate(arrivals))):
        for step in range(first, last):
            peer = lax.rem(seq + step + 1, count), batch
            copy_to(ids_hbm, held.at[step], ids_sems.at[3], ids_sems.at[group], peer)

    for load in loads:
        load.wait()
    embed = embed_ref[...]
    low, high, levels = rows_of(low_ref), rows_of(high_ref), rows_of(levels_ref)
    folded, kappa = level_factors(low, high, levels)
    passed = lag_weights(low)
    make_weights(passed, folded, kappa, embed, weights_ref)
    turned_ref[...] = weights_ref[...].T
    make_tables(ones_ref, class_ref)
    tokens_ref[0:VOCAB, LANES:] = jnp.zeros((VOCAB, LANES), BF16)
    clear_padding(features_ref)
    before_gelu(mix_ref, cot_ref, g_hidden_ref)
    make_hot(tokens_ref, 8 * BACK, ids_ref[...])

    factors_ref[0:2, :] = low_ref[...]
    factors_ref[2:4, :] = high_ref[...]
    factors_ref[4:18, :] = levels_ref[...]
    for level in range(LEVELS + 1):
        factors_ref[18 + level : 19 + level, :] = folded[level]

    def receive(group):
        first, last = arrivals[group]
        drain(held.at[pl.ds(first, last - first)], ids_sems.at[group])
        for step in range(first, last):
            make_hot(tokens_ref, 8 * (BACK - 1 - step), jnp.where(seq > step, held[step], -1))

    receive(0)
    make_near(tokens_ref, class_ref, ones_ref, s7, s8, s9, features_ref)
    add_part(turned_ref, features_ref, y_ref, 0, NEAR)
    receive(1)
    make_middle(tokens_ref, ones_ref, s7, s8, s9, s10, features_ref)
    add_part(turned_ref, features_ref, y_ref, NEAR, LAST)
    receive(2)
    make_last(tokens_ref, ones_ref, s7, s8, s9, s10, features_ref)
    mix_sum = forward(turned_ref, features_ref, y_ref, g_hidden_ref, cot_ref, hidden_ref, g_ref)

    home = part_of(0, 0)

    def spread(phase, source_of, target):
        for slot, (i, j) in enumerate(others):
            copy_to(
                source_of(part_of(i, j)), target.at[slot + 15 * (1 - core)], sends.at[phase], recvs.at[phase], chip(i, j, 0, 1)
            )

        @pl.when(core == 0)
        def _():
            copy_to(source_of(home), target.at[30], sends.at[phase], recvs.at[phase], chip(0, 0, 0, 1))

    for owner in range(OWNERS):
        mix_part[owner] = scale * mix_sum[SHARE * owner : SHARE * (owner + 1)]
    spread(0, lambda owner: mix_part.at[owner], mix_in)
    small = scale * backward(passed, folded, kappa, embed, features_ref, g_ref, cot_ref, z_ref)
    for row in range(2 * OWNERS):
        small_part[row // 2, row % 2] = small[row : row + 1]
    spread(1, lambda owner: small_part.at[owner], small_in)

    @pl.when(core == 1)
    def _():
        drain(mix_in, recvs.at[0])
        mixed = mix_part[home]
        for slot in range(31):
            mixed = mixed + mix_in[slot]
        for row in range(SHARE):
            second[z, row] = mixed[row : row + 1]
        drain(small_in, recvs.at[1])
        rows = small_part[home]
        for slot in range(31):
            rows = rows + small_in[slot]
        second[z, SHARE:PART] = rows
        for k in (2, 1, 3):
            copy_to(second.at[z], second.at[z], sends.at[2], recvs.at[2], chip(0, 0, k, 1))

    outputs(embed, features_ref, hidden_ref, mix_ref, out_ref)
    drain(held, ids_sems.at[3])

    @pl.when(core == 1)
    def _():
        drain(second.at[pl.ds(0, 3)], recvs.at[2])
        third[...] = (second[0] + second[1]) + (second[2] + second[3])
        landing = whole.at[pl.ds(PART * home, PART)]
        for i, j in plane:
            copy_to(third, landing, sends.at[3], recvs.at[3], chip(i, j, 0, 0))
            if (i, j) in others:
                copy_to(third, landing, sends.at[3], recvs.at[3], chip(i, j, 0, 1))
        whole[pl.ds(PART * home, PART)] = third[...]
        drain(mix_in.at[pl.ds(0, 15)], sends.at[0])
        drain(small_in.at[pl.ds(0, 15)], sends.at[1])
        drain(second.at[pl.ds(0, 3)], sends.at[2])
        drain(whole.at[pl.ds(0, 15 * PART)], recvs.at[3])
        drain(whole.at[pl.ds(0, 15 * PART)], sends.at[3])
        drain(whole, sends.at[3])

    @pl.when(core == 0)
    def _():
        drain(mix_in.at[pl.ds(0, 16)], sends.at[0])
        drain(small_in.at[pl.ds(0, 16)], sends.at[1])
        drain(whole, recvs.at[3])


def layer(count, scale, ids, embed, low, high, levels, mix, cot):
    vmem = pl.BlockSpec(memory_space=pltpu.VMEM)
    far = pl.BlockSpec(memory_space=pltpu.HBM)
    arguments = tuple(
        pltpu.with_memory_space_constraint(array, pltpu.HBM) for array in (ids, embed, low, high, levels, mix, cot)
    )
    return pl.pallas_call(
        functools.partial(layer_kernel, count, scale),
        out_shape=(
            jax.ShapeDtypeStruct((TOKENS, WIDTH), F32),
            jax.ShapeDtypeStruct((OWNERS * PART, 1, WIDTH), F32),
            jax.ShapeDtypeStruct((32, WIDTH), F32),
        ),
        in_specs=[far] * 7,
        out_specs=(vmem,) * 3,
        scratch_shapes=[
            pltpu.VMEM((BACK, 8, LANES), jnp.int32),
            pltpu.SemaphoreType.DMA((4,)),
            pltpu.VMEM((2 * LANES, 8 * LANES), BF16),
            pltpu.VMEM((2 * LANES, 29 * LANES), BF16),
            pltpu.VMEM((TILES * VOCAB, 2 * LANES), BF16),
            pltpu.VMEM((8 * VOCAB, TILES * LANES), BF16),
            pltpu.VMEM((9 * VOCAB, TILES * LANES), BF16),
            pltpu.VMEM((10 * VOCAB, TILES * LANES), BF16),
            pltpu.VMEM((11 * VOCAB, TILES * LANES), BF16),
            pltpu.VMEM((ROWS, TOKENS), BF16),
            pltpu.VMEM((ROWS, 2 * WIDTH), BF16),
            pltpu.VMEM((2 * WIDTH, ROWS), BF16),
            pltpu.VMEM((WIDTH, TOKENS), F32),
            pltpu.VMEM((TOKENS, WIDTH), F32),
            pltpu.VMEM((TOKENS, WIDTH), BF16),
            pltpu.VMEM((TOKENS, 2 * WIDTH), BF16),
            pltpu.VMEM((CLASSES * VOCAB, WIDTH), F32),
            *[pltpu.VMEM(array.shape, array.dtype) for array in arguments],
            pltpu.SemaphoreType.DMA((7,)),
            pltpu.VMEM((OWNERS, SHARE, WIDTH), F32),
            pltpu.VMEM((OWNERS, 2, 1, WIDTH), F32),
            pltpu.VMEM((31, SHARE, WIDTH), F32),
            pltpu.VMEM((31, 2, 1, WIDTH), F32),
            pltpu.VMEM((4, PART, 1, WIDTH), F32),
            pltpu.VMEM((PART, 1, WIDTH), F32),
            pltpu.SemaphoreType.DMA((4,)),
            pltpu.SemaphoreType.DMA((4,)),
        ],
        compiler_params=pltpu.CompilerParams(
            collective_id=0, has_side_effects=True, vmem_limit_bytes=44 * 2**20
        ),
    )(*arguments)


def finish_kernel(
    out_ref, whole, factors_ref,
    out_hbm, filters_hbm, levels_hbm, mix_hbm, embed_hbm,
    filters_ref, grad_levels_ref, mix_ref, embed_ref, sems,
):
    stores = []

    def store(source, target):
        copy = pltpu.make_async_copy(source, target, sems.at[len(stores)])
        copy.start()
        stores.append(copy)

    store(out_ref, out_hbm)
    for row in range(WIDTH):
        mix_ref[row : row + 1, :] = whole[PART * (row // SHARE) + row % SHARE]
    store(mix_ref, mix_hbm)
    summed = [whole[PART * (row // 2) + SHARE + row % 2] for row in range(2 * OWNERS)]
    for name in range(VOCAB):
        embed_ref[name : name + 1, :] = summed[16 + name]
    store(embed_ref, embed_hbm)
    shifted = summed[1:14]
    factors = rows_of(factors_ref)
    low, high, levels, folded = factors[0:2], factors[2:4], factors[4:18], factors[18:32]
    current = summed[0]
    low_zero, low_one = summed[14] / low[0], summed[15] / low[1]
    high_zero = high_one = jnp.zeros_like(current)
    for level in range(LEVELS):
        late = shifted[level]
        grad_levels_ref[level : level + 1, :] = high[0] * current + high[1] * late
        low_zero = low_zero + folded[level + 1] * current
        low_one = low_one + folded[level + 1] * late
        high_zero = high_zero + levels[level] * current
        high_one = high_one + levels[level] * late
        current = low[0] * current + low[1] * late
    grad_levels_ref[LEVELS : LEVELS + 1, :] = current
    filters_ref[0, 0:1, :] = low_zero
    filters_ref[0, 1:2, :] = low_one
    filters_ref[1, 0:1, :] = high_zero
    filters_ref[1, 1:2, :] = high_one
    store(filters_ref, filters_hbm)
    store(grad_levels_ref, levels_hbm)
    for copy in stores:
        copy.wait()


def finish(out, whole, factors):
    shapes = [(TOKENS, WIDTH), (2, 2, WIDTH), (LEVELS + 1, WIDTH), (WIDTH, WIDTH), (VOCAB, WIDTH)]
    return pl.pallas_call(
        finish_kernel,
        out_shape=tuple(jax.ShapeDtypeStruct(shape, F32) for shape in shapes),
        in_specs=[pl.BlockSpec(memory_space=pltpu.VMEM)] * 3,
        out_specs=(pl.BlockSpec(memory_space=pl.ANY),) * 5,
        scratch_shapes=[pltpu.VMEM(shape, F32) for shape in shapes[1:]] + [pltpu.SemaphoreType.DMA((5,))],
        compiler_params=pltpu.CompilerParams(vmem_limit_bytes=16 * 2**20),
    )(out, whole, factors)


def per_device(ids, embed, low_filter, high_filter, level_weights, mix, cotangent):
    count = lax.axis_size("seq")
    scale = 1.0 / math.sqrt(count * lax.axis_size("batch") * TOKENS)
    out, whole, factors = layer(
        count, scale, ids.reshape(8, LANES), embed, low_filter, high_filter, level_weights, mix, cotangent[0]
    )
    out, grad_filters, grad_levels, grad_mix, grad_embed = finish(out, whole, factors)
    return out[None], grad_filters, grad_levels, grad_mix, grad_embed


def solution(mesh):
    placed = (P("batch", "seq"), P(), P(), P(), P(), P(), P("batch", "seq", None))
    return jax.shard_map(
        per_device,
        mesh=mesh,
        in_specs=placed,
        out_specs=(P("batch", "seq", None), P(), P(), P(), P()),
        check_vma=False,
    )
```

```python
import functools
import math

import jax
import jax.numpy as jnp
from jax import lax
from jax.experimental import pallas as pl
from jax.experimental.pallas import tpu as pltpu
from jax.sharding import PartitionSpec as P

MESH = pl.DeviceIdType.MESH
F32, BF16 = jnp.float32, jnp.bfloat16
LEVELS = 13
VOCAB = 16
WIDTH = 256
LANES = 128
TOKENS = 1024
BACK = 8
TILES = (BACK + 1) * TOKENS // LANES
SPLIT = {11: range(4, 8), 12: range(4, 9)}
CLASSES = 101
ROWS = 104 * VOCAB
NEAR = 56 * VOCAB
CHUNKS = 32


def class_of(level, ones):
    return 1 + level * (level + 1) // 2 + ones


def block_of(level, ones):
    return slice(class_of(level, ones) * VOCAB, (class_of(level, ones) + 1) * VOCAB)


def rest_of(level, ones):
    place = 92 + 4 * (level - 11) + ones - 4
    return slice(place * VOCAB, (place + 1) * VOCAB)


def dot(a, b):
    return jnp.dot(a, b, preferred_element_type=F32)


def halves(value):
    high = value.astype(BF16)
    return high, (value - high.astype(F32)).astype(BF16)


def level_factors(low, high, weights):
    folded = [None] * (LEVELS + 1)
    kappa = [None] * LEVELS
    folded[LEVELS] = weights[LEVELS]
    for level in range(LEVELS - 1, -1, -1):
        kappa[level] = weights[level] * high[1] + low[1] * folded[level + 1]
        folded[level] = weights[level] * high[0] + low[0] * folded[level + 1]
    return folded, kappa


def rows_of(ref):
    return [ref[row : row + 1, :] for row in range(ref.shape[0])]


def lag_weights(low):
    chains = []
    for row in low:
        chain = [jnp.ones_like(row)]
        for _ in range(LEVELS - 1):
            chain.append(chain[-1] * row)
        chains.append(chain)
    return lambda level, ones: chains[0][level - ones] * chains[1][ones]


def clear_padding(ref):
    ref[CLASSES * VOCAB :, :] = jnp.zeros((ROWS - CLASSES * VOCAB, ref.shape[1]), BF16)


def make_weights(passed, folded, kappa, embed, weights_ref):
    def put(rows, factor):
        high, rest = halves(factor * embed)
        weights_ref[rows, 0:WIDTH] = high
        weights_ref[rows, WIDTH:] = rest

    put(slice(0, VOCAB), folded[0])
    for level in range(LEVELS):
        for ones in range(level + 1):
            put(block_of(level, ones), kappa[level] * passed(level, ones))
            if ones in SPLIT.get(level, ()):
                put(rest_of(level, ones), kappa[level] * passed(level, ones))
    clear_padding(weights_ref)


def where_is(table, value):
    return jnp.where(table == value, 1.0, 0.0).astype(BF16)


def make_tables(ones_ref, class_ref):
    place = lax.broadcasted_iota(jnp.int32, (2 * LANES, LANES), 0)
    lag = lax.broadcasted_iota(jnp.int32, (2 * LANES, LANES), 1) - place
    lag = jnp.where(place >= LANES, lag + 2 * LANES, lag)
    inside = (lag >= 0) & (lag < LANES)
    ones = jnp.zeros_like(lag)
    offset = jnp.zeros_like(lag)
    for bit in range(7):
        ones = ones + ((lag >> bit) & 1)
        offset = offset + jnp.where(lag >= 2**bit, bit, 0)
    klass = jnp.where(inside, jnp.where(lag == 0, 0, offset + ones), -1)
    ones = jnp.where(inside, ones, -1)
    for value in range(8):
        ones_ref[:, value * LANES : (value + 1) * LANES] = where_is(ones, value)
    for value in range(29):
        class_ref[:, value * LANES : (value + 1) * LANES] = where_is(klass, value)


def make_hot(tokens_ref, first, ids):
    names = lax.broadcasted_iota(jnp.int32, (VOCAB, LANES), 0)
    for row in range(8):
        tile = first + row
        hot = where_is(names, jnp.broadcast_to(ids[row : row + 1, :], (VOCAB, LANES)))
        tokens_ref[tile * VOCAB : (tile + 1) * VOCAB, 0:LANES] = hot
        if tile + 1 < TILES:
            tokens_ref[(tile + 1) * VOCAB : (tile + 2) * VOCAB, LANES:] = hot


def put_counts(result, s7, first, last, pair):
    for tile in range(first, last):
        for half in range(2):
            value = 2 * pair + half
            s7[value * VOCAB : (value + 1) * VOCAB, tile * LANES : (tile + 1) * LANES] = result[
                (tile - first) * VOCAB : (tile - first + 1) * VOCAB, half * LANES : (half + 1) * LANES
            ]


def count_tiles(tokens_ref, ones_ref, s7, first, last):
    for pair in range(4):
        table = ones_ref[:, 2 * pair * LANES : 2 * (pair + 1) * LANES]
        result = dot(tokens_ref[first * VOCAB : last * VOCAB, :], table).astype(BF16)
        put_counts(result, s7, first, last, pair)


def widened(source, level, ones, first, last):
    begin, end, span = first * LANES, last * LANES, 2**level
    total = None
    if 0 <= ones <= level:
        total = source[ones * VOCAB : (ones + 1) * VOCAB, begin:end]
    if 1 <= ones <= level + 1:
        late = source[(ones - 1) * VOCAB : ones * VOCAB, begin - span : end - span]
        total = late if total is None else total + late
    return total


def widen(source, target, level, first, last):
    for ones in range(level + 2):
        target[ones * VOCAB : (ones + 1) * VOCAB, first * LANES : last * LANES] = widened(
            source, level, ones, first, last
        )


def place_level(source, level, features_ref):
    rows = slice(class_of(level, 0) * VOCAB, class_of(level + 1, 0) * VOCAB)
    begin = BACK * TOKENS - 2**level
    features_ref[rows, :] = source[:, begin : begin + TOKENS]


def make_near(tokens_ref, class_ref, ones_ref, s7, s8, s9, features_ref):
    own = tokens_ref[64 * VOCAB : 72 * VOCAB, :]
    for first in range(0, 29, 2):
        members = range(first, min(first + 2, 29))
        result = dot(own, class_ref[:, first * LANES : (first + len(members)) * LANES]).astype(BF16)
        for tile in range(8):
            for half, member in enumerate(members):
                features_ref[member * VOCAB : (member + 1) * VOCAB, tile * LANES : (tile + 1) * LANES] = result[
                    tile * VOCAB : (tile + 1) * VOCAB, half * LANES : (half + 1) * LANES
                ]
    count_tiles(tokens_ref, ones_ref, s7, 57, 71)
    widen(s7, s8, 7, 58, 70)
    widen(s8, s9, 8, 60, 68)
    place_level(s7, 7, features_ref)
    place_level(s8, 8, features_ref)
    place_level(s9, 9, features_ref)


def put_sum(features_ref, level, ones, terms):
    terms = [term for term in terms if term is not None]
    if ones in SPLIT[level]:
        total = sum(term.astype(F32) for term in terms)
        high, rest = halves(total)
        features_ref[block_of(level, ones), :] = high
        features_ref[rest_of(level, ones), :] = rest
    else:
        features_ref[block_of(level, ones), :] = sum(terms[1:], terms[0])


def make_far(tokens_ref, ones_ref, s7, s8, s9, s10, features_ref):
    count_tiles(tokens_ref, ones_ref, s7, 1, 57)
    widen(s7, s8, 7, 2, 58)
    widen(s8, s9, 8, 4, 60)
    widen(s9, s10, 9, 8, 64)
    place_level(s10, 10, features_ref)

    def shard(back, ones):
        first = (BACK - back) * 8
        return s10[ones * VOCAB : (ones + 1) * VOCAB, first * LANES : (first + 8) * LANES] if 0 <= ones <= 10 else None

    for ones in range(12):
        put_sum(features_ref, 11, ones, [shard(2, ones), shard(3, ones - 1)])
    for ones in range(13):
        put_sum(
            features_ref, 12, ones, [shard(4, ones), shard(5, ones - 1), shard(6, ones - 1), shard(7, ones - 2)]
        )


def gelu_parts(y):
    root = math.sqrt(2.0 / math.pi)
    square = y * y
    bend = jnp.tanh(root * (y + 0.044715 * square * y))
    half = 0.5 * (1.0 + bend)
    slope = half + 0.5 * y * (1.0 - bend * bend) * (root * (1.0 + 3 * 0.044715 * square))
    return y * half, slope


def near_part(turned_ref, features_ref, y_ref):
    for start in range(0, TOKENS, 256):
        span = slice(start, start + 256)
        both = dot(turned_ref[:, 0:NEAR], features_ref[0:NEAR, span])
        y_ref[:, span] = both[:WIDTH] + both[WIDTH:]


def before_gelu(mix_ref, cot_ref, g_hidden_ref):
    g_hidden_ref[...] = lax.dot_general(
        cot_ref[...], mix_ref[...], (((1,), (1,)), ((), ())), preferred_element_type=F32
    )


def forward(turned_ref, features_ref, y_ref, g_hidden_ref, cot_ref, hidden_ref, g_ref):
    mix_sum = None
    block = 256
    for start in range(0, TOKENS, block):
        span = slice(start, start + block)
        both = dot(turned_ref[:, NEAR:], features_ref[NEAR:, span])
        y = (y_ref[:, span] + both[:WIDTH] + both[WIDTH:]).T
        active, slope = gelu_parts(y)
        hidden = active.astype(BF16)
        hidden_ref[span, :] = hidden
        g_high, g_rest = halves(g_hidden_ref[span, :] * slope)
        g_ref[span, 0:WIDTH] = g_high
        g_ref[span, WIDTH:] = g_rest
        term = lax.dot_general(hidden, cot_ref[span, :], (((0,), (0,)), ((), ())), preferred_element_type=F32)
        mix_sum = term if mix_sum is None else mix_sum + term
    return mix_sum


def outputs(embed, features_ref, hidden_ref, mix_ref, out_ref):
    high, middle = halves(embed)
    rest = (embed - high.astype(F32) - middle.astype(F32)).astype(BF16)
    table = jnp.concatenate([high, middle, rest], axis=0)
    for start in range(0, TOKENS, 256):
        span = slice(start, start + 256)
        hot = features_ref[0:VOCAB, span]
        hot = jnp.concatenate([hot, hot, hot], axis=0)
        x = lax.dot_general(hot, table, (((0,), (0,)), ((), ())), preferred_element_type=F32)
        out_ref[span, :] = x + dot(hidden_ref[span, :], mix_ref[...])


def backward(passed, folded, kappa, embed, features_ref, g_ref, cot_ref, z_ref):
    def over_names(value):
        return jnp.sum(embed * value, axis=0, keepdims=True)

    def products(first, last):
        both = dot(features_ref[first:last, :], g_ref[...])
        z_ref[first:last, :] = both[:, :WIDTH] + both[:, WIDTH:]

    ends = {0: class_of(8, 0) * VOCAB, 8: class_of(11, 0) * VOCAB, 11: CLASSES * VOCAB}

    def z_of(level, ones):
        z = z_ref[block_of(level, ones), :]
        return z + z_ref[rest_of(level, ones), :] if ones in SPLIT.get(level, ()) else z

    begin = 0
    rows = []
    for level in range(LEVELS):
        if level in ends:
            products(begin, ends[level])
            begin = ends[level]
        if level == 0:
            z0 = z_ref[0:VOCAB, :]
            rows.append(over_names(z0))
            embed_sum = folded[0] * z0 + dot(features_ref[0:VOCAB, :], cot_ref[...])
            zero_sum = one_sum = jnp.zeros_like(z0)
        total = passed(level, 0) * z_of(level, 0)
        counted = jnp.zeros_like(total)
        for ones in range(1, level + 1):
            term = passed(level, ones) * z_of(level, ones)
            total = total + term
            counted = counted + float(ones) * term
        rows.append(over_names(total))
        embed_sum = embed_sum + kappa[level] * total
        one_sum = one_sum + kappa[level] * counted
        zero_sum = zero_sum + kappa[level] * (float(level) * total - counted)
    rows += [over_names(zero_sum), over_names(one_sum)]
    return jnp.concatenate(rows + [embed_sum], axis=0)


def layer_kernel(
    count, scale, ids_hbm, embed_hbm, low_hbm, high_hbm, levels_hbm, mix_hbm, cot_hbm,
    out_ref, whole, factors_ref,
    held, ids_sems, ones_ref, class_ref, tokens_ref, s7, s8, s9, s10, features_ref, weights_ref, turned_ref,
    y_ref, g_hidden_ref, hidden_ref, g_ref, z_ref, ids_ref, embed_ref, low_ref, high_ref, levels_ref, mix_ref, cot_ref, local_sem,
    mix_part, small_part, mix_in, small_in, second, third, sends, recvs,
):
    seq, batch = lax.axis_index("seq"), lax.axis_index("batch")
    x, y = lax.rem(seq, 4), lax.rem(lax.div(seq, 4), 4)
    core = lax.rem(batch, 2)
    z = lax.div(seq, 16) * 2 + lax.div(batch, 2)

    def along(order):
        return x + order * (y - x), y + order * (z - y), z + order * (x - z)

    def device(order, spots, core):
        a, b, c = spots
        x, y, z = a + order * (c - a), b + order * (a - b), c + order * (b - c)
        return lax.div(z, 2) * 16 + y * 4 + x, lax.rem(z, 2) * 2 + core

    def moved(spots, i, j, k):
        return lax.rem(spots[0] + i, 4), lax.rem(spots[1] + j, 4), lax.rem(spots[2] + k, 4)

    mine, theirs = along(core), along(1 - core)
    hops = lambda spot: sum(min(step, 4 - step) for step in spot)
    plane = sorted([(i, j) for i in range(4) for j in range(4)], key=hops, reverse=True)
    others = plane[:-1]
    own_peer = lambda i, j, k: device(core, moved(mine, i, j, k), core)
    their_peer = lambda i, j: device(1 - core, moved(theirs, i, j, 0), 1 - core)
    cross_peer = lambda i, j: device(core, moved(mine, i, j, 0), 1 - core)
    chunk_of = lambda core, spots: 16 * core + 4 * spots[0] + spots[1]

    barrier = pltpu.get_barrier_semaphore()

    def greet(peer):
        pl.semaphore_signal(barrier, inc=1, device_id=peer, device_id_type=MESH)

    for step in range(1, BACK + 1):
        greet((lax.rem(seq + count - step, count), batch))
    for i, j in others:
        greet(own_peer(i, j, 0))
    for k in range(1, 4):
        greet(own_peer(0, 0, k))
    for i, j in plane:
        greet(their_peer(i, j))
        if i:
            greet(cross_peer(i + core * (j - i), j + core * (i - j)))
    loads = [
        pltpu.make_async_copy(source, target, local_sem.at[place])
        for place, (source, target) in enumerate(
            [
                (ids_hbm, ids_ref),
                (embed_hbm, embed_ref),
                (low_hbm, low_ref),
                (high_hbm, high_ref),
                (levels_hbm, levels_ref),
                (mix_hbm, mix_ref),
                (cot_hbm, cot_ref),
            ]
        )
    ]
    for load in loads:
        load.start()
    pl.semaphore_wait(barrier, BACK + 46)

    def copy_to(source, target, sent, received, peer):
        copy = pltpu.make_async_remote_copy(
            src_ref=source, dst_ref=target, send_sem=sent, recv_sem=received, device_id=peer, device_id_type=MESH
        )
        copy.start()
        return copy

    def drain(ref, sem):
        pltpu.make_async_copy(ref, ref, sem).wait()

    arrivals = [(0, 1), (1, BACK)]
    for group, (first, last) in reversed(list(enumerate(arrivals))):
        for step in range(first, last):
            peer = lax.rem(seq + step + 1, count), batch
            copy_to(ids_hbm, held.at[step], ids_sems.at[2], ids_sems.at[group], peer)

    for load in loads:
        load.wait()
    embed = embed_ref[...]
    low, high, levels = rows_of(low_ref), rows_of(high_ref), rows_of(levels_ref)
    folded, kappa = level_factors(low, high, levels)
    passed = lag_weights(low)
    make_weights(passed, folded, kappa, embed, weights_ref)
    turned_ref[...] = weights_ref[...].T
    make_tables(ones_ref, class_ref)
    tokens_ref[0:VOCAB, LANES:] = jnp.zeros((VOCAB, LANES), BF16)
    clear_padding(features_ref)
    before_gelu(mix_ref, cot_ref, g_hidden_ref)
    make_hot(tokens_ref, 8 * BACK, ids_ref[...])

    factors_ref[0:2, :] = low_ref[...]
    factors_ref[2:4, :] = high_ref[...]
    factors_ref[4:18, :] = levels_ref[...]
    for level in range(LEVELS + 1):
        factors_ref[18 + level : 19 + level, :] = folded[level]

    def receive(group):
        first, last = arrivals[group]
        drain(held.at[pl.ds(first, last - first)], ids_sems.at[group])
        for step in range(first, last):
            make_hot(tokens_ref, 8 * (BACK - 1 - step), jnp.where(seq > step, held[step], -1))

    receive(0)
    make_near(tokens_ref, class_ref, ones_ref, s7, s8, s9, features_ref)
    near_part(turned_ref, features_ref, y_ref)
    receive(1)
    make_far(tokens_ref, ones_ref, s7, s8, s9, s10, features_ref)
    mix_sum = forward(turned_ref, features_ref, y_ref, g_hidden_ref, cot_ref, hidden_ref, g_ref)

    home = chunk_of(core, mine)

    def spread(phase, part, target):
        for slot, (i, j) in enumerate(plane):
            place = chunk_of(1 - core, moved(theirs, i, j, 0))
            copy_to(part.at[place], target.at[slot + 15], sends.at[phase], recvs.at[phase], their_peer(i, j))
            if (i, j) in others:
                place = chunk_of(core, moved(mine, i, j, 0))
                copy_to(part.at[place], target.at[slot], sends.at[phase], recvs.at[phase], own_peer(i, j, 0))

    for chunk in range(CHUNKS):
        mix_part[chunk] = scale * mix_sum[8 * chunk : 8 * chunk + 8]
    small = scale * backward(passed, folded, kappa, embed, features_ref, g_ref, cot_ref, z_ref)
    spread(0, mix_part, mix_in)
    for chunk in range(CHUNKS):
        small_part[chunk] = small[chunk : chunk + 1]
    spread(1, small_part, small_in)
    drain(mix_in, recvs.at[0])
    mixed = mix_part[home]
    for slot in range(CHUNKS - 1):
        mixed = mixed + mix_in[slot]
    for row in range(8):
        second[mine[2], row] = mixed[row : row + 1]
    drain(small_in, recvs.at[1])
    row = small_part[home]
    for slot in range(CHUNKS - 1):
        row = row + small_in[slot]
    second[mine[2], 8] = row
    spot = second.at[mine[2]]
    for k in (2, 1, 3):
        copy_to(spot, spot, sends.at[2], recvs.at[2], own_peer(0, 0, k))
    outputs(embed, features_ref, hidden_ref, mix_ref, out_ref)
    drain(second.at[pl.ds(0, 3)], recvs.at[2])
    third[...] = (second[0] + second[1]) + (second[2] + second[3])
    landing = whole.at[pl.ds(9 * home, 9)]
    for i, j in plane:
        copy_to(third, landing, sends.at[3], recvs.at[3], cross_peer(i, j))
        if (i, j) in others:
            copy_to(third, landing, sends.at[3], recvs.at[3], own_peer(i, j, 0))
    whole[pl.ds(9 * home, 9)] = third[...]
    drain(held, ids_sems.at[2])
    drain(mix_in, sends.at[0])
    drain(small_in, sends.at[1])
    drain(second.at[pl.ds(0, 3)], sends.at[2])
    gathered = whole.at[pl.ds(0, 9 * (CHUNKS - 1))]
    drain(gathered, recvs.at[3])
    drain(gathered, sends.at[3])


def layer(count, scale, ids, embed, low, high, levels, mix, cot):
    vmem = pl.BlockSpec(memory_space=pltpu.VMEM)
    far = pl.BlockSpec(memory_space=pltpu.HBM)
    arguments = tuple(
        pltpu.with_memory_space_constraint(array, pltpu.HBM) for array in (ids, embed, low, high, levels, mix, cot)
    )
    return pl.pallas_call(
        functools.partial(layer_kernel, count, scale),
        out_shape=(
            jax.ShapeDtypeStruct((TOKENS, WIDTH), F32),
            jax.ShapeDtypeStruct((9 * CHUNKS, 1, WIDTH), F32),
            jax.ShapeDtypeStruct((32, WIDTH), F32),
        ),
        in_specs=[far] * 7,
        out_specs=(vmem,) * 3,
        scratch_shapes=[
            pltpu.VMEM((BACK, 8, LANES), jnp.int32),
            pltpu.SemaphoreType.DMA((3,)),
            pltpu.VMEM((2 * LANES, 8 * LANES), BF16),
            pltpu.VMEM((2 * LANES, 29 * LANES), BF16),
            pltpu.VMEM((TILES * VOCAB, 2 * LANES), BF16),
            pltpu.VMEM((8 * VOCAB, TILES * LANES), BF16),
            pltpu.VMEM((9 * VOCAB, TILES * LANES), BF16),
            pltpu.VMEM((10 * VOCAB, TILES * LANES), BF16),
            pltpu.VMEM((11 * VOCAB, TILES * LANES), BF16),
            pltpu.VMEM((ROWS, TOKENS), BF16),
            pltpu.VMEM((ROWS, 2 * WIDTH), BF16),
            pltpu.VMEM((2 * WIDTH, ROWS), BF16),
            pltpu.VMEM((WIDTH, TOKENS), F32),
            pltpu.VMEM((TOKENS, WIDTH), F32),
            pltpu.VMEM((TOKENS, WIDTH), BF16),
            pltpu.VMEM((TOKENS, 2 * WIDTH), BF16),
            pltpu.VMEM((CLASSES * VOCAB, WIDTH), F32),
            *[pltpu.VMEM(array.shape, array.dtype) for array in arguments],
            pltpu.SemaphoreType.DMA((7,)),
            pltpu.VMEM((CHUNKS, 8, WIDTH), F32),
            pltpu.VMEM((CHUNKS, 1, WIDTH), F32),
            pltpu.VMEM((CHUNKS - 1, 8, WIDTH), F32),
            pltpu.VMEM((CHUNKS - 1, 1, WIDTH), F32),
            pltpu.VMEM((4, 9, 1, WIDTH), F32),
            pltpu.VMEM((9, 1, WIDTH), F32),
            pltpu.SemaphoreType.DMA((4,)),
            pltpu.SemaphoreType.DMA((4,)),
        ],
        compiler_params=pltpu.CompilerParams(
            collective_id=0, has_side_effects=True, vmem_limit_bytes=44 * 2**20
        ),
    )(*arguments)


def finish_kernel(
    out_ref, whole, factors_ref,
    out_hbm, filters_hbm, levels_hbm, mix_hbm, embed_hbm,
    filters_ref, grad_levels_ref, mix_ref, embed_ref, sems,
):
    stores = []

    def store(source, target):
        copy = pltpu.make_async_copy(source, target, sems.at[len(stores)])
        copy.start()
        stores.append(copy)

    store(out_ref, out_hbm)
    for chunk in range(CHUNKS):
        for row in range(8):
            mix_ref[8 * chunk + row : 8 * chunk + row + 1, :] = whole[9 * chunk + row]
    store(mix_ref, mix_hbm)
    summed = [whole[9 * chunk + 8] for chunk in range(CHUNKS)]
    for name in range(VOCAB):
        embed_ref[name : name + 1, :] = summed[16 + name]
    store(embed_ref, embed_hbm)
    shifted = summed[1:14]
    factors = rows_of(factors_ref)
    low, high, levels, folded = factors[0:2], factors[2:4], factors[4:18], factors[18:32]
    current = summed[0]
    low_zero, low_one = summed[14] / low[0], summed[15] / low[1]
    high_zero = high_one = jnp.zeros_like(current)
    for level in range(LEVELS):
        late = shifted[level]
        grad_levels_ref[level : level + 1, :] = high[0] * current + high[1] * late
        low_zero = low_zero + folded[level + 1] * current
        low_one = low_one + folded[level + 1] * late
        high_zero = high_zero + levels[level] * current
        high_one = high_one + levels[level] * late
        current = low[0] * current + low[1] * late
    grad_levels_ref[LEVELS : LEVELS + 1, :] = current
    filters_ref[0, 0:1, :] = low_zero
    filters_ref[0, 1:2, :] = low_one
    filters_ref[1, 0:1, :] = high_zero
    filters_ref[1, 1:2, :] = high_one
    store(filters_ref, filters_hbm)
    store(grad_levels_ref, levels_hbm)
    for copy in stores:
        copy.wait()


def finish(out, whole, factors):
    shapes = [(TOKENS, WIDTH), (2, 2, WIDTH), (LEVELS + 1, WIDTH), (WIDTH, WIDTH), (VOCAB, WIDTH)]
    return pl.pallas_call(
        finish_kernel,
        out_shape=tuple(jax.ShapeDtypeStruct(shape, F32) for shape in shapes),
        in_specs=[pl.BlockSpec(memory_space=pltpu.VMEM)] * 3,
        out_specs=(pl.BlockSpec(memory_space=pl.ANY),) * 5,
        scratch_shapes=[pltpu.VMEM(shape, F32) for shape in shapes[1:]] + [pltpu.SemaphoreType.DMA((5,))],
        compiler_params=pltpu.CompilerParams(vmem_limit_bytes=16 * 2**20),
    )(out, whole, factors)


def per_device(ids, embed, low_filter, high_filter, level_weights, mix, cotangent):
    count = lax.axis_size("seq")
    scale = 1.0 / math.sqrt(count * lax.axis_size("batch") * TOKENS)
    out, whole, factors = layer(
        count, scale, ids.reshape(8, LANES), embed, low_filter, high_filter, level_weights, mix, cotangent[0]
    )
    out, grad_filters, grad_levels, grad_mix, grad_embed = finish(out, whole, factors)
    return out[None], grad_filters, grad_levels, grad_mix, grad_embed


def solution(mesh):
    placed = (P("batch", "seq"), P(), P(), P(), P(), P(), P("batch", "seq", None))
    return jax.shard_map(
        per_device,
        mesh=mesh,
        in_specs=placed,
        out_specs=(P("batch", "seq", None), P(), P(), P(), P()),
        check_vma=False,
    )
```

```python
import functools
import math

import jax
import jax.numpy as jnp
from jax import lax
from jax.experimental import pallas as pl
from jax.experimental.pallas import tpu as pltpu
from jax.sharding import PartitionSpec as P

MESH = pl.DeviceIdType.MESH
F32, BF16 = jnp.float32, jnp.bfloat16
LEVELS = 13
VOCAB = 16
WIDTH = 256
LANES = 128
TOKENS = 1024
BACK = 8
TILES = (BACK + 1) * TOKENS // LANES
SPLIT = {11: range(4, 8), 12: range(4, 9)}
CLASSES = 101
ROWS = 104 * VOCAB
NEAR = 56 * VOCAB
PIECES = ((0, 37 * VOCAB), (37 * VOCAB, 46 * VOCAB), (46 * VOCAB, NEAR), (NEAR, ROWS))
STARTS = (0, 640, 896, 1152)
WEIGHTS = STARTS[3] + ROWS - NEAR
CHUNKS = 32


def class_of(level, ones):
    return 1 + level * (level + 1) // 2 + ones


def block_of(level, ones):
    return slice(class_of(level, ones) * VOCAB, (class_of(level, ones) + 1) * VOCAB)


def rest_of(level, ones):
    place = 92 + 4 * (level - 11) + ones - 4
    return slice(place * VOCAB, (place + 1) * VOCAB)


def dot(a, b):
    return jnp.dot(a, b, preferred_element_type=F32)


def halves(value):
    high = value.astype(BF16)
    return high, (value - high.astype(F32)).astype(BF16)


def level_factors(low, high, weights):
    folded = [None] * (LEVELS + 1)
    kappa = [None] * LEVELS
    folded[LEVELS] = weights[LEVELS]
    for level in range(LEVELS - 1, -1, -1):
        kappa[level] = weights[level] * high[1] + low[1] * folded[level + 1]
        folded[level] = weights[level] * high[0] + low[0] * folded[level + 1]
    return folded, kappa


def rows_of(ref):
    return [ref[row : row + 1, :] for row in range(ref.shape[0])]


def lag_weights(low):
    chains = []
    for row in low:
        chain = [jnp.ones_like(row)]
        for _ in range(LEVELS - 1):
            chain.append(chain[-1] * row)
        chains.append(chain)
    return lambda level, ones: chains[0][level - ones] * chains[1][ones]


def make_weights(passed, folded, kappa, embed, weights_ref):
    weights_ref[...] = jnp.zeros_like(weights_ref)

    def put(rows, factor):
        shift = next(start - piece[0] for piece, start in zip(PIECES, STARTS) if rows.start < piece[1])
        rows = slice(rows.start + shift, rows.stop + shift)
        high, rest = halves(factor * embed)
        weights_ref[rows, 0:WIDTH] = high
        weights_ref[rows, WIDTH:] = rest

    put(slice(0, VOCAB), folded[0])
    for level in range(LEVELS):
        for ones in range(level + 1):
            put(block_of(level, ones), kappa[level] * passed(level, ones))
            if ones in SPLIT.get(level, ()):
                put(rest_of(level, ones), kappa[level] * passed(level, ones))


def where_is(table, value):
    return jnp.where(table == value, 1.0, 0.0).astype(BF16)


def make_tables(ones_ref, class_ref):
    place = lax.broadcasted_iota(jnp.int32, (2 * LANES, LANES), 0)
    lag = lax.broadcasted_iota(jnp.int32, (2 * LANES, LANES), 1) - place
    lag = jnp.where(place >= LANES, lag + 2 * LANES, lag)
    inside = (lag >= 0) & (lag < LANES)
    ones = jnp.zeros_like(lag)
    offset = jnp.zeros_like(lag)
    for bit in range(7):
        ones = ones + ((lag >> bit) & 1)
        offset = offset + jnp.where(lag >= 2**bit, bit, 0)
    klass = jnp.where(inside, jnp.where(lag == 0, 0, offset + ones), -1)
    ones = jnp.where(inside, ones, -1)
    for value in range(8):
        ones_ref[:, value * LANES : (value + 1) * LANES] = where_is(ones, value)
    for value in range(29):
        class_ref[:, value * LANES : (value + 1) * LANES] = where_is(klass, value)


def make_hot(tokens_ref, first, ids):
    names = lax.broadcasted_iota(jnp.int32, (VOCAB, LANES), 0)
    for row in range(8):
        tile = first + row
        hot = where_is(names, jnp.broadcast_to(ids[row : row + 1, :], (VOCAB, LANES)))
        tokens_ref[tile * VOCAB : (tile + 1) * VOCAB, 0:LANES] = hot
        if tile + 1 < TILES:
            tokens_ref[(tile + 1) * VOCAB : (tile + 2) * VOCAB, LANES:] = hot


def put_counts(result, s7, first, last, pair):
    for tile in range(first, last):
        for half in range(2):
            value = 2 * pair + half
            s7[value * VOCAB : (value + 1) * VOCAB, tile * LANES : (tile + 1) * LANES] = result[
                (tile - first) * VOCAB : (tile - first + 1) * VOCAB, half * LANES : (half + 1) * LANES
            ]


def count_tiles(tokens_ref, ones_ref, s7, first, last):
    for pair in range(4):
        table = ones_ref[:, 2 * pair * LANES : 2 * (pair + 1) * LANES]
        result = dot(tokens_ref[first * VOCAB : last * VOCAB, :], table).astype(BF16)
        put_counts(result, s7, first, last, pair)


def widened(source, level, ones, first, last):
    begin, end, span = first * LANES, last * LANES, 2**level
    total = None
    if 0 <= ones <= level:
        total = source[ones * VOCAB : (ones + 1) * VOCAB, begin:end]
    if 1 <= ones <= level + 1:
        late = source[(ones - 1) * VOCAB : ones * VOCAB, begin - span : end - span]
        total = late if total is None else total + late
    return total


def widen(source, target, level, first, last):
    for ones in range(level + 2):
        target[ones * VOCAB : (ones + 1) * VOCAB, first * LANES : last * LANES] = widened(
            source, level, ones, first, last
        )


def place_level(source, level, features_ref):
    rows = slice(class_of(level, 0) * VOCAB, class_of(level + 1, 0) * VOCAB)
    begin = BACK * TOKENS - 2**level
    features_ref[rows, :] = source[:, begin : begin + TOKENS]


def count_classes(tokens_ref, class_ref, features_ref, first, last):
    tokens = tokens_ref[first * VOCAB : last * VOCAB, :]
    for begin in range(0, 29, 2):
        members = range(begin, min(begin + 2, 29))
        result = dot(tokens, class_ref[:, begin * LANES : (begin + len(members)) * LANES]).astype(BF16)
        for tile in range(first, last):
            place = (tile - 8 * BACK) * LANES
            for half, member in enumerate(members):
                features_ref[member * VOCAB : (member + 1) * VOCAB, place : place + LANES] = result[
                    (tile - first) * VOCAB : (tile - first + 1) * VOCAB, half * LANES : (half + 1) * LANES
                ]


def place_tiles(source, level, features_ref, first, last):
    rows = slice(class_of(level, 0) * VOCAB, class_of(level + 1, 0) * VOCAB)
    begin = BACK * TOKENS - 2**level
    features_ref[rows, first * LANES : last * LANES] = source[:, begin + first * LANES : begin + last * LANES]


def make_own(tokens_ref, class_ref, ones_ref, s7, s8, features_ref):
    count_classes(tokens_ref, class_ref, features_ref, 65, 72)
    count_tiles(tokens_ref, ones_ref, s7, 65, 71)
    widen(s7, s8, 7, 66, 70)
    place_tiles(s7, 7, features_ref, 2, 8)
    place_tiles(s8, 8, features_ref, 4, 8)


def make_near(tokens_ref, class_ref, ones_ref, s7, s8, s9, features_ref):
    count_classes(tokens_ref, class_ref, features_ref, 64, 65)
    count_tiles(tokens_ref, ones_ref, s7, 57, 65)
    widen(s7, s8, 7, 58, 66)
    widen(s8, s9, 8, 60, 68)
    place_tiles(s7, 7, features_ref, 0, 2)
    place_tiles(s8, 8, features_ref, 0, 4)
    place_level(s9, 9, features_ref)


def put_sum(features_ref, level, ones, terms):
    terms = [term for term in terms if term is not None]
    if ones in SPLIT[level]:
        total = sum(term.astype(F32) for term in terms)
        high, rest = halves(total)
        features_ref[block_of(level, ones), :] = high
        features_ref[rest_of(level, ones), :] = rest
    else:
        features_ref[block_of(level, ones), :] = sum(terms[1:], terms[0])


def make_far(tokens_ref, ones_ref, s7, s8, s9, s10, features_ref):
    count_tiles(tokens_ref, ones_ref, s7, 1, 57)
    widen(s7, s8, 7, 2, 58)
    widen(s8, s9, 8, 4, 60)
    widen(s9, s10, 9, 8, 64)
    place_level(s10, 10, features_ref)

    def shard(back, ones):
        first = (BACK - back) * 8
        return s10[ones * VOCAB : (ones + 1) * VOCAB, first * LANES : (first + 8) * LANES] if 0 <= ones <= 10 else None

    for ones in range(12):
        put_sum(features_ref, 11, ones, [shard(2, ones), shard(3, ones - 1)])
    for ones in range(13):
        put_sum(
            features_ref, 12, ones, [shard(4, ones), shard(5, ones - 1), shard(6, ones - 1), shard(7, ones - 2)]
        )


def gelu_parts(y):
    root = math.sqrt(2.0 / math.pi)
    square = y * y
    bend = jnp.tanh(root * (y + 0.044715 * square * y))
    half = 0.5 * (1.0 + bend)
    slope = half + 0.5 * y * (1.0 - bend * bend) * (root * (1.0 + 3 * 0.044715 * square))
    return y * half, slope


def piece_of_y(turned_ref, features_ref, piece, span):
    (first, last), start = PIECES[piece], STARTS[piece]
    both = dot(turned_ref[:, start : start + last - first], features_ref[first:last, span])
    return both[:WIDTH] + both[WIDTH:]


def parts_of_y(turned_ref, features_ref, y_ref, wanted):
    for piece, first, last in wanted:
        span = slice(first, last)
        part = piece_of_y(turned_ref, features_ref, piece, span)
        y_ref[:, span] = part if piece == 0 else y_ref[:, span] + part


def before_gelu(mix_ref, cot_ref, g_hidden_ref):
    g_hidden_ref[...] = lax.dot_general(
        cot_ref[...], mix_ref[...], (((1,), (1,)), ((), ())), preferred_element_type=F32
    )


def forward(turned_ref, features_ref, y_ref, g_hidden_ref, cot_ref, hidden_ref, g_ref):
    mix_sum = None
    block = 512
    for start in range(0, TOKENS, block):
        span = slice(start, start + block)
        y = (y_ref[:, span] + piece_of_y(turned_ref, features_ref, 3, span)).T
        active, slope = gelu_parts(y)
        hidden = active.astype(BF16)
        hidden_ref[span, :] = hidden
        g_high, g_rest = halves(g_hidden_ref[span, :] * slope)
        g_ref[span, 0:WIDTH] = g_high
        g_ref[span, WIDTH:] = g_rest
        term = lax.dot_general(hidden, cot_ref[span, :], (((0,), (0,)), ((), ())), preferred_element_type=F32)
        mix_sum = term if mix_sum is None else mix_sum + term
    return mix_sum


def outputs(embed, features_ref, hidden_ref, mix_ref, out_ref):
    high, middle = halves(embed)
    rest = (embed - high.astype(F32) - middle.astype(F32)).astype(BF16)
    table = jnp.concatenate([high, middle, rest], axis=0)
    for start in range(0, TOKENS, 256):
        span = slice(start, start + 256)
        hot = features_ref[0:VOCAB, span]
        hot = jnp.concatenate([hot, hot, hot], axis=0)
        x = lax.dot_general(hot, table, (((0,), (0,)), ((), ())), preferred_element_type=F32)
        out_ref[span, :] = x + dot(hidden_ref[span, :], mix_ref[...])


def backward(passed, folded, kappa, embed, features_ref, g_ref, cot_ref, z_ref):
    def over_names(value):
        return jnp.sum(embed * value, axis=0, keepdims=True)

    def products(first, last):
        both = dot(features_ref[first:last, :], g_ref[...])
        z_ref[first:last, :] = both[:, :WIDTH] + both[:, WIDTH:]

    ends = {0: class_of(8, 0) * VOCAB, 8: class_of(11, 0) * VOCAB, 11: CLASSES * VOCAB}

    def z_of(level, ones):
        z = z_ref[block_of(level, ones), :]
        return z + z_ref[rest_of(level, ones), :] if ones in SPLIT.get(level, ()) else z

    begin = 0
    rows = []
    for level in range(LEVELS):
        if level in ends:
            products(begin, ends[level])
            begin = ends[level]
        if level == 0:
            z0 = z_ref[0:VOCAB, :]
            rows.append(over_names(z0))
            embed_sum = folded[0] * z0 + dot(features_ref[0:VOCAB, :], cot_ref[...])
            zero_sum = one_sum = jnp.zeros_like(z0)
        total = passed(level, 0) * z_of(level, 0)
        counted = jnp.zeros_like(total)
        for ones in range(1, level + 1):
            term = passed(level, ones) * z_of(level, ones)
            total = total + term
            counted = counted + float(ones) * term
        rows.append(over_names(total))
        embed_sum = embed_sum + kappa[level] * total
        one_sum = one_sum + kappa[level] * counted
        zero_sum = zero_sum + kappa[level] * (float(level) * total - counted)
    rows += [over_names(zero_sum), over_names(one_sum)]
    return jnp.concatenate(rows + [embed_sum], axis=0)


def layer_kernel(
    count, scale, ids_hbm, embed_hbm, low_hbm, high_hbm, levels_hbm, mix_hbm, cot_hbm,
    out_ref, whole, factors_ref,
    held, ids_sems, ones_ref, class_ref, tokens_ref, s7, s8, s9, s10, features_ref, weights_ref, turned_ref,
    y_ref, g_hidden_ref, hidden_ref, g_ref, z_ref, ids_ref, embed_ref, low_ref, high_ref, levels_ref, mix_ref, cot_ref, local_sem,
    mix_part, small_part, mix_in, small_in, second, third, sends, recvs,
):
    seq, batch = lax.axis_index("seq"), lax.axis_index("batch")
    x, y = lax.rem(seq, 4), lax.rem(lax.div(seq, 4), 4)
    core = lax.rem(batch, 2)
    z = lax.div(seq, 16) * 2 + lax.div(batch, 2)

    def along(order):
        return x + order * (y - x), y + order * (z - y), z + order * (x - z)

    def device(order, spots, core):
        a, b, c = spots
        x, y, z = a + order * (c - a), b + order * (a - b), c + order * (b - c)
        return lax.div(z, 2) * 16 + y * 4 + x, lax.rem(z, 2) * 2 + core

    def moved(spots, i, j, k):
        return lax.rem(spots[0] + i, 4), lax.rem(spots[1] + j, 4), lax.rem(spots[2] + k, 4)

    mine, theirs = along(core), along(1 - core)
    hops = lambda spot: sum(min(step, 4 - step) for step in spot)
    plane = sorted([(i, j) for i in range(4) for j in range(4)], key=hops, reverse=True)
    others = plane[:-1]
    own_peer = lambda i, j, k: device(core, moved(mine, i, j, k), core)
    their_peer = lambda i, j: device(1 - core, moved(theirs, i, j, 0), 1 - core)
    cross_peer = lambda i, j: device(core, moved(mine, i, j, 0), 1 - core)
    chunk_of = lambda core, spots: 16 * core + 4 * spots[0] + spots[1]

    barrier = pltpu.get_barrier_semaphore()

    def greet(peer):
        pl.semaphore_signal(barrier, inc=1, device_id=peer, device_id_type=MESH)

    for step in range(1, BACK + 1):
        greet((lax.rem(seq + count - step, count), batch))
    for i, j in others:
        greet(own_peer(i, j, 0))
    for k in range(1, 4):
        greet(own_peer(0, 0, k))
    for i, j in plane:
        greet(their_peer(i, j))
        if i:
            greet(cross_peer(i + core * (j - i), j + core * (i - j)))
    loads = [
        pltpu.make_async_copy(source, target, local_sem.at[place])
        for place, (source, target) in enumerate(
            [
                (ids_hbm, ids_ref),
                (embed_hbm, embed_ref),
                (low_hbm, low_ref),
                (high_hbm, high_ref),
                (levels_hbm, levels_ref),
                (mix_hbm, mix_ref),
                (cot_hbm, cot_ref),
            ]
        )
    ]
    for load in loads:
        load.start()
    pl.semaphore_wait(barrier, BACK + 46)

    def copy_to(source, target, sent, received, peer):
        copy = pltpu.make_async_remote_copy(
            src_ref=source, dst_ref=target, send_sem=sent, recv_sem=received, device_id=peer, device_id_type=MESH
        )
        copy.start()
        return copy

    def drain(ref, sem):
        pltpu.make_async_copy(ref, ref, sem).wait()

    arrivals = [(0, 1), (1, BACK)]
    for group, (first, last) in reversed(list(enumerate(arrivals))):
        for step in range(first, last):
            peer = lax.rem(seq + step + 1, count), batch
            copy_to(ids_hbm, held.at[step], ids_sems.at[2], ids_sems.at[group], peer)

    for load in loads:
        load.wait()
    embed = embed_ref[...]
    low, high, levels = rows_of(low_ref), rows_of(high_ref), rows_of(levels_ref)
    folded, kappa = level_factors(low, high, levels)
    passed = lag_weights(low)
    make_weights(passed, folded, kappa, embed, weights_ref)
    turned_ref[...] = weights_ref[...].T
    make_tables(ones_ref, class_ref)
    tokens_ref[0:VOCAB, LANES:] = jnp.zeros((VOCAB, LANES), BF16)
    features_ref[CLASSES * VOCAB :, :] = jnp.zeros((ROWS - CLASSES * VOCAB, TOKENS), BF16)
    before_gelu(mix_ref, cot_ref, g_hidden_ref)
    make_hot(tokens_ref, 8 * BACK, ids_ref[...])
    make_own(tokens_ref, class_ref, ones_ref, s7, s8, features_ref)
    parts_of_y(turned_ref, features_ref, y_ref, ((0, 256, 1024), (1, 512, 1024)))

    factors_ref[0:2, :] = low_ref[...]
    factors_ref[2:4, :] = high_ref[...]
    factors_ref[4:18, :] = levels_ref[...]
    for level in range(LEVELS + 1):
        factors_ref[18 + level : 19 + level, :] = folded[level]

    def receive(group):
        first, last = arrivals[group]
        drain(held.at[pl.ds(first, last - first)], ids_sems.at[group])
        for step in range(first, last):
            make_hot(tokens_ref, 8 * (BACK - 1 - step), jnp.where(seq > step, held[step], -1))

    receive(0)
    make_near(tokens_ref, class_ref, ones_ref, s7, s8, s9, features_ref)
    parts_of_y(turned_ref, features_ref, y_ref, ((0, 0, 256), (1, 0, 512), (2, 0, 1024)))
    receive(1)
    make_far(tokens_ref, ones_ref, s7, s8, s9, s10, features_ref)
    mix_sum = forward(turned_ref, features_ref, y_ref, g_hidden_ref, cot_ref, hidden_ref, g_ref)

    home = chunk_of(core, mine)

    def spread(phase, part, target):
        for slot, (i, j) in enumerate(plane):
            place = chunk_of(1 - core, moved(theirs, i, j, 0))
            copy_to(part.at[place], target.at[slot + 15], sends.at[phase], recvs.at[phase], their_peer(i, j))
            if (i, j) in others:
                place = chunk_of(core, moved(mine, i, j, 0))
                copy_to(part.at[place], target.at[slot], sends.at[phase], recvs.at[phase], own_peer(i, j, 0))

    for chunk in range(CHUNKS):
        mix_part[chunk] = scale * mix_sum[8 * chunk : 8 * chunk + 8]
    small = scale * backward(passed, folded, kappa, embed, features_ref, g_ref, cot_ref, z_ref)
    spread(0, mix_part, mix_in)
    for chunk in range(CHUNKS):
        small_part[chunk] = small[chunk : chunk + 1]
    spread(1, small_part, small_in)
    drain(mix_in, recvs.at[0])
    mixed = mix_part[home]
    for slot in range(CHUNKS - 1):
        mixed = mixed + mix_in[slot]
    for row in range(8):
        second[mine[2], row] = mixed[row : row + 1]
    drain(small_in, recvs.at[1])
    row = small_part[home]
    for slot in range(CHUNKS - 1):
        row = row + small_in[slot]
    second[mine[2], 8] = row
    spot = second.at[mine[2]]
    for k in (2, 1, 3):
        copy_to(spot, spot, sends.at[2], recvs.at[2], own_peer(0, 0, k))
    outputs(embed, features_ref, hidden_ref, mix_ref, out_ref)
    drain(second.at[pl.ds(0, 3)], recvs.at[2])
    third[...] = (second[0] + second[1]) + (second[2] + second[3])
    landing = whole.at[pl.ds(9 * home, 9)]
    for i, j in plane:
        copy_to(third, landing, sends.at[3], recvs.at[3], cross_peer(i, j))
        if (i, j) in others:
            copy_to(third, landing, sends.at[3], recvs.at[3], own_peer(i, j, 0))
    whole[pl.ds(9 * home, 9)] = third[...]
    drain(held, ids_sems.at[2])
    drain(mix_in, sends.at[0])
    drain(small_in, sends.at[1])
    drain(second.at[pl.ds(0, 3)], sends.at[2])
    gathered = whole.at[pl.ds(0, 9 * (CHUNKS - 1))]
    drain(gathered, recvs.at[3])
    drain(gathered, sends.at[3])


def layer(count, scale, ids, embed, low, high, levels, mix, cot):
    vmem = pl.BlockSpec(memory_space=pltpu.VMEM)
    far = pl.BlockSpec(memory_space=pltpu.HBM)
    arguments = tuple(
        pltpu.with_memory_space_constraint(array, pltpu.HBM) for array in (ids, embed, low, high, levels, mix, cot)
    )
    return pl.pallas_call(
        functools.partial(layer_kernel, count, scale),
        out_shape=(
            jax.ShapeDtypeStruct((TOKENS, WIDTH), F32),
            jax.ShapeDtypeStruct((9 * CHUNKS, 1, WIDTH), F32),
            jax.ShapeDtypeStruct((32, WIDTH), F32),
        ),
        in_specs=[far] * 7,
        out_specs=(vmem,) * 3,
        scratch_shapes=[
            pltpu.VMEM((BACK, 8, LANES), jnp.int32),
            pltpu.SemaphoreType.DMA((3,)),
            pltpu.VMEM((2 * LANES, 8 * LANES), BF16),
            pltpu.VMEM((2 * LANES, 29 * LANES), BF16),
            pltpu.VMEM((TILES * VOCAB, 2 * LANES), BF16),
            pltpu.VMEM((8 * VOCAB, TILES * LANES), BF16),
            pltpu.VMEM((9 * VOCAB, TILES * LANES), BF16),
            pltpu.VMEM((10 * VOCAB, TILES * LANES), BF16),
            pltpu.VMEM((11 * VOCAB, TILES * LANES), BF16),
            pltpu.VMEM((ROWS, TOKENS), BF16),
            pltpu.VMEM((WEIGHTS, 2 * WIDTH), BF16),
            pltpu.VMEM((2 * WIDTH, WEIGHTS), BF16),
            pltpu.VMEM((WIDTH, TOKENS), F32),
            pltpu.VMEM((TOKENS, WIDTH), F32),
            pltpu.VMEM((TOKENS, WIDTH), BF16),
            pltpu.VMEM((TOKENS, 2 * WIDTH), BF16),
            pltpu.VMEM((CLASSES * VOCAB, WIDTH), F32),
            *[pltpu.VMEM(array.shape, array.dtype) for array in arguments],
            pltpu.SemaphoreType.DMA((7,)),
            pltpu.VMEM((CHUNKS, 8, WIDTH), F32),
            pltpu.VMEM((CHUNKS, 1, WIDTH), F32),
            pltpu.VMEM((CHUNKS - 1, 8, WIDTH), F32),
            pltpu.VMEM((CHUNKS - 1, 1, WIDTH), F32),
            pltpu.VMEM((4, 9, 1, WIDTH), F32),
            pltpu.VMEM((9, 1, WIDTH), F32),
            pltpu.SemaphoreType.DMA((4,)),
            pltpu.SemaphoreType.DMA((4,)),
        ],
        compiler_params=pltpu.CompilerParams(
            collective_id=0, has_side_effects=True, vmem_limit_bytes=44 * 2**20
        ),
    )(*arguments)


def finish_kernel(
    out_ref, whole, factors_ref,
    out_hbm, filters_hbm, levels_hbm, mix_hbm, embed_hbm,
    filters_ref, grad_levels_ref, mix_ref, embed_ref, sems,
):
    stores = []

    def store(source, target):
        copy = pltpu.make_async_copy(source, target, sems.at[len(stores)])
        copy.start()
        stores.append(copy)

    store(out_ref, out_hbm)
    for chunk in range(CHUNKS):
        for row in range(8):
            mix_ref[8 * chunk + row : 8 * chunk + row + 1, :] = whole[9 * chunk + row]
    store(mix_ref, mix_hbm)
    summed = [whole[9 * chunk + 8] for chunk in range(CHUNKS)]
    for name in range(VOCAB):
        embed_ref[name : name + 1, :] = summed[16 + name]
    store(embed_ref, embed_hbm)
    shifted = summed[1:14]
    factors = rows_of(factors_ref)
    low, high, levels, folded = factors[0:2], factors[2:4], factors[4:18], factors[18:32]
    current = summed[0]
    low_zero, low_one = summed[14] / low[0], summed[15] / low[1]
    high_zero = high_one = jnp.zeros_like(current)
    for level in range(LEVELS):
        late = shifted[level]
        grad_levels_ref[level : level + 1, :] = high[0] * current + high[1] * late
        low_zero = low_zero + folded[level + 1] * current
        low_one = low_one + folded[level + 1] * late
        high_zero = high_zero + levels[level] * current
        high_one = high_one + levels[level] * late
        current = low[0] * current + low[1] * late
    grad_levels_ref[LEVELS : LEVELS + 1, :] = current
    filters_ref[0, 0:1, :] = low_zero
    filters_ref[0, 1:2, :] = low_one
    filters_ref[1, 0:1, :] = high_zero
    filters_ref[1, 1:2, :] = high_one
    store(filters_ref, filters_hbm)
    store(grad_levels_ref, levels_hbm)
    for copy in stores:
        copy.wait()


def finish(out, whole, factors):
    shapes = [(TOKENS, WIDTH), (2, 2, WIDTH), (LEVELS + 1, WIDTH), (WIDTH, WIDTH), (VOCAB, WIDTH)]
    return pl.pallas_call(
        finish_kernel,
        out_shape=tuple(jax.ShapeDtypeStruct(shape, F32) for shape in shapes),
        in_specs=[pl.BlockSpec(memory_space=pltpu.VMEM)] * 3,
        out_specs=(pl.BlockSpec(memory_space=pl.ANY),) * 5,
        scratch_shapes=[pltpu.VMEM(shape, F32) for shape in shapes[1:]] + [pltpu.SemaphoreType.DMA((5,))],
        compiler_params=pltpu.CompilerParams(vmem_limit_bytes=16 * 2**20),
    )(out, whole, factors)


def per_device(ids, embed, low_filter, high_filter, level_weights, mix, cotangent):
    count = lax.axis_size("seq")
    scale = 1.0 / math.sqrt(count * lax.axis_size("batch") * TOKENS)
    out, whole, factors = layer(
        count, scale, ids.reshape(8, LANES), embed, low_filter, high_filter, level_weights, mix, cotangent[0]
    )
    out, grad_filters, grad_levels, grad_mix, grad_embed = finish(out, whole, factors)
    return out[None], grad_filters, grad_levels, grad_mix, grad_embed


def solution(mesh):
    placed = (P("batch", "seq"), P(), P(), P(), P(), P(), P("batch", "seq", None))
    return jax.shard_map(
        per_device,
        mesh=mesh,
        in_specs=placed,
        out_specs=(P("batch", "seq", None), P(), P(), P(), P()),
        check_vma=False,
    )
```

```python
import functools
import math

import jax
import jax.numpy as jnp
from jax import lax
from jax.experimental import pallas as pl
from jax.experimental.pallas import tpu as pltpu
from jax.sharding import PartitionSpec as P

MESH = pl.DeviceIdType.MESH
F32, BF16 = jnp.float32, jnp.bfloat16
LEVELS = 13
VOCAB = 16
WIDTH = 256
LANES = 128
TOKENS = 1024
BACK = 8
TILES = (BACK + 1) * TOKENS // LANES
SPLIT = {11: range(4, 8), 12: range(4, 9)}
CLASSES = 101
ROWS = 104 * VOCAB
NEAR = 56 * VOCAB
PIECES = ((0, 37 * VOCAB), (37 * VOCAB, 46 * VOCAB), (46 * VOCAB, NEAR), (NEAR, ROWS))
STARTS = (0, 640, 896, 1152)
WEIGHTS = STARTS[3] + ROWS - NEAR
CHUNKS = 32


def class_of(level, ones):
    return 1 + level * (level + 1) // 2 + ones


def block_of(level, ones):
    return slice(class_of(level, ones) * VOCAB, (class_of(level, ones) + 1) * VOCAB)


def rest_of(level, ones):
    place = 92 + 4 * (level - 11) + ones - 4
    return slice(place * VOCAB, (place + 1) * VOCAB)


def dot(a, b):
    return jnp.dot(a, b, preferred_element_type=F32)


def halves(value):
    high = value.astype(BF16)
    return high, (value - high.astype(F32)).astype(BF16)


def level_factors(low, high, weights):
    folded = [None] * (LEVELS + 1)
    kappa = [None] * LEVELS
    folded[LEVELS] = weights[LEVELS]
    for level in range(LEVELS - 1, -1, -1):
        kappa[level] = weights[level] * high[1] + low[1] * folded[level + 1]
        folded[level] = weights[level] * high[0] + low[0] * folded[level + 1]
    return folded, kappa


def rows_of(ref):
    return [ref[row : row + 1, :] for row in range(ref.shape[0])]


def lag_weights(low):
    chains = []
    for row in low:
        chain = [jnp.ones_like(row)]
        for _ in range(LEVELS - 1):
            chain.append(chain[-1] * row)
        chains.append(chain)
    return lambda level, ones: chains[0][level - ones] * chains[1][ones]


def make_weights(passed, folded, kappa, embed, weights_ref):
    weights_ref[...] = jnp.zeros_like(weights_ref)

    def put(rows, factor):
        shift = next(start - piece[0] for piece, start in zip(PIECES, STARTS) if rows.start < piece[1])
        rows = slice(rows.start + shift, rows.stop + shift)
        high, rest = halves(factor * embed)
        weights_ref[rows, 0:WIDTH] = high
        weights_ref[rows, WIDTH:] = rest

    put(slice(0, VOCAB), folded[0])
    for level in range(LEVELS):
        for ones in range(level + 1):
            put(block_of(level, ones), kappa[level] * passed(level, ones))
            if ones in SPLIT.get(level, ()):
                put(rest_of(level, ones), kappa[level] * passed(level, ones))


def where_is(table, value):
    return jnp.where(table == value, 1.0, 0.0).astype(BF16)


def make_tables(ones_ref, class_ref):
    place = lax.broadcasted_iota(jnp.int32, (2 * LANES, LANES), 0)
    lag = lax.broadcasted_iota(jnp.int32, (2 * LANES, LANES), 1) - place
    lag = jnp.where(place >= LANES, lag + 2 * LANES, lag)
    inside = (lag >= 0) & (lag < LANES)
    ones = jnp.zeros_like(lag)
    offset = jnp.zeros_like(lag)
    for bit in range(7):
        ones = ones + ((lag >> bit) & 1)
        offset = offset + jnp.where(lag >= 2**bit, bit, 0)
    klass = jnp.where(inside, jnp.where(lag == 0, 0, offset + ones), -1)
    ones = jnp.where(inside, ones, -1)
    for value in range(8):
        ones_ref[:, value * LANES : (value + 1) * LANES] = where_is(ones, value)
    for value in range(29):
        class_ref[:, value * LANES : (value + 1) * LANES] = where_is(klass, value)


def make_hot(tokens_ref, first, ids):
    names = lax.broadcasted_iota(jnp.int32, (VOCAB, LANES), 0)
    for row in range(8):
        tile = first + row
        hot = where_is(names, jnp.broadcast_to(ids[row : row + 1, :], (VOCAB, LANES)))
        tokens_ref[tile * VOCAB : (tile + 1) * VOCAB, 0:LANES] = hot
        if tile + 1 < TILES:
            tokens_ref[(tile + 1) * VOCAB : (tile + 2) * VOCAB, LANES:] = hot


def put_counts(result, s7, first, last, begin):
    for tile in range(first, last):
        for place in range(4):
            value = begin + place
            s7[value * VOCAB : (value + 1) * VOCAB, tile * LANES : (tile + 1) * LANES] = result[
                (tile - first) * VOCAB : (tile - first + 1) * VOCAB, place * LANES : (place + 1) * LANES
            ]


def count_tiles(tokens_ref, ones_ref, s7, first, last):
    for half in range(2):
        table = ones_ref[:, 4 * half * LANES : 4 * (half + 1) * LANES]
        result = dot(tokens_ref[first * VOCAB : last * VOCAB, :], table).astype(BF16)
        put_counts(result, s7, first, last, 4 * half)


def widened(source, level, ones, first, last):
    begin, end, span = first * LANES, last * LANES, 2**level
    total = None
    if 0 <= ones <= level:
        total = source[ones * VOCAB : (ones + 1) * VOCAB, begin:end]
    if 1 <= ones <= level + 1:
        late = source[(ones - 1) * VOCAB : ones * VOCAB, begin - span : end - span]
        total = late if total is None else total + late
    return total


def widen(source, target, level, first, last):
    for ones in range(level + 2):
        target[ones * VOCAB : (ones + 1) * VOCAB, first * LANES : last * LANES] = widened(
            source, level, ones, first, last
        )


def place_level(source, level, features_ref):
    rows = slice(class_of(level, 0) * VOCAB, class_of(level + 1, 0) * VOCAB)
    begin = BACK * TOKENS - 2**level
    features_ref[rows, :] = source[:, begin : begin + TOKENS]


def count_classes(tokens_ref, class_ref, features_ref, first, last):
    tokens = tokens_ref[first * VOCAB : last * VOCAB, :]
    for begin in range(0, 29, 8):
        members = range(begin, min(begin + 8, 29))
        result = dot(tokens, class_ref[:, begin * LANES : (begin + len(members)) * LANES]).astype(BF16)
        for tile in range(first, last):
            place = (tile - 8 * BACK) * LANES
            for half, member in enumerate(members):
                features_ref[member * VOCAB : (member + 1) * VOCAB, place : place + LANES] = result[
                    (tile - first) * VOCAB : (tile - first + 1) * VOCAB, half * LANES : (half + 1) * LANES
                ]


def place_tiles(source, level, features_ref, first, last):
    rows = slice(class_of(level, 0) * VOCAB, class_of(level + 1, 0) * VOCAB)
    begin = BACK * TOKENS - 2**level
    features_ref[rows, first * LANES : last * LANES] = source[:, begin + first * LANES : begin + last * LANES]


def make_own(tokens_ref, class_ref, ones_ref, s7, s8, features_ref):
    count_classes(tokens_ref, class_ref, features_ref, 65, 72)
    count_tiles(tokens_ref, ones_ref, s7, 65, 71)
    widen(s7, s8, 7, 66, 70)
    place_tiles(s7, 7, features_ref, 2, 8)
    place_tiles(s8, 8, features_ref, 4, 8)


def make_near(tokens_ref, class_ref, ones_ref, s7, s8, s9, features_ref):
    count_classes(tokens_ref, class_ref, features_ref, 64, 65)
    count_tiles(tokens_ref, ones_ref, s7, 57, 65)
    widen(s7, s8, 7, 58, 66)
    widen(s8, s9, 8, 60, 68)
    place_tiles(s7, 7, features_ref, 0, 2)
    place_tiles(s8, 8, features_ref, 0, 4)
    place_level(s9, 9, features_ref)


def put_sum(features_ref, level, ones, terms):
    terms = [term for term in terms if term is not None]
    if ones in SPLIT[level]:
        total = sum(term.astype(F32) for term in terms)
        high, rest = halves(total)
        features_ref[block_of(level, ones), :] = high
        features_ref[rest_of(level, ones), :] = rest
    else:
        features_ref[block_of(level, ones), :] = sum(terms[1:], terms[0])


def make_far(tokens_ref, ones_ref, s7, s8, s9, s10, features_ref):
    count_tiles(tokens_ref, ones_ref, s7, 1, 57)
    widen(s7, s8, 7, 2, 58)
    widen(s8, s9, 8, 4, 60)
    widen(s9, s10, 9, 8, 64)
    place_level(s10, 10, features_ref)

    def shard(back, ones):
        first = (BACK - back) * 8
        return s10[ones * VOCAB : (ones + 1) * VOCAB, first * LANES : (first + 8) * LANES] if 0 <= ones <= 10 else None

    for ones in range(12):
        put_sum(features_ref, 11, ones, [shard(2, ones), shard(3, ones - 1)])
    for ones in range(13):
        put_sum(
            features_ref, 12, ones, [shard(4, ones), shard(5, ones - 1), shard(6, ones - 1), shard(7, ones - 2)]
        )


def gelu_parts(y):
    root = math.sqrt(2.0 / math.pi)
    square = y * y
    bend = jnp.tanh(root * (y + 0.044715 * square * y))
    half = 0.5 * (1.0 + bend)
    slope = half + 0.5 * y * (1.0 - bend * bend) * (root * (1.0 + 3 * 0.044715 * square))
    return y * half, slope


def piece_of_y(turned_ref, features_ref, piece, span):
    (first, last), start = PIECES[piece], STARTS[piece]
    both = dot(turned_ref[:, start : start + last - first], features_ref[first:last, span])
    return both[:WIDTH] + both[WIDTH:]


def parts_of_y(turned_ref, features_ref, y_ref, wanted):
    for piece, first, last in wanted:
        span = slice(first, last)
        part = piece_of_y(turned_ref, features_ref, piece, span)
        y_ref[:, span] = part if piece == 0 else y_ref[:, span] + part


def before_gelu(mix_ref, cot_ref, g_hidden_ref):
    g_hidden_ref[...] = lax.dot_general(
        cot_ref[...], mix_ref[...], (((1,), (1,)), ((), ())), preferred_element_type=F32
    )


def forward(turned_ref, features_ref, y_ref, g_hidden_ref, cot_ref, hidden_ref, g_ref):
    mix_sum = None
    block = 512
    for start in range(0, TOKENS, block):
        span = slice(start, start + block)
        y = (y_ref[:, span] + piece_of_y(turned_ref, features_ref, 3, span)).T
        active, slope = gelu_parts(y)
        hidden = active.astype(BF16)
        hidden_ref[span, :] = hidden
        g_high, g_rest = halves(g_hidden_ref[span, :] * slope)
        g_ref[span, 0:WIDTH] = g_high
        g_ref[span, WIDTH:] = g_rest
        term = lax.dot_general(hidden, cot_ref[span, :], (((0,), (0,)), ((), ())), preferred_element_type=F32)
        mix_sum = term if mix_sum is None else mix_sum + term
    return mix_sum


def outputs(embed, features_ref, hidden_ref, mix_ref, out_ref):
    high, middle = halves(embed)
    rest = (embed - high.astype(F32) - middle.astype(F32)).astype(BF16)
    table = jnp.concatenate([high, middle, rest], axis=0)
    for start in range(0, TOKENS, 256):
        span = slice(start, start + 256)
        hot = features_ref[0:VOCAB, span]
        hot = jnp.concatenate([hot, hot, hot], axis=0)
        x = lax.dot_general(hot, table, (((0,), (0,)), ((), ())), preferred_element_type=F32)
        out_ref[span, :] = x + dot(hidden_ref[span, :], mix_ref[...])


def backward(passed, folded, kappa, embed, features_ref, g_ref, cot_ref, z_ref):
    def over_names(value):
        return jnp.sum(embed * value, axis=0, keepdims=True)

    def products(first, last):
        both = dot(features_ref[first:last, :], g_ref[...])
        z_ref[first:last, :] = both[:, :WIDTH] + both[:, WIDTH:]

    ends = {0: class_of(8, 0) * VOCAB, 8: class_of(11, 0) * VOCAB, 11: CLASSES * VOCAB}

    def z_of(level, ones):
        z = z_ref[block_of(level, ones), :]
        return z + z_ref[rest_of(level, ones), :] if ones in SPLIT.get(level, ()) else z

    begin = 0
    rows = []
    for level in range(LEVELS):
        if level in ends:
            products(begin, ends[level])
            begin = ends[level]
        if level == 0:
            z0 = z_ref[0:VOCAB, :]
            rows.append(over_names(z0))
            embed_sum = folded[0] * z0 + dot(features_ref[0:VOCAB, :], cot_ref[...])
            zero_sum = one_sum = jnp.zeros_like(z0)
        total = passed(level, 0) * z_of(level, 0)
        counted = jnp.zeros_like(total)
        for ones in range(1, level + 1):
            term = passed(level, ones) * z_of(level, ones)
            total = total + term
            counted = counted + float(ones) * term
        rows.append(over_names(total))
        embed_sum = embed_sum + kappa[level] * total
        one_sum = one_sum + kappa[level] * counted
        zero_sum = zero_sum + kappa[level] * (float(level) * total - counted)
    rows += [over_names(zero_sum), over_names(one_sum)]
    return jnp.concatenate(rows + [embed_sum], axis=0)


def layer_kernel(
    count, scale, ids_hbm, embed_hbm, low_hbm, high_hbm, levels_hbm, mix_hbm, cot_hbm,
    out_ref, whole, factors_ref,
    held, ids_sems, ones_ref, class_ref, tokens_ref, s7, s8, s9, s10, features_ref, weights_ref, turned_ref,
    y_ref, g_hidden_ref, hidden_ref, g_ref, z_ref, ids_ref, embed_ref, low_ref, high_ref, levels_ref, mix_ref, cot_ref, local_sem,
    mix_part, small_part, mix_in, small_in, second, third, sends, recvs,
):
    seq, batch = lax.axis_index("seq"), lax.axis_index("batch")
    x, y = lax.rem(seq, 4), lax.rem(lax.div(seq, 4), 4)
    core = lax.rem(batch, 2)
    z = lax.div(seq, 16) * 2 + lax.div(batch, 2)

    def along(order):
        return x + order * (y - x), y + order * (z - y), z + order * (x - z)

    def device(order, spots, core):
        a, b, c = spots
        x, y, z = a + order * (c - a), b + order * (a - b), c + order * (b - c)
        return lax.div(z, 2) * 16 + y * 4 + x, lax.rem(z, 2) * 2 + core

    def moved(spots, i, j, k):
        return lax.rem(spots[0] + i, 4), lax.rem(spots[1] + j, 4), lax.rem(spots[2] + k, 4)

    mine, theirs = along(core), along(1 - core)
    hops = lambda spot: sum(min(step, 4 - step) for step in spot)
    plane = sorted([(i, j) for i in range(4) for j in range(4)], key=hops, reverse=True)
    others = plane[:-1]
    own_peer = lambda i, j, k: device(core, moved(mine, i, j, k), core)
    their_peer = lambda i, j: device(1 - core, moved(theirs, i, j, 0), 1 - core)
    cross_peer = lambda i, j: device(core, moved(mine, i, j, 0), 1 - core)
    chunk_of = lambda core, spots: 16 * core + 4 * spots[0] + spots[1]

    barrier = pltpu.get_barrier_semaphore()

    def greet(peer):
        pl.semaphore_signal(barrier, inc=1, device_id=peer, device_id_type=MESH)

    for step in range(1, BACK + 1):
        greet((lax.rem(seq + count - step, count), batch))
    for i, j in others:
        greet(own_peer(i, j, 0))
    for k in range(1, 4):
        greet(own_peer(0, 0, k))
    for i, j in plane:
        greet(their_peer(i, j))
        if i:
            greet(cross_peer(i + core * (j - i), j + core * (i - j)))
    loads = [
        pltpu.make_async_copy(source, target, local_sem.at[place])
        for place, (source, target) in enumerate(
            [
                (ids_hbm, ids_ref),
                (embed_hbm, embed_ref),
                (low_hbm, low_ref),
                (high_hbm, high_ref),
                (levels_hbm, levels_ref),
                (mix_hbm, mix_ref),
                (cot_hbm, cot_ref),
            ]
        )
    ]
    for load in loads:
        load.start()
    pl.semaphore_wait(barrier, BACK + 46)

    def copy_to(source, target, sent, received, peer):
        copy = pltpu.make_async_remote_copy(
            src_ref=source, dst_ref=target, send_sem=sent, recv_sem=received, device_id=peer, device_id_type=MESH
        )
        copy.start()
        return copy

    def drain(ref, sem):
        pltpu.make_async_copy(ref, ref, sem).wait()

    arrivals = [(0, 1), (1, BACK)]
    for group, (first, last) in reversed(list(enumerate(arrivals))):
        for step in range(first, last):
            peer = lax.rem(seq + step + 1, count), batch
            copy_to(ids_hbm, held.at[step], ids_sems.at[2], ids_sems.at[group], peer)

    for load in loads:
        load.wait()
    embed = embed_ref[...]
    low, high, levels = rows_of(low_ref), rows_of(high_ref), rows_of(levels_ref)
    folded, kappa = level_factors(low, high, levels)
    passed = lag_weights(low)
    make_weights(passed, folded, kappa, embed, weights_ref)
    turned_ref[...] = weights_ref[...].T
    make_tables(ones_ref, class_ref)
    tokens_ref[0:VOCAB, LANES:] = jnp.zeros((VOCAB, LANES), BF16)
    features_ref[CLASSES * VOCAB :, :] = jnp.zeros((ROWS - CLASSES * VOCAB, TOKENS), BF16)
    before_gelu(mix_ref, cot_ref, g_hidden_ref)
    make_hot(tokens_ref, 8 * BACK, ids_ref[...])
    make_own(tokens_ref, class_ref, ones_ref, s7, s8, features_ref)
    parts_of_y(turned_ref, features_ref, y_ref, ((0, 256, 1024), (1, 512, 1024)))

    factors_ref[0:2, :] = low_ref[...]
    factors_ref[2:4, :] = high_ref[...]
    factors_ref[4:18, :] = levels_ref[...]
    for level in range(LEVELS + 1):
        factors_ref[18 + level : 19 + level, :] = folded[level]

    def receive(group):
        first, last = arrivals[group]
        drain(held.at[pl.ds(first, last - first)], ids_sems.at[group])
        for step in range(first, last):
            make_hot(tokens_ref, 8 * (BACK - 1 - step), jnp.where(seq > step, held[step], -1))

    receive(0)
    make_near(tokens_ref, class_ref, ones_ref, s7, s8, s9, features_ref)
    parts_of_y(turned_ref, features_ref, y_ref, ((0, 0, 256), (1, 0, 512), (2, 0, 1024)))
    receive(1)
    make_far(tokens_ref, ones_ref, s7, s8, s9, s10, features_ref)
    mix_sum = forward(turned_ref, features_ref, y_ref, g_hidden_ref, cot_ref, hidden_ref, g_ref)

    home = chunk_of(core, mine)

    def spread(phase, part, target):
        for slot, (i, j) in enumerate(plane):
            place = chunk_of(1 - core, moved(theirs, i, j, 0))
            copy_to(part.at[place], target.at[slot + 15], sends.at[phase], recvs.at[phase], their_peer(i, j))
            if (i, j) in others:
                place = chunk_of(core, moved(mine, i, j, 0))
                copy_to(part.at[place], target.at[slot], sends.at[phase], recvs.at[phase], own_peer(i, j, 0))

    for chunk in range(CHUNKS):
        mix_part[chunk] = scale * mix_sum[8 * chunk : 8 * chunk + 8]
    small = scale * backward(passed, folded, kappa, embed, features_ref, g_ref, cot_ref, z_ref)
    spread(0, mix_part, mix_in)
    for chunk in range(CHUNKS):
        small_part[chunk] = small[chunk : chunk + 1]
    spread(1, small_part, small_in)
    outputs(embed, features_ref, hidden_ref, mix_ref, out_ref)
    drain(mix_in, recvs.at[0])
    mixed = mix_part[home]
    for slot in range(CHUNKS - 1):
        mixed = mixed + mix_in[slot]
    for row in range(8):
        second[mine[2], row] = mixed[row : row + 1]
    drain(small_in, recvs.at[1])
    row = small_part[home]
    for slot in range(CHUNKS - 1):
        row = row + small_in[slot]
    second[mine[2], 8] = row
    spot = second.at[mine[2]]
    for k in (2, 1, 3):
        copy_to(spot, spot, sends.at[2], recvs.at[2], own_peer(0, 0, k))
    drain(second.at[pl.ds(0, 3)], recvs.at[2])
    third[...] = (second[0] + second[1]) + (second[2] + second[3])
    landing = whole.at[pl.ds(9 * home, 9)]
    for i, j in plane:
        copy_to(third, landing, sends.at[3], recvs.at[3], cross_peer(i, j))
        if (i, j) in others:
            copy_to(third, landing, sends.at[3], recvs.at[3], own_peer(i, j, 0))
    whole[pl.ds(9 * home, 9)] = third[...]
    drain(held, ids_sems.at[2])
    drain(mix_in, sends.at[0])
    drain(small_in, sends.at[1])
    drain(second.at[pl.ds(0, 3)], sends.at[2])
    gathered = whole.at[pl.ds(0, 9 * (CHUNKS - 1))]
    drain(gathered, recvs.at[3])
    drain(gathered, sends.at[3])


def layer(count, scale, ids, embed, low, high, levels, mix, cot):
    vmem = pl.BlockSpec(memory_space=pltpu.VMEM)
    far = pl.BlockSpec(memory_space=pltpu.HBM)
    arguments = tuple(
        pltpu.with_memory_space_constraint(array, pltpu.HBM) for array in (ids, embed, low, high, levels, mix, cot)
    )
    return pl.pallas_call(
        functools.partial(layer_kernel, count, scale),
        out_shape=(
            jax.ShapeDtypeStruct((TOKENS, WIDTH), F32),
            jax.ShapeDtypeStruct((9 * CHUNKS, 1, WIDTH), F32),
            jax.ShapeDtypeStruct((32, WIDTH), F32),
        ),
        in_specs=[far] * 7,
        out_specs=(vmem,) * 3,
        scratch_shapes=[
            pltpu.VMEM((BACK, 8, LANES), jnp.int32),
            pltpu.SemaphoreType.DMA((3,)),
            pltpu.VMEM((2 * LANES, 8 * LANES), BF16),
            pltpu.VMEM((2 * LANES, 29 * LANES), BF16),
            pltpu.VMEM((TILES * VOCAB, 2 * LANES), BF16),
            pltpu.VMEM((8 * VOCAB, TILES * LANES), BF16),
            pltpu.VMEM((9 * VOCAB, TILES * LANES), BF16),
            pltpu.VMEM((10 * VOCAB, TILES * LANES), BF16),
            pltpu.VMEM((11 * VOCAB, TILES * LANES), BF16),
            pltpu.VMEM((ROWS, TOKENS), BF16),
            pltpu.VMEM((WEIGHTS, 2 * WIDTH), BF16),
            pltpu.VMEM((2 * WIDTH, WEIGHTS), BF16),
            pltpu.VMEM((WIDTH, TOKENS), F32),
            pltpu.VMEM((TOKENS, WIDTH), F32),
            pltpu.VMEM((TOKENS, WIDTH), BF16),
            pltpu.VMEM((TOKENS, 2 * WIDTH), BF16),
            pltpu.VMEM((CLASSES * VOCAB, WIDTH), F32),
            *[pltpu.VMEM(array.shape, array.dtype) for array in arguments],
            pltpu.SemaphoreType.DMA((7,)),
            pltpu.VMEM((CHUNKS, 8, WIDTH), F32),
            pltpu.VMEM((CHUNKS, 1, WIDTH), F32),
            pltpu.VMEM((CHUNKS - 1, 8, WIDTH), F32),
            pltpu.VMEM((CHUNKS - 1, 1, WIDTH), F32),
            pltpu.VMEM((4, 9, 1, WIDTH), F32),
            pltpu.VMEM((9, 1, WIDTH), F32),
            pltpu.SemaphoreType.DMA((4,)),
            pltpu.SemaphoreType.DMA((4,)),
        ],
        compiler_params=pltpu.CompilerParams(
            collective_id=0, has_side_effects=True, vmem_limit_bytes=44 * 2**20
        ),
    )(*arguments)


def finish_kernel(
    out_ref, whole, factors_ref,
    out_hbm, filters_hbm, levels_hbm, mix_hbm, embed_hbm,
    filters_ref, grad_levels_ref, mix_ref, embed_ref, sems,
):
    stores = []

    def store(source, target):
        copy = pltpu.make_async_copy(source, target, sems.at[len(stores)])
        copy.start()
        stores.append(copy)

    store(out_ref, out_hbm)
    for chunk in range(CHUNKS):
        for row in range(8):
            mix_ref[8 * chunk + row : 8 * chunk + row + 1, :] = whole[9 * chunk + row]
    store(mix_ref, mix_hbm)
    summed = [whole[9 * chunk + 8] for chunk in range(CHUNKS)]
    for name in range(VOCAB):
        embed_ref[name : name + 1, :] = summed[16 + name]
    store(embed_ref, embed_hbm)
    shifted = summed[1:14]
    factors = rows_of(factors_ref)
    low, high, levels, folded = factors[0:2], factors[2:4], factors[4:18], factors[18:32]
    current = summed[0]
    low_zero, low_one = summed[14] / low[0], summed[15] / low[1]
    high_zero = high_one = jnp.zeros_like(current)
    for level in range(LEVELS):
        late = shifted[level]
        grad_levels_ref[level : level + 1, :] = high[0] * current + high[1] * late
        low_zero = low_zero + folded[level + 1] * current
        low_one = low_one + folded[level + 1] * late
        high_zero = high_zero + levels[level] * current
        high_one = high_one + levels[level] * late
        current = low[0] * current + low[1] * late
    grad_levels_ref[LEVELS : LEVELS + 1, :] = current
    filters_ref[0, 0:1, :] = low_zero
    filters_ref[0, 1:2, :] = low_one
    filters_ref[1, 0:1, :] = high_zero
    filters_ref[1, 1:2, :] = high_one
    store(filters_ref, filters_hbm)
    store(grad_levels_ref, levels_hbm)
    for copy in stores:
        copy.wait()


def finish(out, whole, factors):
    shapes = [(TOKENS, WIDTH), (2, 2, WIDTH), (LEVELS + 1, WIDTH), (WIDTH, WIDTH), (VOCAB, WIDTH)]
    return pl.pallas_call(
        finish_kernel,
        out_shape=tuple(jax.ShapeDtypeStruct(shape, F32) for shape in shapes),
        in_specs=[pl.BlockSpec(memory_space=pltpu.VMEM)] * 3,
        out_specs=(pl.BlockSpec(memory_space=pl.ANY),) * 5,
        scratch_shapes=[pltpu.VMEM(shape, F32) for shape in shapes[1:]] + [pltpu.SemaphoreType.DMA((5,))],
        compiler_params=pltpu.CompilerParams(vmem_limit_bytes=16 * 2**20),
    )(out, whole, factors)


def per_device(ids, embed, low_filter, high_filter, level_weights, mix, cotangent):
    count = lax.axis_size("seq")
    scale = 1.0 / math.sqrt(count * lax.axis_size("batch") * TOKENS)
    out, whole, factors = layer(
        count, scale, ids.reshape(8, LANES), embed, low_filter, high_filter, level_weights, mix, cotangent[0]
    )
    out, grad_filters, grad_levels, grad_mix, grad_embed = finish(out, whole, factors)
    return out[None], grad_filters, grad_levels, grad_mix, grad_embed


def solution(mesh):
    placed = (P("batch", "seq"), P(), P(), P(), P(), P(), P("batch", "seq", None))
    return jax.shard_map(
        per_device,
        mesh=mesh,
        in_specs=placed,
        out_specs=(P("batch", "seq", None), P(), P(), P(), P()),
        check_vma=False,
    )
```

```python
import functools
import math

import jax
import jax.numpy as jnp
from jax import lax
from jax.experimental import pallas as pl
from jax.experimental.pallas import tpu as pltpu
from jax.sharding import PartitionSpec as P

MESH = pl.DeviceIdType.MESH
F32, BF16 = jnp.float32, jnp.bfloat16
LEVELS = 13
VOCAB = 16
WIDTH = 256
LANES = 128
TOKENS = 1024
BACK = 8
TILES = (BACK + 1) * TOKENS // LANES
SPLIT = {11: range(4, 8), 12: range(4, 9)}
CLASSES = 101
ROWS = 104 * VOCAB
NEAR = 56 * VOCAB
PIECES = ((0, 37 * VOCAB), (37 * VOCAB, 46 * VOCAB), (46 * VOCAB, NEAR), (NEAR, ROWS))
STARTS = (0, 640, 896, 1152)
WEIGHTS = STARTS[3] + ROWS - NEAR
CHUNKS = 32


def class_of(level, ones):
    return 1 + level * (level + 1) // 2 + ones


def block_of(level, ones):
    return slice(class_of(level, ones) * VOCAB, (class_of(level, ones) + 1) * VOCAB)


def rest_of(level, ones):
    place = 92 + 4 * (level - 11) + ones - 4
    return slice(place * VOCAB, (place + 1) * VOCAB)


def dot(a, b):
    return jnp.dot(a, b, preferred_element_type=F32)


def halves(value):
    high = value.astype(BF16)
    return high, (value - high.astype(F32)).astype(BF16)


def level_factors(low, high, weights):
    folded = [None] * (LEVELS + 1)
    kappa = [None] * LEVELS
    folded[LEVELS] = weights[LEVELS]
    for level in range(LEVELS - 1, -1, -1):
        kappa[level] = weights[level] * high[1] + low[1] * folded[level + 1]
        folded[level] = weights[level] * high[0] + low[0] * folded[level + 1]
    return folded, kappa


def rows_of(ref):
    return [ref[row : row + 1, :] for row in range(ref.shape[0])]


def lag_weights(low):
    chains = []
    for row in low:
        chain = [jnp.ones_like(row)]
        for _ in range(LEVELS - 1):
            chain.append(chain[-1] * row)
        chains.append(chain)
    return lambda level, ones: chains[0][level - ones] * chains[1][ones]


def make_weights(passed, folded, kappa, embed, weights_ref):
    weights_ref[...] = jnp.zeros_like(weights_ref)

    def put(rows, factor):
        shift = next(start - piece[0] for piece, start in zip(PIECES, STARTS) if rows.start < piece[1])
        rows = slice(rows.start + shift, rows.stop + shift)
        high, rest = halves(factor * embed)
        weights_ref[rows, 0:WIDTH] = high
        weights_ref[rows, WIDTH:] = rest

    put(slice(0, VOCAB), folded[0])
    for level in range(LEVELS):
        for ones in range(level + 1):
            put(block_of(level, ones), kappa[level] * passed(level, ones))
            if ones in SPLIT.get(level, ()):
                put(rest_of(level, ones), kappa[level] * passed(level, ones))


def where_is(table, value):
    return jnp.where(table == value, 1.0, 0.0).astype(BF16)


def make_tables(ones_ref, class_ref):
    place = lax.broadcasted_iota(jnp.int32, (2 * LANES, LANES), 0)
    lag = lax.broadcasted_iota(jnp.int32, (2 * LANES, LANES), 1) - place
    lag = jnp.where(place >= LANES, lag + 2 * LANES, lag)
    inside = (lag >= 0) & (lag < LANES)
    ones = jnp.zeros_like(lag)
    offset = jnp.zeros_like(lag)
    for bit in range(7):
        ones = ones + ((lag >> bit) & 1)
        offset = offset + jnp.where(lag >= 2**bit, bit, 0)
    klass = jnp.where(inside, jnp.where(lag == 0, 0, offset + ones), -1)
    ones = jnp.where(inside, ones, -1)
    for value in range(8):
        ones_ref[:, value * LANES : (value + 1) * LANES] = where_is(ones, value)
    for value in range(29):
        class_ref[:, value * LANES : (value + 1) * LANES] = where_is(klass, value)


def make_hot(tokens_ref, first, ids):
    names = lax.broadcasted_iota(jnp.int32, (VOCAB, LANES), 0)
    for row in range(8):
        tile = first + row
        hot = where_is(names, jnp.broadcast_to(ids[row : row + 1, :], (VOCAB, LANES)))
        tokens_ref[tile * VOCAB : (tile + 1) * VOCAB, 0:LANES] = hot
        if tile + 1 < TILES:
            tokens_ref[(tile + 1) * VOCAB : (tile + 2) * VOCAB, LANES:] = hot


def put_counts(result, s7, first, last, pair):
    for tile in range(first, last):
        for half in range(2):
            value = 2 * pair + half
            s7[value * VOCAB : (value + 1) * VOCAB, tile * LANES : (tile + 1) * LANES] = result[
                (tile - first) * VOCAB : (tile - first + 1) * VOCAB, half * LANES : (half + 1) * LANES
            ]


def count_tiles(tokens_ref, ones_ref, s7, first, last):
    for pair in range(4):
        table = ones_ref[:, 2 * pair * LANES : 2 * (pair + 1) * LANES]
        result = dot(tokens_ref[first * VOCAB : last * VOCAB, :], table).astype(BF16)
        put_counts(result, s7, first, last, pair)


def widened(source, level, ones, first, last):
    begin, end, span = first * LANES, last * LANES, 2**level
    total = None
    if 0 <= ones <= level:
        total = source[ones * VOCAB : (ones + 1) * VOCAB, begin:end]
    if 1 <= ones <= level + 1:
        late = source[(ones - 1) * VOCAB : ones * VOCAB, begin - span : end - span]
        total = late if total is None else total + late
    return total


def widen(source, target, level, first, last):
    for ones in range(level + 2):
        target[ones * VOCAB : (ones + 1) * VOCAB, first * LANES : last * LANES] = widened(
            source, level, ones, first, last
        )


def place_level(source, level, features_ref):
    rows = slice(class_of(level, 0) * VOCAB, class_of(level + 1, 0) * VOCAB)
    begin = BACK * TOKENS - 2**level
    features_ref[rows, :] = source[:, begin : begin + TOKENS]


def count_classes(tokens_ref, class_ref, features_ref, first, last):
    tokens = tokens_ref[first * VOCAB : last * VOCAB, :]
    for begin in range(0, 29, 2):
        members = range(begin, min(begin + 2, 29))
        result = dot(tokens, class_ref[:, begin * LANES : (begin + len(members)) * LANES]).astype(BF16)
        for tile in range(first, last):
            place = (tile - 8 * BACK) * LANES
            for half, member in enumerate(members):
                features_ref[member * VOCAB : (member + 1) * VOCAB, place : place + LANES] = result[
                    (tile - first) * VOCAB : (tile - first + 1) * VOCAB, half * LANES : (half + 1) * LANES
                ]


def place_tiles(source, level, features_ref, first, last):
    rows = slice(class_of(level, 0) * VOCAB, class_of(level + 1, 0) * VOCAB)
    begin = BACK * TOKENS - 2**level
    features_ref[rows, first * LANES : last * LANES] = source[:, begin + first * LANES : begin + last * LANES]


def make_own(tokens_ref, class_ref, ones_ref, s7, s8, features_ref):
    count_classes(tokens_ref, class_ref, features_ref, 65, 72)
    count_tiles(tokens_ref, ones_ref, s7, 65, 71)
    widen(s7, s8, 7, 66, 70)
    place_tiles(s7, 7, features_ref, 2, 8)
    place_tiles(s8, 8, features_ref, 4, 8)


def make_near(tokens_ref, class_ref, ones_ref, s7, s8, s9, features_ref):
    count_classes(tokens_ref, class_ref, features_ref, 64, 65)
    count_tiles(tokens_ref, ones_ref, s7, 57, 65)
    widen(s7, s8, 7, 58, 66)
    widen(s8, s9, 8, 60, 68)
    place_tiles(s7, 7, features_ref, 0, 2)
    place_tiles(s8, 8, features_ref, 0, 4)
    place_level(s9, 9, features_ref)


def put_sum(features_ref, level, ones, terms):
    terms = [term for term in terms if term is not None]
    if ones in SPLIT[level]:
        total = sum(term.astype(F32) for term in terms)
        high, rest = halves(total)
        features_ref[block_of(level, ones), :] = high
        features_ref[rest_of(level, ones), :] = rest
    else:
        features_ref[block_of(level, ones), :] = sum(terms[1:], terms[0])


def make_far(tokens_ref, ones_ref, s7, s8, s9, s10, features_ref):
    count_tiles(tokens_ref, ones_ref, s7, 1, 57)
    widen(s7, s8, 7, 2, 58)
    widen(s8, s9, 8, 4, 60)
    widen(s9, s10, 9, 8, 64)
    place_level(s10, 10, features_ref)

    def shard(back, ones):
        first = (BACK - back) * 8
        return s10[ones * VOCAB : (ones + 1) * VOCAB, first * LANES : (first + 8) * LANES] if 0 <= ones <= 10 else None

    for ones in range(12):
        put_sum(features_ref, 11, ones, [shard(2, ones), shard(3, ones - 1)])
    for ones in range(13):
        put_sum(
            features_ref, 12, ones, [shard(4, ones), shard(5, ones - 1), shard(6, ones - 1), shard(7, ones - 2)]
        )


def gelu_parts(y):
    root = math.sqrt(2.0 / math.pi)
    square = y * y
    bend = jnp.tanh(root * (y + 0.044715 * square * y))
    half = 0.5 * (1.0 + bend)
    slope = half + 0.5 * y * (1.0 - bend * bend) * (root * (1.0 + 3 * 0.044715 * square))
    return y * half, slope


def piece_of_y(turned_ref, features_ref, piece, span):
    (first, last), start = PIECES[piece], STARTS[piece]
    both = dot(turned_ref[:, start : start + last - first], features_ref[first:last, span])
    return both[:WIDTH] + both[WIDTH:]


def parts_of_y(turned_ref, features_ref, y_ref, wanted):
    for piece, first, last in wanted:
        span = slice(first, last)
        part = piece_of_y(turned_ref, features_ref, piece, span)
        y_ref[:, span] = part if piece == 0 else y_ref[:, span] + part


def before_gelu(mix_ref, cot_ref, g_hidden_ref):
    g_hidden_ref[...] = lax.dot_general(
        cot_ref[...], mix_ref[...], (((1,), (1,)), ((), ())), preferred_element_type=F32
    )


def forward(turned_ref, features_ref, y_ref, g_hidden_ref, cot_ref, hidden_ref, g_ref):
    block = 512
    for start in range(0, TOKENS, block):
        span = slice(start, start + block)
        y = (y_ref[:, span] + piece_of_y(turned_ref, features_ref, 3, span)).T
        active, slope = gelu_parts(y)
        hidden = active.astype(BF16)
        hidden_ref[span, :] = hidden
        g_high, g_rest = halves(g_hidden_ref[span, :] * slope)
        g_ref[span, 0:WIDTH] = g_high
        g_ref[span, WIDTH:] = g_rest
    return lax.dot_general(
        hidden_ref[...], cot_ref[...], (((0,), (0,)), ((), ())), preferred_element_type=F32
    )


def outputs(embed, features_ref, hidden_ref, mix_ref, out_ref):
    high, middle = halves(embed)
    rest = (embed - high.astype(F32) - middle.astype(F32)).astype(BF16)
    table = jnp.concatenate([high, middle, rest], axis=0)
    for start in range(0, TOKENS, 256):
        span = slice(start, start + 256)
        hot = features_ref[0:VOCAB, span]
        hot = jnp.concatenate([hot, hot, hot], axis=0)
        x = lax.dot_general(hot, table, (((0,), (0,)), ((), ())), preferred_element_type=F32)
        out_ref[span, :] = x + dot(hidden_ref[span, :], mix_ref[...])


def backward(passed, folded, kappa, embed, features_ref, g_ref, cot_ref, z_ref):
    def over_names(value):
        return jnp.sum(embed * value, axis=0, keepdims=True)

    def products(first, last):
        both = dot(features_ref[first:last, :], g_ref[...])
        z_ref[first:last, :] = both[:, :WIDTH] + both[:, WIDTH:]

    ends = {0: class_of(8, 0) * VOCAB, 8: class_of(11, 0) * VOCAB, 11: CLASSES * VOCAB}

    def z_of(level, ones):
        z = z_ref[block_of(level, ones), :]
        return z + z_ref[rest_of(level, ones), :] if ones in SPLIT.get(level, ()) else z

    begin = 0
    rows = []
    for level in range(LEVELS):
        if level in ends:
            products(begin, ends[level])
            begin = ends[level]
        if level == 0:
            z0 = z_ref[0:VOCAB, :]
            rows.append(over_names(z0))
            embed_sum = folded[0] * z0 + dot(features_ref[0:VOCAB, :], cot_ref[...])
            zero_sum = one_sum = jnp.zeros_like(z0)
        total = passed(level, 0) * z_of(level, 0)
        counted = jnp.zeros_like(total)
        for ones in range(1, level + 1):
            term = passed(level, ones) * z_of(level, ones)
            total = total + term
            counted = counted + float(ones) * term
        rows.append(over_names(total))
        embed_sum = embed_sum + kappa[level] * total
        one_sum = one_sum + kappa[level] * counted
        zero_sum = zero_sum + kappa[level] * (float(level) * total - counted)
    rows += [over_names(zero_sum), over_names(one_sum)]
    return jnp.concatenate(rows + [embed_sum], axis=0)


def layer_kernel(
    count, scale, ids_hbm, embed_hbm, low_hbm, high_hbm, levels_hbm, mix_hbm, cot_hbm,
    out_ref, whole, factors_ref,
    held, ids_sems, ones_ref, class_ref, tokens_ref, s7, s8, s9, s10, features_ref, weights_ref, turned_ref,
    y_ref, g_hidden_ref, hidden_ref, g_ref, z_ref, ids_ref, embed_ref, low_ref, high_ref, levels_ref, mix_ref, cot_ref, local_sem,
    mix_part, small_part, mix_in, small_in, second, third, sends, recvs,
):
    seq, batch = lax.axis_index("seq"), lax.axis_index("batch")
    x, y = lax.rem(seq, 4), lax.rem(lax.div(seq, 4), 4)
    core = lax.rem(batch, 2)
    z = lax.div(seq, 16) * 2 + lax.div(batch, 2)

    def along(order):
        return x + order * (y - x), y + order * (z - y), z + order * (x - z)

    def device(order, spots, core):
        a, b, c = spots
        x, y, z = a + order * (c - a), b + order * (a - b), c + order * (b - c)
        return lax.div(z, 2) * 16 + y * 4 + x, lax.rem(z, 2) * 2 + core

    def moved(spots, i, j, k):
        return lax.rem(spots[0] + i, 4), lax.rem(spots[1] + j, 4), lax.rem(spots[2] + k, 4)

    mine, theirs = along(core), along(1 - core)
    hops = lambda spot: sum(min(step, 4 - step) for step in spot)
    plane = sorted([(i, j) for i in range(4) for j in range(4)], key=hops, reverse=True)
    others = plane[:-1]
    own_peer = lambda i, j, k: device(core, moved(mine, i, j, k), core)
    their_peer = lambda i, j: device(1 - core, moved(theirs, i, j, 0), 1 - core)
    cross_peer = lambda i, j: device(core, moved(mine, i, j, 0), 1 - core)
    chunk_of = lambda core, spots: 16 * core + 4 * spots[0] + spots[1]

    barrier = pltpu.get_barrier_semaphore()

    def greet(peer):
        pl.semaphore_signal(barrier, inc=1, device_id=peer, device_id_type=MESH)

    for step in range(1, BACK + 1):
        greet((lax.rem(seq + count - step, count), batch))
    for i, j in others:
        greet(own_peer(i, j, 0))
    for k in range(1, 4):
        greet(own_peer(0, 0, k))
    for i, j in plane:
        greet(their_peer(i, j))
        if i:
            greet(cross_peer(i + core * (j - i), j + core * (i - j)))
    loads = [
        pltpu.make_async_copy(source, target, local_sem.at[place])
        for place, (source, target) in enumerate(
            [
                (ids_hbm, ids_ref),
                (embed_hbm, embed_ref),
                (low_hbm, low_ref),
                (high_hbm, high_ref),
                (levels_hbm, levels_ref),
                (mix_hbm, mix_ref),
                (cot_hbm, cot_ref),
            ]
        )
    ]
    for load in loads:
        load.start()
    pl.semaphore_wait(barrier, BACK + 46)

    def copy_to(source, target, sent, received, peer):
        copy = pltpu.make_async_remote_copy(
            src_ref=source, dst_ref=target, send_sem=sent, recv_sem=received, device_id=peer, device_id_type=MESH
        )
        copy.start()
        return copy

    def drain(ref, sem):
        pltpu.make_async_copy(ref, ref, sem).wait()

    arrivals = [(0, 1), (1, BACK)]
    for group, (first, last) in reversed(list(enumerate(arrivals))):
        for step in range(first, last):
            peer = lax.rem(seq + step + 1, count), batch
            copy_to(ids_hbm, held.at[step], ids_sems.at[2], ids_sems.at[group], peer)

    for load in loads:
        load.wait()
    embed = embed_ref[...]
    low, high, levels = rows_of(low_ref), rows_of(high_ref), rows_of(levels_ref)
    folded, kappa = level_factors(low, high, levels)
    passed = lag_weights(low)
    make_weights(passed, folded, kappa, embed, weights_ref)
    turned_ref[...] = weights_ref[...].T
    make_tables(ones_ref, class_ref)
    tokens_ref[0:VOCAB, LANES:] = jnp.zeros((VOCAB, LANES), BF16)
    features_ref[CLASSES * VOCAB :, :] = jnp.zeros((ROWS - CLASSES * VOCAB, TOKENS), BF16)
    before_gelu(mix_ref, cot_ref, g_hidden_ref)
    make_hot(tokens_ref, 8 * BACK, ids_ref[...])
    make_own(tokens_ref, class_ref, ones_ref, s7, s8, features_ref)
    parts_of_y(turned_ref, features_ref, y_ref, ((0, 256, 1024), (1, 512, 1024)))

    factors_ref[0:2, :] = low_ref[...]
    factors_ref[2:4, :] = high_ref[...]
    factors_ref[4:18, :] = levels_ref[...]
    for level in range(LEVELS + 1):
        factors_ref[18 + level : 19 + level, :] = folded[level]

    def receive(group):
        first, last = arrivals[group]
        drain(held.at[pl.ds(first, last - first)], ids_sems.at[group])
        for step in range(first, last):
            make_hot(tokens_ref, 8 * (BACK - 1 - step), jnp.where(seq > step, held[step], -1))

    receive(0)
    make_near(tokens_ref, class_ref, ones_ref, s7, s8, s9, features_ref)
    parts_of_y(turned_ref, features_ref, y_ref, ((0, 0, 256), (1, 0, 512), (2, 0, 1024)))
    receive(1)
    make_far(tokens_ref, ones_ref, s7, s8, s9, s10, features_ref)
    mix_sum = forward(turned_ref, features_ref, y_ref, g_hidden_ref, cot_ref, hidden_ref, g_ref)

    home = chunk_of(core, mine)

    def spread(phase, part, target):
        for slot, (i, j) in enumerate(plane):
            place = chunk_of(1 - core, moved(theirs, i, j, 0))
            copy_to(part.at[place], target.at[slot + 15], sends.at[phase], recvs.at[phase], their_peer(i, j))
            if (i, j) in others:
                place = chunk_of(core, moved(mine, i, j, 0))
                copy_to(part.at[place], target.at[slot], sends.at[phase], recvs.at[phase], own_peer(i, j, 0))

    for chunk in range(CHUNKS):
        mix_part[chunk] = scale * mix_sum[8 * chunk : 8 * chunk + 8]
    small = scale * backward(passed, folded, kappa, embed, features_ref, g_ref, cot_ref, z_ref)
    spread(0, mix_part, mix_in)
    for chunk in range(CHUNKS):
        small_part[chunk] = small[chunk : chunk + 1]
    spread(1, small_part, small_in)
    drain(mix_in, recvs.at[0])
    mixed = mix_part[home]
    for slot in range(CHUNKS - 1):
        mixed = mixed + mix_in[slot]
    for row in range(8):
        second[mine[2], row] = mixed[row : row + 1]
    drain(small_in, recvs.at[1])
    row = small_part[home]
    for slot in range(CHUNKS - 1):
        row = row + small_in[slot]
    second[mine[2], 8] = row
    spot = second.at[mine[2]]
    for k in (2, 1, 3):
        copy_to(spot, spot, sends.at[2], recvs.at[2], own_peer(0, 0, k))
    outputs(embed, features_ref, hidden_ref, mix_ref, out_ref)
    drain(second.at[pl.ds(0, 3)], recvs.at[2])
    third[...] = (second[0] + second[1]) + (second[2] + second[3])
    landing = whole.at[pl.ds(9 * home, 9)]
    for i, j in plane:
        copy_to(third, landing, sends.at[3], recvs.at[3], cross_peer(i, j))
        if (i, j) in others:
            copy_to(third, landing, sends.at[3], recvs.at[3], own_peer(i, j, 0))
    whole[pl.ds(9 * home, 9)] = third[...]
    drain(held, ids_sems.at[2])
    drain(mix_in, sends.at[0])
    drain(small_in, sends.at[1])
    drain(second.at[pl.ds(0, 3)], sends.at[2])
    gathered = whole.at[pl.ds(0, 9 * (CHUNKS - 1))]
    drain(gathered, recvs.at[3])
    drain(gathered, sends.at[3])


def layer(count, scale, ids, embed, low, high, levels, mix, cot):
    vmem = pl.BlockSpec(memory_space=pltpu.VMEM)
    far = pl.BlockSpec(memory_space=pltpu.HBM)
    arguments = tuple(
        pltpu.with_memory_space_constraint(array, pltpu.HBM) for array in (ids, embed, low, high, levels, mix, cot)
    )
    return pl.pallas_call(
        functools.partial(layer_kernel, count, scale),
        out_shape=(
            jax.ShapeDtypeStruct((TOKENS, WIDTH), F32),
            jax.ShapeDtypeStruct((9 * CHUNKS, 1, WIDTH), F32),
            jax.ShapeDtypeStruct((32, WIDTH), F32),
        ),
        in_specs=[far] * 7,
        out_specs=(vmem,) * 3,
        scratch_shapes=[
            pltpu.VMEM((BACK, 8, LANES), jnp.int32),
            pltpu.SemaphoreType.DMA((3,)),
            pltpu.VMEM((2 * LANES, 8 * LANES), BF16),
            pltpu.VMEM((2 * LANES, 29 * LANES), BF16),
            pltpu.VMEM((TILES * VOCAB, 2 * LANES), BF16),
            pltpu.VMEM((8 * VOCAB, TILES * LANES), BF16),
            pltpu.VMEM((9 * VOCAB, TILES * LANES), BF16),
            pltpu.VMEM((10 * VOCAB, TILES * LANES), BF16),
            pltpu.VMEM((11 * VOCAB, TILES * LANES), BF16),
            pltpu.VMEM((ROWS, TOKENS), BF16),
            pltpu.VMEM((WEIGHTS, 2 * WIDTH), BF16),
            pltpu.VMEM((2 * WIDTH, WEIGHTS), BF16),
            pltpu.VMEM((WIDTH, TOKENS), F32),
            pltpu.VMEM((TOKENS, WIDTH), F32),
            pltpu.VMEM((TOKENS, WIDTH), BF16),
            pltpu.VMEM((TOKENS, 2 * WIDTH), BF16),
            pltpu.VMEM((CLASSES * VOCAB, WIDTH), F32),
            *[pltpu.VMEM(array.shape, array.dtype) for array in arguments],
            pltpu.SemaphoreType.DMA((7,)),
            pltpu.VMEM((CHUNKS, 8, WIDTH), F32),
            pltpu.VMEM((CHUNKS, 1, WIDTH), F32),
            pltpu.VMEM((CHUNKS - 1, 8, WIDTH), F32),
            pltpu.VMEM((CHUNKS - 1, 1, WIDTH), F32),
            pltpu.VMEM((4, 9, 1, WIDTH), F32),
            pltpu.VMEM((9, 1, WIDTH), F32),
            pltpu.SemaphoreType.DMA((4,)),
            pltpu.SemaphoreType.DMA((4,)),
        ],
        compiler_params=pltpu.CompilerParams(
            collective_id=0, has_side_effects=True, vmem_limit_bytes=44 * 2**20
        ),
    )(*arguments)


def finish_kernel(
    out_ref, whole, factors_ref,
    out_hbm, filters_hbm, levels_hbm, mix_hbm, embed_hbm,
    filters_ref, grad_levels_ref, mix_ref, embed_ref, sems,
):
    stores = []

    def store(source, target):
        copy = pltpu.make_async_copy(source, target, sems.at[len(stores)])
        copy.start()
        stores.append(copy)

    store(out_ref, out_hbm)
    for chunk in range(CHUNKS):
        for row in range(8):
            mix_ref[8 * chunk + row : 8 * chunk + row + 1, :] = whole[9 * chunk + row]
    store(mix_ref, mix_hbm)
    summed = [whole[9 * chunk + 8] for chunk in range(CHUNKS)]
    for name in range(VOCAB):
        embed_ref[name : name + 1, :] = summed[16 + name]
    store(embed_ref, embed_hbm)
    shifted = summed[1:14]
    factors = rows_of(factors_ref)
    low, high, levels, folded = factors[0:2], factors[2:4], factors[4:18], factors[18:32]
    current = summed[0]
    low_zero, low_one = summed[14] / low[0], summed[15] / low[1]
    high_zero = high_one = jnp.zeros_like(current)
    for level in range(LEVELS):
        late = shifted[level]
        grad_levels_ref[level : level + 1, :] = high[0] * current + high[1] * late
        low_zero = low_zero + folded[level + 1] * current
        low_one = low_one + folded[level + 1] * late
        high_zero = high_zero + levels[level] * current
        high_one = high_one + levels[level] * late
        current = low[0] * current + low[1] * late
    grad_levels_ref[LEVELS : LEVELS + 1, :] = current
    filters_ref[0, 0:1, :] = low_zero
    filters_ref[0, 1:2, :] = low_one
    filters_ref[1, 0:1, :] = high_zero
    filters_ref[1, 1:2, :] = high_one
    store(filters_ref, filters_hbm)
    store(grad_levels_ref, levels_hbm)
    for copy in stores:
        copy.wait()


def finish(out, whole, factors):
    shapes = [(TOKENS, WIDTH), (2, 2, WIDTH), (LEVELS + 1, WIDTH), (WIDTH, WIDTH), (VOCAB, WIDTH)]
    return pl.pallas_call(
        finish_kernel,
        out_shape=tuple(jax.ShapeDtypeStruct(shape, F32) for shape in shapes),
        in_specs=[pl.BlockSpec(memory_space=pltpu.VMEM)] * 3,
        out_specs=(pl.BlockSpec(memory_space=pl.ANY),) * 5,
        scratch_shapes=[pltpu.VMEM(shape, F32) for shape in shapes[1:]] + [pltpu.SemaphoreType.DMA((5,))],
        compiler_params=pltpu.CompilerParams(vmem_limit_bytes=16 * 2**20),
    )(out, whole, factors)


def per_device(ids, embed, low_filter, high_filter, level_weights, mix, cotangent):
    count = lax.axis_size("seq")
    scale = 1.0 / math.sqrt(count * lax.axis_size("batch") * TOKENS)
    out, whole, factors = layer(
        count, scale, ids.reshape(8, LANES), embed, low_filter, high_filter, level_weights, mix, cotangent[0]
    )
    out, grad_filters, grad_levels, grad_mix, grad_embed = finish(out, whole, factors)
    return out[None], grad_filters, grad_levels, grad_mix, grad_embed


def solution(mesh):
    placed = (P("batch", "seq"), P(), P(), P(), P(), P(), P("batch", "seq", None))
    return jax.shard_map(
        per_device,
        mesh=mesh,
        in_specs=placed,
        out_specs=(P("batch", "seq", None), P(), P(), P(), P()),
        check_vma=False,
    )
```
